256 devices in a mesh: gx: 32 (over y, z), gy: 8 (over x, core).
Axes of the slice: x: 4, y: 4, z: 8, core: 2. Of those that a mesh axis runs over, the one named last changes fastest.
Arguments:
- features: bfloat16 [32, 4, 256, 1024], P(None, None, 'gx', 'gy'), may hold values from -8 to 8
- vessel_label: int32 [4, 256, 1024], P(None, 'gx', 'gy'), may hold values from 0 to 1, as said below
- conv_weight: bfloat16 [27, 32], replicated, may hold values from -0.21875 to 0.21875
- conv_bias: float32 [1], replicated, may hold values from -1.5 to 1.5
Outputs:
- cldice_loss: float32 [], replicated
- weight_grad: float32 [27, 32], replicated
- bias_grad: float32 [1], replicated
- feature_grad: bfloat16 [32, 4, 256, 1024], P(None, None, 'gx', 'gy')
The draws below stay inside these ranges and needn't reach their ends.
Inputs may be any that keep to these rules, and one draw needn't show every extreme that they name: `vessel_label`: 1 marks a vessel voxel, 0 the background.
All inputs are finite; a program needn't handle non-finite values.
Results may differ from the reference program's by a relative error of at most 0.012.
Values may be sent and summed in bfloat16 or wider, within the bound.
No kernel may reach another device: no remote copies, remote signals or barrier semaphores. Data moves between devices by JAX's collectives and lax.ppermute only.
A program may use at most 64 MiB of HBM per device.

```python
import jax
import jax.numpy as jnp
from jax import lax

C = 32
ITERS = 5
ZD = 4
NX = 256
NY = 1024


def label_field(key):
    levels = jax.random.randint(jax.random.fold_in(key, 11), (ZD, NX, NY), 0, 1000)
    row_ids = jnp.arange(NX, dtype=jnp.int32)[None, :, None]
    cutoff = 150 + 300 * row_ids // NX
    return (levels < cutoff).astype(jnp.int32)


def draw_vessel_label(key, part):
    return label_field(key)


def draw_features(key, part):
    vessel = label_field(key).astype(jnp.float32)
    channel_signs = jnp.clip(jax.random.normal(jax.random.fold_in(key, 12), (C, 1, 1, 1), jnp.float32), -2.0, 2.0)
    background = jnp.clip(jax.random.normal(jax.random.fold_in(key, 13), (C, ZD, NX, NY), jnp.float32), -6.0, 6.0)
    return (background + 0.6 * channel_signs * (2.0 * vessel[None] - 1.0)).astype(jnp.bfloat16)


def normal_values(own_key, shape, spread, bound, kind=jnp.bfloat16):
    return jnp.clip(spread * jax.random.normal(own_key, shape, jnp.float32), -bound, bound).astype(kind)


def setup_inputs(seed: int = 0) -> dict:
    splits = jax.random.split(jax.random.key(seed), 5)
    return {
        "features": draw_features(jax.random.fold_in(splits[4], 71), 0),
        "vessel_label": draw_vessel_label(jax.random.fold_in(splits[4], 71), 0),
        "conv_weight": normal_values(splits[2], (27, C), (27 * C) ** -0.5, 0.21875),
        "conv_bias": jnp.clip(jax.random.uniform(splits[3], (1,), jnp.float32, -1.5, 1.5), -1.5, 1.5),
    }


softmin_sharpness = 0.1
softness = 0.05

def soft_relu(source_grid):
    return softness * jax.nn.softplus(source_grid / softness)

def soft_dilate(source_grid):
    scaled_powers = jnp.exp(jnp.pad(source_grid, 1) / softmin_sharpness)
    collapsed_aggregate = scaled_powers[:-2] + scaled_powers[1:-1] + scaled_powers[2:]
    collapsed_aggregate = collapsed_aggregate[:, :-2] + collapsed_aggregate[:, 1:-1] + collapsed_aggregate[:, 2:]
    collapsed_aggregate = collapsed_aggregate[:, :, :-2] + collapsed_aggregate[:, :, 1:-1] + collapsed_aggregate[:, :, 2:]
    return softmin_sharpness * jnp.log(collapsed_aggregate / 27.0)

def soft_erode(source_grid):
    scaled_powers = jnp.exp(-jnp.pad(source_grid, 1) / softmin_sharpness)
    middle_cell = scaled_powers[1:-1, 1:-1, 1:-1]
    neighbouring_cells = scaled_powers[2:, 1:-1, 1:-1] + scaled_powers[:-2, 1:-1, 1:-1] + scaled_powers[1:-1, 2:, 1:-1] + scaled_powers[1:-1, :-2, 1:-1] + scaled_powers[1:-1, 1:-1, 2:] + scaled_powers[1:-1, 1:-1, :-2]
    return -softmin_sharpness * jnp.log(middle_cell / 3.0 + neighbouring_cells / 9.0)

def soft_open(source_grid):
    return soft_dilate(soft_erode(source_grid))

def skeleton(source_grid):
    current = source_grid
    skeleton_sum = soft_relu(current - soft_open(current))
    for erosion in range(ITERS):
        current = soft_erode(current)
        change_term = soft_relu(current - soft_open(current))
        skeleton_sum = skeleton_sum + soft_relu(change_term - skeleton_sum * change_term)
    return skeleton_sum

def topology_loss(totals):
    precision = (totals[0] + 1.0) / (totals[1] + 1.0)
    sensitivity = (totals[2] + 1.0) / (totals[3] + 1.0)
    return 1.0 - 2.0 * precision * sensitivity / (precision + sensitivity)

def reference(features, vessel_label, conv_weight, conv_bias):
    depth_cells, total_rows, total_cols = vessel_label.shape
    weight_float = conv_weight.astype(jnp.float32)

    def add_channel(running, channel_pair):
        channel, weight_col = channel_pair
        padded = jnp.pad(channel.astype(jnp.float32), 1)
        for position in range(27):
            depth_shift, row_shift, col_shift = (position // 9, position // 3 % 3, position % 3)
            running = running + weight_col[position] * padded[depth_shift:depth_shift + depth_cells, row_shift:row_shift + total_rows, col_shift:col_shift + total_cols]
        return (running, None)
    start_logits = jnp.zeros((depth_cells, total_rows, total_cols), jnp.float32) + conv_bias[0]
    logits = lax.scan(add_channel, start_logits, (features, weight_float.T))[0]
    label_float = vessel_label.astype(jnp.float32)
    true_skel = skeleton(label_float)

    def loss_of_logits(logit_field):
        prob = jax.nn.sigmoid(logit_field)
        pred_skel = skeleton(prob)
        totals = jnp.stack([jnp.sum(pred_skel * label_float), jnp.sum(pred_skel), jnp.sum(true_skel * prob), jnp.sum(true_skel)])
        return topology_loss(totals)
    loss_value, grad_logits = jax.value_and_grad(loss_of_logits)(logits)
    padded_grad = jnp.pad(grad_logits, 1)
    voxel_count = float(depth_cells * total_rows * total_cols)

    def per_channel(running, channel_pair):
        channel, weight_col = channel_pair
        padded = jnp.pad(channel.astype(jnp.float32), 1)
        weight_terms = []
        feature_term = jnp.zeros((depth_cells, total_rows, total_cols), jnp.float32)
        for position in range(27):
            depth_shift, row_shift, col_shift = (position // 9, position // 3 % 3, position % 3)
            window = padded[depth_shift:depth_shift + depth_cells, row_shift:row_shift + total_rows, col_shift:col_shift + total_cols]
            weight_terms.append(jnp.sum(grad_logits * window))
            back_window = padded_grad[2 - depth_shift:2 - depth_shift + depth_cells, 2 - row_shift:2 - row_shift + total_rows, 2 - col_shift:2 - col_shift + total_cols]
            feature_term = feature_term + weight_col[position] * back_window
        return (running, (jnp.stack(weight_terms), (feature_term * voxel_count).astype(jnp.bfloat16)))
    running_zero = jnp.zeros((), jnp.float32)
    per_weight, feature_grad = lax.scan(per_channel, running_zero, (features, weight_float.T))[1]
    weight_grad = per_weight.T
    bias_grad = jnp.sum(grad_logits)[None]
    return (loss_value, weight_grad, bias_grad, feature_grad)
```

```python
import jax
import jax.numpy as jnp
from jax import lax
from jax.experimental import pallas as pl
from jax.experimental.pallas import tpu as pltpu
from jax.sharding import PartitionSpec as P

ITERS = 5
F32 = jnp.float32
BF16 = jnp.bfloat16
SHARP = 10.0
SOFT = 0.05
EDGE = 16
VMEM_LIMIT = 48 * 1024 * 1024


def iota(shape, dim):
    return lax.broadcasted_iota(jnp.int32, shape, dim)


def dot(a, b, dims, precision=None):
    return lax.dot_general(a, b, (dims, ((), ())), precision=precision, preferred_element_type=F32)


def edge_row(q):
    return jnp.where(q < 8, q, jnp.where(q == 8, 8, jnp.where(q == 15, -1, -100)))


def weight_matrix(w):
    spread = jnp.where((iota((32, 256), 1) >> 3) == iota((32, 256), 0), 1.0, 0.0).astype(BF16)
    by_lane = dot(w, spread, ((1,), (0,))).astype(BF16)
    row = iota((144, 27), 0)
    ad = row >> 4
    base = ad + 6 * (jnp.where(ad >= 3, 1, 0) + jnp.where(ad >= 6, 1, 0))
    col = iota((144, 27), 1)
    offset = (iota((144, 256), 1) & 7) - edge_row(iota((144, 256), 0) & 15) + 1
    matrix = jnp.zeros((144, 256), F32)
    for b in range(3):
        pick = jnp.where(col == base + 3 * b, 1.0, 0.0).astype(BF16)
        matrix = matrix + jnp.where(offset == b, dot(pick, by_lane, ((1,), (0,))), 0.0)
    return matrix.astype(BF16)


def partial_logits_kernel(w_ref, f_ref, lab_ref, a_ref, near_ref, far_ref):
    matrix = weight_matrix(w_ref[...])
    a_ref[...] = matrix
    lane = iota((16, 128), 1)
    terms = [
        dot(matrix, f_ref[:, z].reshape(256, 128), ((1,), (0,))).reshape(3, 3, 16, 128)
        for z in range(4)
    ]
    corner = jnp.zeros((16, 128), F32)
    for z in range(4):
        byd = []
        for d in range(3):
            byd.append(sum(terms[z + a - 1][a, d] for a in range(3) if 0 <= z + a - 1 < 4))
        main = byd[1]
        main = main + jnp.where(lane >= 1, pltpu.roll(byd[0], 1, 1), 0.0)
        main = main + jnp.where(lane <= 126, pltpu.roll(byd[2], 127, 1), 0.0)
        near_ref[16 * z : 16 * z + 16] = main
        far_ref[16 * z : 16 * z + 16] = main
        shift = 32 * z + 17
        corner = jnp.where(lane == shift - 1, pltpu.roll(byd[0], shift, 1), corner)
        corner = jnp.where(lane == shift, pltpu.roll(byd[2], shift, 1), corner)
    near_ref[64:80] = corner
    far_ref[64:80] = corner
    near_ref[80:112] = lab_ref[...].reshape(32, 128).astype(F32)


def rows_kernel(own_ref, m1_ref, p1_ref, m2_ref, p2_ref, main_ref, lab_ref, right_ref, left_ref):
    blocks = [m2_ref, m1_ref, own_ref, p1_ref, p2_ref]
    sub = iota((8, 128), 0)

    def assemble(start):
        tiles = []
        for t in range(5):
            tile = blocks[t][start : start + 8]
            if t > 0:
                tile = tile + jnp.where(sub == 0, blocks[t - 1][start + 8 : start + 16], 0.0)
            if t < 4:
                tile = tile + jnp.where(sub == 7, blocks[t + 1][start + 8 : start + 16], 0.0)
            tiles.append(tile)
        return jnp.concatenate(tiles, axis=0)

    corner = assemble(64)
    group = iota((64, 128), 1) >> 5
    right = jnp.zeros((64, 128), F32)
    left = jnp.zeros((64, 128), F32)
    for z in range(4):
        main = assemble(16 * z)
        main_ref[z] = main
        lab = jnp.concatenate(
            [ref[80 + 8 * z : 88 + 8 * z] for ref in (m1_ref, own_ref, p1_ref)], axis=0
        )
        lab_ref[z] = lab
        both = jnp.concatenate([main, lab], axis=0)
        right = jnp.where(group == z, pltpu.roll(both, (32 * z + 16) % 128, 1), right)
        left = jnp.where(group == z, pltpu.roll(both, 32 * z, 1), left)
    main_ref[4] = corner
    spread = jnp.concatenate([corner, jnp.zeros((24, 128), F32)], axis=0)
    place = iota((64, 128), 1) & 31
    right_ref[...] = jnp.where(place < 16, right, spread)
    left_ref[...] = jnp.where(place < 16, left, spread)


def shift_rows(x, s):
    return pltpu.roll(x, s % x.shape[0], 0)


def shift_cols(x, s):
    return pltpu.roll(x, s % x.shape[1], 1)


def cross(fields, outside):
    result = []
    for z in range(4):
        x = fields[z]
        around = shift_rows(x, 1) + shift_rows(x, -1) + shift_cols(x, 1) + shift_cols(x, -1)
        before = fields[z - 1] if z > 0 else outside
        after = fields[z + 1] if z < 3 else outside
        result.append((around + (before + after)) * (1.0 / 9.0) + x * (1.0 / 3.0))
    return result


def box(fields, outside, crop):
    result = []
    for z in range(4):
        before = fields[z - 1] if z > 0 else outside
        after = fields[z + 1] if z < 3 else outside
        x = fields[z] + (before + after)
        x = x + shift_rows(x, 1) + shift_rows(x, -1)
        if crop:
            x = x[8:32]
        result.append(x + shift_cols(x, 1) + shift_cols(x, -1))
    return result


def inverse(x):
    return 1.0 / x


def forward(e0, q0, inside, crop, keep):
    def middle(x):
        return x[8:32] if crop else x

    e, q, s = e0, q0, None
    for i in range(ITERS + 1):
        e = [jnp.where(inside, x, 1.0) for x in cross(e, 1.0)]
        q_next = [inverse(x) for x in e]
        mean = box(q_next, 1.0, crop)
        s_next = []
        for z in range(4):
            d_inv = inverse(mean[z] * (1.0 / 27.0))
            qz = middle(q[z])
            ratio = qz * d_inv
            ratio = ratio * ratio
            log_term = jnp.log(1.0 + ratio)
            change = SOFT * log_term
            if i == 0:
                s_next.append(change)
                keep(i, z, qz, d_inv, ratio, None, None, None)
            else:
                rest = 1.0 - s[z]
                power = jnp.exp(log_term * rest)
                s_next.append(s[z] + SOFT * jnp.log(1.0 + power))
                keep(i, z, qz, d_inv, ratio, change, rest, power)
        s, q = s_next, q_next
    return s, q


def skeleton_kernel(
    bias_ref, f_ref, main_ref, lab_ref, from_left_ref, from_right_ref,
    grad_ref, sums_ref,
    qs_ref, ds_ref, rs_ref, gain_ref, direct_ref,
):
    row_ids = lax.axis_index("gx") * 8 - 16 + iota((40, 256), 0)
    lane = iota((40, 256), 1)
    col = jnp.where(lane < 144, lane, lane - 256)
    col_ids = lax.axis_index("gy") * 128 + col
    inside = (row_ids >= 0) & (row_ids < lax.axis_size("gx") * 8)
    inside = inside & (col_ids >= 0) & (col_ids < lax.axis_size("gy") * 128) & (col >= -16)
    inside_f = jnp.where(inside, 1.0, 0.0)
    inner = inside_f[8:32]
    inner_b = inner > 0.5
    bias = bias_ref[0]

    lane1 = iota((64, 128), 1)
    from_left = from_left_ref[...]
    from_right = from_right_ref[...]
    corner = main_ref[4]
    lane40 = lane1[:40]
    e0, q0, slope, probs, labels = [], [], [], [], []
    for z in range(4):
        start = 32 * z
        extra_left = pltpu.roll(from_left, (112 - start) % 128, 1)
        extra_right = pltpu.roll(from_right, (128 - start) % 128, 1)
        extra = jnp.where(lane1 >= 112, extra_left, jnp.where(lane1 < 16, extra_right, 0.0))
        at_zero = pltpu.roll(from_left[:40], (128 - start - 16) % 128, 1)
        at_last = pltpu.roll(from_right[:40], (110 - start) % 128, 1)
        main = main_ref[z]
        main = main + jnp.where(lane40 == 0, at_zero, jnp.where(lane40 == 127, at_last, 0.0))
        own_zero = pltpu.roll(corner, (128 - start - 16) % 128, 1)
        own_last = pltpu.roll(corner, (110 - start) % 128, 1)
        tail = extra[:40]
        tail = tail + jnp.where(lane40 == 0, own_zero, jnp.where(lane40 == 127, own_last, 0.0))
        logits = jnp.concatenate([main, tail], axis=1) + bias
        small = jnp.exp(-jnp.abs(logits))
        scale = inverse(1.0 + small)
        prob = jnp.where(logits >= 0.0, scale, small * scale)
        prob = jnp.where(inside, prob, 0.0)
        e = jnp.exp(-SHARP * prob)
        e0.append(e)
        q0.append(inverse(e))
        weight = (small * scale) * scale
        slope.append(((-SHARP) * e * weight)[8:32] * inner)
        probs.append((prob[8:32], weight[8:32]))
        labels.append(jnp.concatenate([lab_ref[z], extra[40:]], axis=1))

    low, high = jnp.exp(-SHARP * jnp.ones((24, 256), F32)), jnp.exp(SHARP * jnp.ones((24, 256), F32))
    true_skel, _ = forward(
        [jnp.where(x > 0.5, low, 1.0) for x in labels],
        [jnp.where(x > 0.5, high, 1.0) for x in labels],
        inner_b, False, lambda *factors: None,
    )

    def keep(i, z, qz, d_inv, ratio, change, rest, power):
        qs_ref[i, z] = qz
        ds_ref[i, z] = d_inv
        part = (-2.0 * SOFT) * (ratio * inverse(1.0 + ratio))
        if i > 0:
            share = power * inverse(1.0 + power)
            part = part * (share * rest)
            gain_ref[i, z] = 1.0 - share * change
        rs_ref[i, z] = part

    pred_skel, q_last = forward(e0, q0, inside, True, keep)

    def own(x):
        return x[8:16, :128]

    def total(values):
        acc = values[0] + values[1] + values[2] + values[3]
        return jnp.sum(jnp.sum(acc, axis=1, keepdims=True), axis=0, keepdims=True)

    t0 = total([own(pred_skel[z] * labels[z]) for z in range(4)])
    t1 = total([own(pred_skel[z]) for z in range(4)])
    t2 = total([own(true_skel[z] * probs[z][0]) for z in range(4)])
    t3 = total([own(true_skel[z]) for z in range(4)])

    weights = [labels, [inner] * 4]
    running = [jnp.ones((24, 256), F32)] * 4
    deep = [None, None]
    for i in range(ITERS, -1, -1):
        coefs = []
        for z in range(4):
            coefs.append(rs_ref[i, z] * running[z])
            if i > 0:
                running[z] = running[z] * gain_ref[i, z]
        for f in range(2):
            scaled = [coefs[z] * weights[f][z] for z in range(4)]
            spread = box([scaled[z] * ds_ref[i, z] for z in range(4)], 0.0, False)
            q_of = [q_last[z][8:32] if i == ITERS else qs_ref[i + 1, z] for z in range(4)]
            incoming = []
            for z in range(4):
                value = spread[z] * (q_of[z] * q_of[z]) * (-1.0 / 27.0)
                if deep[f] is not None:
                    value = value + deep[f][z]
                incoming.append(value * inner)
            moved = cross(incoming, 0.0)
            deep[f] = [moved[z] + scaled[z] * qs_ref[i, z] for z in range(4)]
    fields = [
        [deep[0][z] * slope[z] for z in range(4)],
        [deep[1][z] * slope[z] for z in range(4)],
        [true_skel[z] * probs[z][1] * inner for z in range(4)],
    ]
    bias_sums = [total([own(x) for x in field]) for field in fields]

    sub = iota((8, 256), 0)
    stacks = []
    for z in range(4):
        pieces = []
        for f in range(3):
            x = fields[f][z]
            edge = jnp.where(sub == 0, x[16:24], jnp.where(sub == 7, x[0:8], 0.0))
            block = jnp.concatenate([x[8:16], edge], axis=0)
            grad_ref[f, z] = block
            for d in range(3):
                moved = (shift_cols(block, d - 1) if d != 1 else block)[:, :128]
                upper = moved.astype(BF16)
                lower = (moved - upper.astype(F32)).astype(BF16)
                pieces += [upper, lower]
        stacks.append(jnp.concatenate(pieces, axis=0))
    offset = (iota((16, 256), 1) & 7) - edge_row(iota((16, 256), 0)) + 1
    rows = [[None] * 9 for _ in range(3)]
    picked = {}
    for a in range(3):
        moments = jnp.zeros((288, 256), F32)
        for z in range(4):
            if 0 <= z + a - 1 < 4:
                feats = f_ref[:, z + a - 1].reshape(256, 128)
                moments = moments + dot(stacks[z], feats, ((1,), (1,)))
        for f in range(3):
            for d in range(3):
                start = (f * 3 + d) * 32
                pair = moments[start : start + 16] + moments[start + 16 : start + 32]
                for b in range(3):
                    chosen = jnp.where(offset == b, pair, 0.0)
                    picked[b, f, a, d] = jnp.sum(chosen, axis=0, keepdims=True)
    result = jnp.zeros((32, 128), F32)
    for b in range(3):
        stacked = jnp.concatenate(
            [picked[b, f, a, d] for f in range(3) for a in range(3) for d in range(3)]
            + [jnp.zeros((5, 256), F32)],
            axis=0,
        )
        collect = jnp.where((iota((256, 128), 0) >> 3) + 32 * b == iota((256, 128), 1), 1.0, 0.0)
        result = result + dot(stacked, collect, ((1,), (0,)), precision=lax.Precision.HIGHEST)
    row32, lane32 = iota((32, 128), 0), iota((32, 128), 1)
    for k, value in enumerate([t0, t1, t2, t3] + bias_sums):
        result = jnp.where((row32 == 31) & (lane32 == k), value, result)
    for n in range(sums_ref.shape[0]):
        sums_ref[n] = result


def add_kernel(in_ref, out_ref):
    acc = in_ref[0]
    for n in range(1, in_ref.shape[0]):
        acc = acc + in_ref[n]
    for n in range(out_ref.shape[0]):
        out_ref[n] = acc


def final_kernel(in_ref, grad_ref, a_ref, loss_ref, weight_ref, bias_ref, out_ref, *, voxels):
    acc = in_ref[0]
    for n in range(1, in_ref.shape[0]):
        acc = acc + in_ref[n]
    sums = [acc[31:32, k : k + 1] for k in range(7)]
    precision = (sums[0] + 1.0) / (sums[1] + 1.0)
    sensitivity = (sums[2] + 1.0) / (sums[3] + 1.0)
    both = precision + sensitivity
    loss_ref[...] = 1.0 - 2.0 * precision * sensitivity / both
    by_precision = -2.0 * (sensitivity / both) * (sensitivity / both)
    by_sensitivity = -2.0 * (precision / both) * (precision / both)
    slopes = [
        by_precision / (sums[1] + 1.0),
        -by_precision * precision / (sums[1] + 1.0),
        by_sensitivity / (sums[3] + 1.0),
    ]
    bias_ref[...] = slopes[0] * sums[4] + slopes[1] * sums[5] + slopes[2] * sums[6]
    weight = slopes[0] * acc[0:9] + slopes[1] * acc[9:18] + slopes[2] * acc[18:27]
    for b in range(3):
        part = weight if b == 0 else pltpu.roll(weight, 128 - 32 * b, 1)
        for a in range(3):
            weight_ref[9 * a + 3 * b : 9 * a + 3 * b + 3] = part[3 * a : 3 * a + 3, :32]
    matrix = a_ref[...]
    parts = []
    for z in range(4):
        block = slopes[0] * grad_ref[0, z] + slopes[1] * grad_ref[1, z] + slopes[2] * grad_ref[2, z]
        block = block * voxels
        byd = []
        for d in range(3):
            moved = (shift_cols(block, d - 1) if d != 1 else block)[:, :128]
            upper = moved.astype(BF16)
            byd.append((upper, (moved - upper.astype(F32)).astype(BF16)))
        parts.append(byd)
    none = jnp.zeros((16, 128), BF16)
    for z in range(4):
        acc_z = None
        for level in range(2):
            stack = []
            for a in range(3):
                for d in range(3):
                    at = z - a + 1
                    stack.append(parts[at][d][level] if 0 <= at < 4 else none)
            term = dot(matrix, jnp.concatenate(stack, axis=0), ((0,), (0,)))
            acc_z = term if acc_z is None else acc_z + term
        out_ref[:, z] = acc_z.reshape(32, 8, 128).astype(BF16)


def call(kernel, out_shapes, *args, scratch=(), smem=()):
    spec = pl.BlockSpec(memory_space=pltpu.VMEM)
    in_specs = [pl.BlockSpec(memory_space=pltpu.SMEM) if n in smem else spec for n in range(len(args))]
    return pl.pallas_call(
        kernel,
        out_shape=[jax.ShapeDtypeStruct(shape, dtype) for shape, dtype in out_shapes],
        in_specs=in_specs,
        out_specs=[spec] * len(out_shapes),
        scratch_shapes=list(scratch),
        compiler_params=pltpu.CompilerParams(vmem_limit_bytes=VMEM_LIMIT),
    )(*args)


def passed(x, axis, steps):
    count = lax.axis_size(axis)
    pairs = [(n, n + steps) for n in range(count) if 0 <= n + steps < count]
    return lax.ppermute(x, axis, pairs)


def local(features, vessel_label, conv_weight, conv_bias):
    gx, gy = lax.axis_size("gx"), lax.axis_size("gy")
    voxels = float(4 * 8 * gx * 128 * gy)
    matrix, near, far = call(
        partial_logits_kernel,
        [((144, 256), BF16), ((112, 128), F32), ((80, 128), F32)],
        conv_weight, features, vessel_label,
    )
    m2, p2 = passed(far, "gx", 2), passed(far, "gx", -2)
    m1, p1 = passed(near, "gx", 1), passed(near, "gx", -1)
    main, labels, right, left = call(
        rows_kernel,
        [((5, 40, 128), F32), ((4, 24, 128), F32), ((64, 128), F32), ((64, 128), F32)],
        near, m1, p1, m2, p2,
    )
    from_left, from_right = passed(right, "gy", 1), passed(left, "gy", -1)
    field = pltpu.VMEM((ITERS + 1, 4, 24, 256), F32)
    grads, sums = call(
        skeleton_kernel,
        [((3, 4, 16, 256), F32), ((gy, 32, 128), F32)],
        conv_bias, features, main, labels, from_left, from_right,
        scratch=[field] * 5, smem=(0,),
    )
    sums = lax.all_to_all(sums, "gy", 0, 0, tiled=True)
    sums = call(add_kernel, [((gx, 32, 128), F32)], sums)[0]
    sums = lax.all_to_all(sums, "gx", 0, 0, tiled=True)

    def finish(*refs):
        final_kernel(*refs, voxels=voxels)

    loss, weight_grad, bias_grad, feature_grad = call(
        finish,
        [((1, 1), F32), ((27, 32), F32), ((1, 1), F32), ((32, 4, 8, 128), BF16)],
        sums, grads, matrix,
    )
    return (loss.reshape(()), weight_grad, bias_grad.reshape((1,)), feature_grad)


def solution(mesh):
    in_specs = (P(None, None, "gx", "gy"), P(None, "gx", "gy"), P(), P())
    out_specs = (P(), P(), P(), P(None, None, "gx", "gy"))
    return jax.shard_map(local, mesh=mesh, in_specs=in_specs, out_specs=out_specs, check_vma=False)
```

```python
import jax
import jax.numpy as jnp
from jax import lax
from jax.experimental import pallas as pl
from jax.experimental.pallas import tpu as pltpu
from jax.sharding import PartitionSpec as P

ITERS = 5
F32 = jnp.float32
BF16 = jnp.bfloat16
SHARP = 10.0
SOFT = 0.05
EDGE = 16
VMEM_LIMIT = 48 * 1024 * 1024


def iota(shape, dim):
    return lax.broadcasted_iota(jnp.int32, shape, dim)


def dot(a, b, dims, precision=None):
    return lax.dot_general(a, b, (dims, ((), ())), precision=precision, preferred_element_type=F32)


def edge_row(q):
    return jnp.where(q < 8, q, jnp.where(q == 8, 8, jnp.where(q == 15, -1, -100)))


def weight_matrix(w):
    spread = jnp.where((iota((32, 256), 1) >> 3) == iota((32, 256), 0), 1.0, 0.0).astype(BF16)
    by_lane = dot(w, spread, ((1,), (0,))).astype(BF16)
    row = iota((144, 27), 0)
    ad = row >> 4
    base = ad + 6 * (jnp.where(ad >= 3, 1, 0) + jnp.where(ad >= 6, 1, 0))
    col = iota((144, 27), 1)
    offset = (iota((144, 256), 1) & 7) - edge_row(iota((144, 256), 0) & 15) + 1
    matrix = jnp.zeros((144, 256), F32)
    for b in range(3):
        pick = jnp.where(col == base + 3 * b, 1.0, 0.0).astype(BF16)
        matrix = matrix + jnp.where(offset == b, dot(pick, by_lane, ((1,), (0,))), 0.0)
    return matrix.astype(BF16)


def partial_logits_kernel(
    w_hbm, f_hbm, lab_hbm, a_ref, near_ref, far_ref, w_ref, f_ref, lab_ref, sems
):
    pairs = [(w_hbm, w_ref), (f_hbm, f_ref), (lab_hbm, lab_ref)]
    copies = [pltpu.make_async_copy(x, y, sems.at[n]) for n, (x, y) in enumerate(pairs)]
    for copy in copies:
        copy.start()
    copies[0].wait()
    matrix = weight_matrix(w_ref[...])
    a_ref[...] = matrix
    copies[1].wait()
    lane = iota((16, 128), 1)
    terms = [
        dot(matrix, f_ref[:, z].reshape(256, 128), ((1,), (0,))).reshape(3, 3, 16, 128)
        for z in range(4)
    ]
    corner = jnp.zeros((16, 128), F32)
    for z in range(4):
        byd = []
        for d in range(3):
            byd.append(sum(terms[z + a - 1][a, d] for a in range(3) if 0 <= z + a - 1 < 4))
        main = byd[1]
        main = main + jnp.where(lane >= 1, pltpu.roll(byd[0], 1, 1), 0.0)
        main = main + jnp.where(lane <= 126, pltpu.roll(byd[2], 127, 1), 0.0)
        near_ref[16 * z : 16 * z + 16] = main
        far_ref[16 * z : 16 * z + 16] = main
        low, high = 16 * z, 16 * z + 15
        corner = jnp.where(lane == low, pltpu.roll(byd[0], low + 1, 1), corner)
        corner = jnp.where(lane == high, pltpu.roll(byd[2], high, 1), corner)
    near_ref[64:80] = corner
    far_ref[64:80] = corner
    copies[2].wait()
    near_ref[80:112] = lab_ref[...].reshape(32, 128).astype(F32)


def rows_kernel(
    own_ref, one_a_ref, one_b_ref, two_a_ref, two_b_ref, main_ref, lab_ref, send_a_ref, send_b_ref
):
    row_block, col_block = lax.axis_index("gx"), lax.axis_index("gy")
    even1 = (row_block & 1) == 0
    even2 = (row_block & 2) == 0
    even_col = (col_block & 1) == 0
    own = own_ref[...]
    one_a, one_b, two_a, two_b = one_a_ref[...], one_b_ref[...], two_a_ref[...], two_b_ref[...]
    before, after = jnp.where(even1, one_b, one_a), jnp.where(even1, one_a, one_b)
    blocks = [jnp.where(even2, two_b, two_a), before, own, after, jnp.where(even2, two_a, two_b)]
    sub = iota((8, 128), 0)

    def assemble(start):
        tiles = []
        for t in range(5):
            tile = blocks[t][start : start + 8]
            if t > 0:
                tile = tile + jnp.where(sub == 0, blocks[t - 1][start + 8 : start + 16], 0.0)
            if t < 4:
                tile = tile + jnp.where(sub == 7, blocks[t + 1][start + 8 : start + 16], 0.0)
            tiles.append(tile)
        return jnp.concatenate(tiles, axis=0)

    corner = assemble(64)
    main_ref[4] = corner
    lane = iota((40, 128), 1)
    right = jnp.zeros((40, 128), F32)
    left = jnp.zeros((40, 128), F32)
    for z in range(4):
        main = assemble(16 * z)
        main_ref[z] = main
        lab = jnp.concatenate([x[80 + 8 * z : 88 + 8 * z] for x in (before, own, after)], axis=0)
        lab_ref[z] = lab
        lab = jnp.concatenate([lab, jnp.zeros((16, 128), F32)], axis=0)
        right = jnp.where((lane >> 4) == z, pltpu.roll(main, 16 * z + 16, 1), right)
        right = jnp.where((lane >> 4) == z + 4, pltpu.roll(lab, (16 * z + 80) % 128, 1), right)
        left = jnp.where((lane >> 4) == z, pltpu.roll(main, 16 * z, 1), left)
        left = jnp.where((lane >> 4) == z + 4, pltpu.roll(lab, 16 * z + 64, 1), left)
    right = jnp.where((lane < 64) & ((lane & 15) == 0), corner, right)
    left = jnp.where((lane < 64) & ((lane & 15) == 15), corner, left)
    send_a_ref[...] = jnp.where(even_col, right, left)
    send_b_ref[...] = jnp.where(even_col, left, right)


def shift_rows(x, s):
    return pltpu.roll(x, s % x.shape[0], 0)


def shift_cols(x, s):
    return pltpu.roll(x, s % x.shape[1], 1)


def cross(fields, outside):
    result = []
    for z in range(4):
        x = fields[z]
        around = shift_rows(x, 1) + shift_rows(x, -1) + shift_cols(x, 1) + shift_cols(x, -1)
        before = fields[z - 1] if z > 0 else outside
        after = fields[z + 1] if z < 3 else outside
        result.append((around + (before + after)) * (1.0 / 9.0) + x * (1.0 / 3.0))
    return result


def box(fields, outside, crop):
    result = []
    for z in range(4):
        before = fields[z - 1] if z > 0 else outside
        after = fields[z + 1] if z < 3 else outside
        x = fields[z] + (before + after)
        x = x + shift_rows(x, 1) + shift_rows(x, -1)
        if crop:
            x = x[8:32]
        result.append(x + shift_cols(x, 1) + shift_cols(x, -1))
    return result


def inverse(x):
    return 1.0 / x


def forward(e0, q0, inside, crop, keep):
    def middle(x):
        return x[8:32] if crop else x

    e, q, s = e0, q0, None
    for i in range(ITERS + 1):
        e = [jnp.where(inside, x, 1.0) for x in cross(e, 1.0)]
        q_next = [inverse(x) for x in e]
        mean = box(q_next, 1.0, crop)
        s_next = []
        for z in range(4):
            d_inv = inverse(mean[z] * (1.0 / 27.0))
            qz = middle(q[z])
            ratio = qz * d_inv
            ratio = ratio * ratio
            log_term = jnp.log(1.0 + ratio)
            change = SOFT * log_term
            if i == 0:
                s_next.append(change)
                keep(i, z, qz, d_inv, ratio, None, None, None)
            else:
                rest = 1.0 - s[z]
                power = jnp.exp(log_term * rest)
                s_next.append(s[z] + SOFT * jnp.log(1.0 + power))
                keep(i, z, qz, d_inv, ratio, change, rest, power)
        s, q = s_next, q_next
    return s, q


def skeleton_kernel(
    bias_ref, f_ref, main_ref, lab_ref, got_a_ref, got_b_ref,
    grad_ref, sums_ref,
    qs_ref, ds_ref, rs_ref, gain_ref,
):
    row_ids = lax.axis_index("gx") * 8 - 16 + iota((40, 256), 0)
    lane = iota((40, 256), 1)
    col = jnp.where(lane < 144, lane, lane - 256)
    col_ids = lax.axis_index("gy") * 128 + col
    inside = (row_ids >= 0) & (row_ids < lax.axis_size("gx") * 8)
    inside = inside & (col_ids >= 0) & (col_ids < lax.axis_size("gy") * 128) & (col >= -16)
    inside_f = jnp.where(inside, 1.0, 0.0)
    inner = inside_f[8:32]
    inner_b = inner > 0.5
    bias = bias_ref[0]

    even_col = (lax.axis_index("gy") & 1) == 0
    from_left = jnp.where(even_col, got_b_ref[...], got_a_ref[...])
    from_right = jnp.where(even_col, got_a_ref[...], got_b_ref[...])
    corner = main_ref[4]
    lane40 = iota((40, 128), 1)
    lane24 = lane40[:24]
    e0, q0, slope, probs, labels = [], [], [], [], []
    for z in range(4):
        to_zero, to_last = (128 - 16 * z) % 128, 112 - 16 * z
        left_zero, left_last = pltpu.roll(from_left, to_zero, 1), pltpu.roll(from_left, to_last, 1)
        right_zero, right_last = pltpu.roll(from_right, to_zero, 1), pltpu.roll(from_right, to_last, 1)
        main = main_ref[z]
        main = main + jnp.where(lane40 == 0, left_zero, jnp.where(lane40 == 127, right_last, 0.0))
        tail = jnp.where(lane40 >= 112, left_last, jnp.where(lane40 < 16, right_zero, 0.0))
        own_zero, own_last = pltpu.roll(corner, to_zero, 1), pltpu.roll(corner, to_last, 1)
        tail = tail + jnp.where(lane40 == 0, own_zero, jnp.where(lane40 == 127, own_last, 0.0))
        lab_left = pltpu.roll(from_left[:24], 48 - 16 * z, 1)
        lab_right = pltpu.roll(from_right[:24], 64 - 16 * z, 1)
        lab_tail = jnp.where(lane24 >= 112, lab_left, jnp.where(lane24 < 16, lab_right, 0.0))
        logits = jnp.concatenate([main, tail], axis=1) + bias
        small = jnp.exp(-jnp.abs(logits))
        scale = inverse(1.0 + small)
        prob = jnp.where(logits >= 0.0, scale, small * scale)
        prob = jnp.where(inside, prob, 0.0)
        e = jnp.exp(-SHARP * prob)
        e0.append(e)
        q0.append(inverse(e))
        weight = (small * scale) * scale
        slope.append(((-SHARP) * e * weight)[8:32] * inner)
        probs.append((prob[8:32], weight[8:32]))
        labels.append(jnp.concatenate([lab_ref[z], lab_tail], axis=1))

    low, high = jnp.exp(-SHARP * jnp.ones((24, 256), F32)), jnp.exp(SHARP * jnp.ones((24, 256), F32))
    true_skel, _ = forward(
        [jnp.where(x > 0.5, low, 1.0) for x in labels],
        [jnp.where(x > 0.5, high, 1.0) for x in labels],
        inner_b, False, lambda *factors: None,
    )

    def keep(i, z, qz, d_inv, ratio, change, rest, power):
        qs_ref[i, z] = qz
        ds_ref[i, z] = d_inv
        part = (-2.0 * SOFT) * (ratio * inverse(1.0 + ratio))
        if i > 0:
            share = power * inverse(1.0 + power)
            part = part * (share * rest)
            gain_ref[i, z] = 1.0 - share * change
        rs_ref[i, z] = part

    pred_skel, q_last = forward(e0, q0, inside, True, keep)

    def own(x):
        return x[8:16, :128]

    def total(values):
        acc = values[0] + values[1] + values[2] + values[3]
        return jnp.sum(jnp.sum(acc, axis=1, keepdims=True), axis=0, keepdims=True)

    t0 = total([own(pred_skel[z] * labels[z]) for z in range(4)])
    t1 = total([own(pred_skel[z]) for z in range(4)])
    t2 = total([own(true_skel[z] * probs[z][0]) for z in range(4)])
    t3 = total([own(true_skel[z]) for z in range(4)])

    weights = [labels, [inner] * 4]
    running = [jnp.ones((24, 256), F32)] * 4
    deep = [None, None]
    for i in range(ITERS, -1, -1):
        coefs = []
        for z in range(4):
            coefs.append(rs_ref[i, z] * running[z])
            if i > 0:
                running[z] = running[z] * gain_ref[i, z]
        for f in range(2):
            scaled = [coefs[z] * weights[f][z] for z in range(4)]
            spread = box([scaled[z] * ds_ref[i, z] for z in range(4)], 0.0, False)
            q_of = [q_last[z][8:32] if i == ITERS else qs_ref[i + 1, z] for z in range(4)]
            incoming = []
            for z in range(4):
                value = spread[z] * (q_of[z] * q_of[z]) * (-1.0 / 27.0)
                if deep[f] is not None:
                    value = value + deep[f][z]
                incoming.append(value * inner)
            moved = cross(incoming, 0.0)
            deep[f] = [moved[z] + scaled[z] * qs_ref[i, z] for z in range(4)]
    fields = [
        [deep[0][z] * slope[z] for z in range(4)],
        [deep[1][z] * slope[z] for z in range(4)],
        [true_skel[z] * probs[z][1] * inner for z in range(4)],
    ]
    bias_sums = [total([own(x) for x in field]) for field in fields]

    sub = iota((8, 256), 0)
    stacks = []
    for z in range(4):
        pieces = []
        for f in range(3):
            x = fields[f][z]
            edge = jnp.where(sub == 0, x[16:24], jnp.where(sub == 7, x[0:8], 0.0))
            block = jnp.concatenate([x[8:16], edge], axis=0)
            grad_ref[f, z] = block
            for d in range(3):
                moved = (shift_cols(block, d - 1) if d != 1 else block)[:, :128]
                upper = moved.astype(BF16)
                lower = (moved - upper.astype(F32)).astype(BF16)
                pieces += [upper, lower]
        stacks.append(jnp.concatenate(pieces, axis=0))
    offset = (iota((16, 256), 1) & 7) - edge_row(iota((16, 256), 0)) + 1
    picked = {}
    for a in range(3):
        moments = jnp.zeros((288, 256), F32)
        for z in range(4):
            if 0 <= z + a - 1 < 4:
                feats = f_ref[:, z + a - 1].reshape(256, 128)
                moments = moments + dot(stacks[z], feats, ((1,), (1,)))
        for f in range(3):
            for d in range(3):
                start = (f * 3 + d) * 32
                pair = moments[start : start + 16] + moments[start + 16 : start + 32]
                for b in range(3):
                    chosen = jnp.where(offset == b, pair, 0.0)
                    picked[b, f, a, d] = jnp.sum(chosen, axis=0, keepdims=True)
    order = [(f, a, d) for f in range(3) for a in range(3) for d in range(3)]
    groups = [[picked[(b,) + at] for at in order[:24]] for b in range(3)]
    rest = [picked[(b,) + at] for b in range(3) for at in order[24:]]
    groups.append(rest + [jnp.zeros((15, 256), F32)])
    result = jnp.zeros((24, 128), F32)
    for b in range(4):
        stacked = jnp.concatenate(groups[b], axis=0)
        collect = jnp.where((iota((256, 128), 0) >> 3) + 32 * b == iota((256, 128), 1), 1.0, 0.0)
        result = result + dot(stacked, collect, ((1,), (0,)), precision=lax.Precision.HIGHEST)
    row24, lane_of = iota((24, 128), 0), iota((24, 128), 1)
    for k, value in enumerate([t0, t1, t2, t3] + bias_sums):
        result = jnp.where((row24 == 23) & (lane_of == 96 + k), value, result)
    for n in range(sums_ref.shape[0]):
        sums_ref[n] = result


def add_kernel(in_ref, out_ref):
    acc = in_ref[0]
    for n in range(1, in_ref.shape[0]):
        acc = acc + in_ref[n]
    for n in range(out_ref.shape[0]):
        out_ref[n] = acc


def final_kernel(in_ref, grad_ref, a_ref, loss_ref, weight_ref, bias_ref, out_ref, *, voxels):
    acc = in_ref[0]
    for n in range(1, in_ref.shape[0]):
        acc = acc + in_ref[n]
    sums = [acc[23:24, 96 + k : 97 + k] for k in range(7)]
    precision = (sums[0] + 1.0) / (sums[1] + 1.0)
    sensitivity = (sums[2] + 1.0) / (sums[3] + 1.0)
    both = precision + sensitivity
    loss_ref[...] = 1.0 - 2.0 * precision * sensitivity / both
    by_precision = -2.0 * (sensitivity / both) * (sensitivity / both)
    by_sensitivity = -2.0 * (precision / both) * (precision / both)
    slopes = [
        by_precision / (sums[1] + 1.0),
        -by_precision * precision / (sums[1] + 1.0),
        by_sensitivity / (sums[3] + 1.0),
    ]
    bias_ref[...] = slopes[0] * sums[4] + slopes[1] * sums[5] + slopes[2] * sums[6]
    group = iota((3, 128), 1) >> 5
    last = acc[18:21]
    for b in range(3):
        last = jnp.where(group == b, pltpu.roll(acc[3 * b : 3 * b + 3], (32 * b + 32) % 128, 1), last)
    third = jnp.concatenate([acc[18:24], last], axis=0)
    weight = slopes[0] * acc[0:9] + slopes[1] * acc[9:18] + slopes[2] * third
    for b in range(3):
        part = weight if b == 0 else pltpu.roll(weight, 128 - 32 * b, 1)
        for a in range(3):
            weight_ref[9 * a + 3 * b : 9 * a + 3 * b + 3] = part[3 * a : 3 * a + 3, :32]
    matrix = a_ref[...]
    parts = []
    for z in range(4):
        block = slopes[0] * grad_ref[0, z] + slopes[1] * grad_ref[1, z] + slopes[2] * grad_ref[2, z]
        block = block * voxels
        byd = []
        for d in range(3):
            moved = (shift_cols(block, d - 1) if d != 1 else block)[:, :128]
            upper = moved.astype(BF16)
            byd.append((upper, (moved - upper.astype(F32)).astype(BF16)))
        parts.append(byd)
    none = jnp.zeros((16, 128), BF16)
    for z in range(4):
        acc_z = None
        for level in range(2):
            stack = []
            for a in range(3):
                for d in range(3):
                    at = z - a + 1
                    stack.append(parts[at][d][level] if 0 <= at < 4 else none)
            term = dot(matrix, jnp.concatenate(stack, axis=0), ((0,), (0,)))
            acc_z = term if acc_z is None else acc_z + term
        out_ref[:, z] = acc_z.reshape(32, 8, 128).astype(BF16)


def call(kernel, out_shapes, *args, scratch=(), spaces={}):
    spec = pl.BlockSpec(memory_space=pltpu.VMEM)
    in_specs = [pl.BlockSpec(memory_space=spaces.get(n, pltpu.VMEM)) for n in range(len(args))]
    return pl.pallas_call(
        kernel,
        out_shape=[jax.ShapeDtypeStruct(shape, dtype) for shape, dtype in out_shapes],
        in_specs=in_specs,
        out_specs=[spec] * len(out_shapes),
        scratch_shapes=list(scratch),
        compiler_params=pltpu.CompilerParams(vmem_limit_bytes=VMEM_LIMIT),
    )(*args)


def swapped(x, axis, step, phase):
    count = lax.axis_size(axis)
    pairs = []
    for n in range(count - step):
        if (n // step) % 2 == phase:
            pairs += [(n, n + step), (n + step, n)]
    return lax.ppermute(x, axis, pairs)


def local(features, vessel_label, conv_weight, conv_bias):
    gx, gy = lax.axis_size("gx"), lax.axis_size("gy")
    voxels = float(4 * 8 * gx * 128 * gy)
    matrix, near, far = call(
        partial_logits_kernel,
        [((144, 256), BF16), ((112, 128), F32), ((80, 128), F32)],
        *[pltpu.with_memory_space_constraint(x, pltpu.HBM) for x in (conv_weight, features, vessel_label)],
        scratch=[
            pltpu.VMEM((27, 32), BF16),
            pltpu.VMEM((32, 4, 8, 128), BF16),
            pltpu.VMEM((4, 8, 128), jnp.int32),
            pltpu.SemaphoreType.DMA((3,)),
        ],
        spaces={0: pltpu.HBM, 1: pltpu.HBM, 2: pltpu.HBM},
    )
    two = [swapped(far, "gx", 2, phase) for phase in range(2)]
    one = [swapped(near, "gx", 1, phase) for phase in range(2)]
    main, labels, send_a, send_b = call(
        rows_kernel,
        [((5, 40, 128), F32), ((4, 24, 128), F32), ((40, 128), F32), ((40, 128), F32)],
        near, *one, *two,
    )
    got = [swapped(send_a, "gy", 1, 0), swapped(send_b, "gy", 1, 1)]
    field = pltpu.VMEM((ITERS + 1, 4, 24, 256), F32)
    grads, sums = call(
        skeleton_kernel,
        [((3, 4, 16, 256), F32), ((gy, 24, 128), F32)],
        conv_bias, features, main, labels, *got,
        scratch=[field] * 4, spaces={0: pltpu.SMEM},
    )
    sums = lax.all_to_all(sums, "gy", 0, 0, tiled=True)
    sums = call(add_kernel, [((gx, 24, 128), F32)], sums)[0]
    sums = lax.all_to_all(sums, "gx", 0, 0, tiled=True)

    def finish(*refs):
        final_kernel(*refs, voxels=voxels)

    loss, weight_grad, bias_grad, feature_grad = call(
        finish,
        [((1, 1), F32), ((27, 32), F32), ((1, 1), F32), ((32, 4, 8, 128), BF16)],
        sums, grads, matrix,
    )
    return (loss.reshape(()), weight_grad, bias_grad.reshape((1,)), feature_grad)


def solution(mesh):
    in_specs = (P(None, None, "gx", "gy"), P(None, "gx", "gy"), P(), P())
    out_specs = (P(), P(), P(), P(None, None, "gx", "gy"))
    return jax.shard_map(local, mesh=mesh, in_specs=in_specs, out_specs=out_specs, check_vma=False)
```

```python
import jax
import jax.numpy as jnp
from jax import lax
from jax.experimental import pallas as pl
from jax.experimental.pallas import tpu as pltpu
from jax.sharding import PartitionSpec as P

ITERS = 5
F32 = jnp.float32
BF16 = jnp.bfloat16
SHARP = 10.0
SOFT = 0.05
EDGE = 16
VMEM_LIMIT = 24 * 1024 * 1024


def iota(shape, dim):
    return lax.broadcasted_iota(jnp.int32, shape, dim)


def dot(a, b, dims, precision=None):
    return lax.dot_general(a, b, (dims, ((), ())), precision=precision, preferred_element_type=F32)


def edge_row(q):
    return jnp.where(q < 8, q, jnp.where(q == 8, 8, jnp.where(q == 15, -1, -100)))


def weight_matrix(w):
    spread = jnp.where((iota((32, 256), 1) >> 3) == iota((32, 256), 0), 1.0, 0.0).astype(BF16)
    by_lane = dot(w, spread, ((1,), (0,))).astype(BF16)
    row = iota((144, 27), 0)
    ad = row >> 4
    base = ad + 6 * (jnp.where(ad >= 3, 1, 0) + jnp.where(ad >= 6, 1, 0))
    col = iota((144, 27), 1)
    offset = (iota((144, 256), 1) & 7) - edge_row(iota((144, 256), 0) & 15) + 1
    matrix = jnp.zeros((144, 256), F32)
    for b in range(3):
        pick = jnp.where(col == base + 3 * b, 1.0, 0.0).astype(BF16)
        matrix = matrix + jnp.where(offset == b, dot(pick, by_lane, ((1,), (0,))), 0.0)
    return matrix.astype(BF16)


def turned(x, s):
    return x if s == 0 else pltpu.roll(x, s % x.shape[0], 0)


def at_end(lane):
    return ((lane & 15) == 0) | ((lane & 15) == 15)


def partial_logits_kernel(
    w_hbm, f_hbm, lab_hbm, a_ref, near_ref, far_ref, f_ref, w_ref, lab_ref, sems
):
    pairs = [(w_hbm, w_ref), (f_hbm, f_ref), (lab_hbm, lab_ref)]
    copies = [pltpu.make_async_copy(x, y, sems.at[n]) for n, (x, y) in enumerate(pairs)]
    for copy in copies:
        copy.start()
    copies[0].wait()
    matrix = weight_matrix(w_ref[...])
    a_ref[...] = matrix
    copies[1].wait()
    lane = iota((16, 128), 1)
    sub = iota((8, 128), 0)
    terms = [
        dot(matrix, f_ref[:, z].reshape(256, 128), ((1,), (0,))).reshape(3, 3, 16, 128)
        for z in range(4)
    ]
    corner = jnp.zeros((16, 128), F32)
    edges = jnp.zeros((8, 128), F32)
    for z in range(4):
        byd = []
        for d in range(3):
            byd.append(sum(terms[z + a - 1][a, d] for a in range(3) if 0 <= z + a - 1 < 4))
        main = byd[1]
        main = main + jnp.where(lane >= 1, pltpu.roll(byd[0], 1, 1), 0.0)
        main = main + jnp.where(lane <= 126, pltpu.roll(byd[2], 127, 1), 0.0)
        near_ref[8 * z : 8 * z + 8] = main[:8]
        far_ref[8 * z : 8 * z + 8] = main[:8]
        edges = jnp.where(sub == z, turned(main[8:], z), edges)
        edges = jnp.where(sub == 7 - z, turned(main[8:], -z), edges)
        low, high = 16 * z, 16 * z + 15
        corner = jnp.where(lane == low, pltpu.roll(byd[0], low + 1, 1), corner)
        corner = jnp.where(lane == high, pltpu.roll(byd[2], high, 1), corner)
    corners = jnp.where(at_end(lane[:8]), corner[:8], pltpu.roll(corner[8:], 2, 1))
    near_ref[32:40] = edges
    far_ref[32:40] = edges
    near_ref[40:48] = corners
    far_ref[40:48] = corners
    copies[2].wait()
    near_ref[48:80] = lab_ref[...].reshape(32, 128).astype(F32)


def rows_kernel(
    own_ref, one_a_ref, one_b_ref, two_a_ref, two_b_ref, main_ref, lab_ref, send_a_ref, send_b_ref
):
    row_block, col_block = lax.axis_index("gx"), lax.axis_index("gy")
    even1 = (row_block & 1) == 0
    even2 = (row_block & 2) == 0
    even_col = (col_block & 1) == 0
    own = own_ref[...]
    one_a, one_b, two_a, two_b = one_a_ref[...], one_b_ref[...], two_a_ref[...], two_b_ref[...]
    before, after = jnp.where(even1, one_b, one_a), jnp.where(even1, one_a, one_b)
    blocks = [jnp.where(even2, two_b, two_a), before, own, after, jnp.where(even2, two_a, two_b)]
    sub = iota((8, 128), 0)
    ends = at_end(iota((8, 128), 1))

    def assemble(tiles, firsts, lasts):
        result = []
        for t in range(5):
            tile = tiles[t]
            if t > 0:
                tile = tile + jnp.where(sub == 0, firsts[t - 1], 0.0)
            if t < 4:
                tile = tile + jnp.where(sub == 7, lasts[t + 1], 0.0)
            result.append(tile)
        return jnp.concatenate(result, axis=0)

    corners = [jnp.where(ends, x[40:48], 0.0) for x in blocks]
    beyond = [jnp.where(ends, pltpu.roll(x[40:48], 126, 1), 0.0) for x in blocks]
    corner = assemble(corners, beyond, beyond)
    main_ref[4] = corner
    lane = iota((40, 128), 1)
    right = jnp.zeros((40, 128), F32)
    left = jnp.zeros((40, 128), F32)
    for z in range(4):
        main = assemble(
            [x[8 * z : 8 * z + 8] for x in blocks],
            [turned(x[32:40], -z) for x in blocks],
            [turned(x[32:40], z) for x in blocks],
        )
        main_ref[z] = main
        lab = jnp.concatenate([x[48 + 8 * z : 56 + 8 * z] for x in (before, own, after)], axis=0)
        lab_ref[z] = lab
        lab = jnp.concatenate([lab, jnp.zeros((16, 128), F32)], axis=0)
        right = jnp.where((lane >> 4) == z, pltpu.roll(main, 16 * z + 16, 1), right)
        right = jnp.where((lane >> 4) == z + 4, pltpu.roll(lab, (16 * z + 80) % 128, 1), right)
        left = jnp.where((lane >> 4) == z, pltpu.roll(main, 16 * z, 1), left)
        left = jnp.where((lane >> 4) == z + 4, pltpu.roll(lab, 16 * z + 64, 1), left)
    right = jnp.where((lane < 64) & ((lane & 15) == 0), corner, right)
    left = jnp.where((lane < 64) & ((lane & 15) == 15), corner, left)
    send_a_ref[...] = jnp.where(even_col, right, left)
    send_b_ref[...] = jnp.where(even_col, left, right)


def shift_rows(x, s):
    return pltpu.roll(x, s % x.shape[0], 0)


def shift_cols(x, s):
    return pltpu.roll(x, s % x.shape[1], 1)


def cross(fields, outside):
    result = []
    for z in range(4):
        x = fields[z]
        around = shift_rows(x, 1) + shift_rows(x, -1) + shift_cols(x, 1) + shift_cols(x, -1)
        before = fields[z - 1] if z > 0 else outside
        after = fields[z + 1] if z < 3 else outside
        result.append((around + (before + after)) * (1.0 / 9.0) + x * (1.0 / 3.0))
    return result


def box(fields, outside, crop):
    result = []
    for z in range(4):
        before = fields[z - 1] if z > 0 else outside
        after = fields[z + 1] if z < 3 else outside
        x = fields[z] + (before + after)
        x = x + shift_rows(x, 1) + shift_rows(x, -1)
        if crop:
            x = x[8:32]
        result.append(x + shift_cols(x, 1) + shift_cols(x, -1))
    return result


def inverse(x):
    return 1.0 / x


def forward(e0, q0, inside, crop, keep):
    def middle(x):
        return x[8:32] if crop else x

    e, q, s = e0, q0, None
    for i in range(ITERS + 1):
        e = [jnp.where(inside, x, 1.0) for x in cross(e, 1.0)]
        q_next = [inverse(x) for x in e]
        mean = box(q_next, 1.0, crop)
        s_next = []
        for z in range(4):
            d_inv = inverse(mean[z] * (1.0 / 27.0))
            qz = middle(q[z])
            ratio = qz * d_inv
            ratio = ratio * ratio
            log_term = jnp.log(1.0 + ratio)
            change = SOFT * log_term
            if i == 0:
                s_next.append(change)
                keep(i, z, qz, d_inv, ratio, None, None, None)
            else:
                rest = 1.0 - s[z]
                power = jnp.exp(log_term * rest)
                s_next.append(s[z] + SOFT * jnp.log(1.0 + power))
                keep(i, z, qz, d_inv, ratio, change, rest, power)
        s, q = s_next, q_next
    return s, q


def skeleton_kernel(
    bias_ref, f_ref, main_ref, lab_ref, got_a_ref, got_b_ref,
    grad_ref, sums_ref,
    qs_ref, ds_ref, rs_ref, gain_ref,
):
    row_ids = lax.axis_index("gx") * 8 - 16 + iota((40, 256), 0)
    lane = iota((40, 256), 1)
    col = jnp.where(lane < 144, lane, lane - 256)
    col_ids = lax.axis_index("gy") * 128 + col
    inside = (row_ids >= 0) & (row_ids < lax.axis_size("gx") * 8)
    inside = inside & (col_ids >= 0) & (col_ids < lax.axis_size("gy") * 128) & (col >= -16)
    inside_f = jnp.where(inside, 1.0, 0.0)
    inner = inside_f[8:32]
    inner_b = inner > 0.5
    bias = bias_ref[0]

    even_col = (lax.axis_index("gy") & 1) == 0
    from_left = jnp.where(even_col, got_b_ref[...], got_a_ref[...])
    from_right = jnp.where(even_col, got_a_ref[...], got_b_ref[...])
    corner = main_ref[4]
    lane40 = iota((40, 128), 1)
    lane24 = lane40[:24]
    e0, q0, slope, probs, labels = [], [], [], [], []
    for z in range(4):
        to_zero, to_last = (128 - 16 * z) % 128, 112 - 16 * z
        left_zero, left_last = pltpu.roll(from_left, to_zero, 1), pltpu.roll(from_left, to_last, 1)
        right_zero, right_last = pltpu.roll(from_right, to_zero, 1), pltpu.roll(from_right, to_last, 1)
        main = main_ref[z]
        main = main + jnp.where(lane40 == 0, left_zero, jnp.where(lane40 == 127, right_last, 0.0))
        tail = jnp.where(lane40 >= 112, left_last, jnp.where(lane40 < 16, right_zero, 0.0))
        own_zero, own_last = pltpu.roll(corner, to_zero, 1), pltpu.roll(corner, to_last, 1)
        tail = tail + jnp.where(lane40 == 0, own_zero, jnp.where(lane40 == 127, own_last, 0.0))
        lab_left = pltpu.roll(from_left[:24], 48 - 16 * z, 1)
        lab_right = pltpu.roll(from_right[:24], 64 - 16 * z, 1)
        lab_tail = jnp.where(lane24 >= 112, lab_left, jnp.where(lane24 < 16, lab_right, 0.0))
        logits = jnp.concatenate([main, tail], axis=1) + bias
        small = jnp.exp(-jnp.abs(logits))
        scale = inverse(1.0 + small)
        prob = jnp.where(logits >= 0.0, scale, small * scale)
        prob = jnp.where(inside, prob, 0.0)
        e = jnp.exp(-SHARP * prob)
        e0.append(e)
        q0.append(inverse(e))
        weight = (small * scale) * scale
        slope.append(((-SHARP) * e * weight)[8:32] * inner)
        probs.append((prob[8:32], weight[8:32]))
        labels.append(jnp.concatenate([lab_ref[z], lab_tail], axis=1))

    low, high = jnp.exp(-SHARP * jnp.ones((24, 256), F32)), jnp.exp(SHARP * jnp.ones((24, 256), F32))
    true_skel, _ = forward(
        [jnp.where(x > 0.5, low, 1.0) for x in labels],
        [jnp.where(x > 0.5, high, 1.0) for x in labels],
        inner_b, False, lambda *factors: None,
    )

    def keep(i, z, qz, d_inv, ratio, change, rest, power):
        qs_ref[i, z] = qz
        ds_ref[i, z] = d_inv
        part = (-2.0 * SOFT) * (ratio * inverse(1.0 + ratio))
        if i > 0:
            share = power * inverse(1.0 + power)
            part = part * (share * rest)
            gain_ref[i, z] = 1.0 - share * change
        rs_ref[i, z] = part

    pred_skel, q_last = forward(e0, q0, inside, True, keep)

    def own(x):
        return x[8:16, :128]

    def total(values):
        acc = values[0] + values[1] + values[2] + values[3]
        return jnp.sum(jnp.sum(acc, axis=1, keepdims=True), axis=0, keepdims=True)

    t0 = total([own(pred_skel[z] * labels[z]) for z in range(4)])
    t1 = total([own(pred_skel[z]) for z in range(4)])
    t2 = total([own(true_skel[z] * probs[z][0]) for z in range(4)])
    t3 = total([own(true_skel[z]) for z in range(4)])

    weights = [labels, [inner] * 4]
    running = [jnp.ones((24, 256), F32)] * 4
    deep = [None, None]
    for i in range(ITERS, -1, -1):
        coefs = []
        for z in range(4):
            coefs.append(rs_ref[i, z] * running[z])
            if i > 0:
                running[z] = running[z] * gain_ref[i, z]
        for f in range(2):
            scaled = [coefs[z] * weights[f][z] for z in range(4)]
            spread = box([scaled[z] * ds_ref[i, z] for z in range(4)], 0.0, False)
            q_of = [q_last[z][8:32] if i == ITERS else qs_ref[i + 1, z] for z in range(4)]
            incoming = []
            for z in range(4):
                value = spread[z] * (q_of[z] * q_of[z]) * (-1.0 / 27.0)
                if deep[f] is not None:
                    value = value + deep[f][z]
                incoming.append(value * inner)
            moved = cross(incoming, 0.0)
            deep[f] = [moved[z] + scaled[z] * qs_ref[i, z] for z in range(4)]
    fields = [
        [deep[0][z] * slope[z] for z in range(4)],
        [deep[1][z] * slope[z] for z in range(4)],
        [true_skel[z] * probs[z][1] * inner for z in range(4)],
    ]
    bias_sums = [total([own(x) for x in field]) for field in fields]

    sub = iota((8, 256), 0)
    stacks = []
    for z in range(4):
        pieces = []
        for f in range(3):
            x = fields[f][z]
            edge = jnp.where(sub == 0, x[16:24], jnp.where(sub == 7, x[0:8], 0.0))
            block = jnp.concatenate([x[8:16], edge], axis=0)
            grad_ref[f, z] = block
            for d in range(3):
                moved = (shift_cols(block, d - 1) if d != 1 else block)[:, :128]
                upper = moved.astype(BF16)
                lower = (moved - upper.astype(F32)).astype(BF16)
                pieces += [upper, lower]
        stacks.append(jnp.concatenate(pieces, axis=0))
    offset = (iota((16, 256), 1) & 7) - edge_row(iota((16, 256), 0)) + 1
    picked = {}
    for a in range(3):
        moments = jnp.zeros((288, 256), F32)
        for z in range(4):
            if 0 <= z + a - 1 < 4:
                feats = f_ref[:, z + a - 1].reshape(256, 128)
                moments = moments + dot(stacks[z], feats, ((1,), (1,)))
        for f in range(3):
            for d in range(3):
                start = (f * 3 + d) * 32
                pair = moments[start : start + 16] + moments[start + 16 : start + 32]
                for b in range(3):
                    chosen = jnp.where(offset == b, pair, 0.0)
                    picked[b, f, a, d] = jnp.sum(chosen, axis=0, keepdims=True)
    order = [(f, a, d) for f in range(3) for a in range(3) for d in range(3)]
    groups = [[picked[(b,) + at] for at in order[:24]] for b in range(3)]
    rest = [picked[(b,) + at] for b in range(3) for at in order[24:]]
    groups.append(rest + [jnp.zeros((15, 256), F32)])
    result = jnp.zeros((24, 128), F32)
    for b in range(4):
        stacked = jnp.concatenate(groups[b], axis=0)
        collect = jnp.where((iota((256, 128), 0) >> 3) + 32 * b == iota((256, 128), 1), 1.0, 0.0)
        result = result + dot(stacked, collect, ((1,), (0,)), precision=lax.Precision.HIGHEST)
    row24, lane_of = iota((24, 128), 0), iota((24, 128), 1)
    for k, value in enumerate([t0, t1, t2, t3] + bias_sums):
        result = jnp.where((row24 == 23) & (lane_of == 96 + k), value, result)
    for n in range(sums_ref.shape[0]):
        sums_ref[n] = result


def add_kernel(in_ref, out_ref):
    acc = in_ref[0]
    for n in range(1, in_ref.shape[0]):
        acc = acc + in_ref[n]
    for n in range(out_ref.shape[0]):
        out_ref[n] = acc


def final_kernel(in_ref, part_ref, loss_ref, weight_ref, bias_ref, out_ref, *, voxels):
    acc = in_ref[0]
    for n in range(1, in_ref.shape[0]):
        acc = acc + in_ref[n]
    sums = [acc[23:24, 96 + k : 97 + k] for k in range(7)]
    precision = (sums[0] + 1.0) / (sums[1] + 1.0)
    sensitivity = (sums[2] + 1.0) / (sums[3] + 1.0)
    both = precision + sensitivity
    loss_ref[...] = 1.0 - 2.0 * precision * sensitivity / both
    by_precision = -2.0 * (sensitivity / both) * (sensitivity / both)
    by_sensitivity = -2.0 * (precision / both) * (precision / both)
    slopes = [
        by_precision / (sums[1] + 1.0),
        -by_precision * precision / (sums[1] + 1.0),
        by_sensitivity / (sums[3] + 1.0),
    ]
    bias_ref[...] = slopes[0] * sums[4] + slopes[1] * sums[5] + slopes[2] * sums[6]
    group = iota((3, 128), 1) >> 5
    last = acc[18:21]
    for b in range(3):
        last = jnp.where(group == b, pltpu.roll(acc[3 * b : 3 * b + 3], (32 * b + 32) % 128, 1), last)
    third = jnp.concatenate([acc[18:24], last], axis=0)
    weight = slopes[0] * acc[0:9] + slopes[1] * acc[9:18] + slopes[2] * third
    for b in range(3):
        part = weight if b == 0 else pltpu.roll(weight, 128 - 32 * b, 1)
        for a in range(3):
            weight_ref[9 * a + 3 * b : 9 * a + 3 * b + 3] = part[3 * a : 3 * a + 3, :32]
    for z in range(4):
        value = slopes[0] * part_ref[0, z] + slopes[1] * part_ref[1, z] + slopes[2] * part_ref[2, z]
        out_ref[:, z] = (value * voxels).reshape(32, 8, 128).astype(BF16)


def feature_kernel(grad_ref, a_ref, part_ref):
    matrix = a_ref[...]
    none = jnp.zeros((16, 128), BF16)
    for f in range(3):
        parts = []
        for z in range(4):
            block = grad_ref[f, z]
            byd = []
            for d in range(3):
                moved = (shift_cols(block, d - 1) if d != 1 else block)[:, :128]
                upper = moved.astype(BF16)
                byd.append((upper, (moved - upper.astype(F32)).astype(BF16)))
            parts.append(byd)
        for z in range(4):
            acc = None
            for level in range(2):
                stack = []
                for a in range(3):
                    for d in range(3):
                        at = z - a + 1
                        stack.append(parts[at][d][level] if 0 <= at < 4 else none)
                term = dot(matrix, jnp.concatenate(stack, axis=0), ((0,), (0,)))
                acc = term if acc is None else acc + term
            part_ref[f, z] = acc


def call(kernel, out_shapes, *args, scratch=(), spaces={}, cost=None):
    spec = pl.BlockSpec(memory_space=pltpu.VMEM)
    in_specs = [pl.BlockSpec(memory_space=spaces.get(n, pltpu.VMEM)) for n in range(len(args))]
    return pl.pallas_call(
        kernel,
        out_shape=[jax.ShapeDtypeStruct(shape, dtype) for shape, dtype in out_shapes],
        in_specs=in_specs,
        out_specs=[spec] * len(out_shapes),
        scratch_shapes=list(scratch),
        cost_estimate=cost and pl.CostEstimate(flops=1000 * cost, bytes_accessed=cost, transcendentals=0),
        compiler_params=pltpu.CompilerParams(vmem_limit_bytes=VMEM_LIMIT),
    )(*args)


def swapped(x, axis, step, phase):
    count = lax.axis_size(axis)
    pairs = []
    for n in range(count - step):
        if (n // step) % 2 == phase:
            pairs += [(n, n + step), (n + step, n)]
    return lax.ppermute(x, axis, pairs)


def local(features, vessel_label, conv_weight, conv_bias):
    gx, gy = lax.axis_size("gx"), lax.axis_size("gy")
    voxels = float(4 * 8 * gx * 128 * gy)
    matrix, near, far, features = call(
        partial_logits_kernel,
        [((144, 256), BF16), ((80, 128), F32), ((48, 128), F32), (features.shape, BF16)],
        *[pltpu.with_memory_space_constraint(x, pltpu.HBM) for x in (conv_weight, features, vessel_label)],
        scratch=[
            pltpu.VMEM((27, 32), BF16),
            pltpu.VMEM((4, 8, 128), jnp.int32),
            pltpu.SemaphoreType.DMA((3,)),
        ],
        spaces={0: pltpu.HBM, 1: pltpu.HBM, 2: pltpu.HBM},
    )
    two = [swapped(far, "gx", 2, phase) for phase in range(2)]
    one = [swapped(near, "gx", 1, phase) for phase in range(2)]
    main, labels, send_a, send_b = call(
        rows_kernel,
        [((5, 40, 128), F32), ((4, 24, 128), F32), ((40, 128), F32), ((40, 128), F32)],
        near, *one, *two,
    )
    got = [swapped(send_a, "gy", 1, 0), swapped(send_b, "gy", 1, 1)]
    field = pltpu.VMEM((ITERS + 1, 4, 24, 256), F32)
    grads, sums = call(
        skeleton_kernel,
        [((3, 4, 16, 256), F32), ((gy, 24, 128), F32)],
        conv_bias, features, main, labels, *got,
        scratch=[field] * 4, spaces={0: pltpu.SMEM},
    )
    parts = call(feature_kernel, [((3, 4, 256, 128), F32)], grads, matrix, cost=2000000)[0]
    sums = lax.all_to_all(sums, "gy", 0, 0, tiled=True)
    sums = call(add_kernel, [((gx, 24, 128), F32)], sums)[0]
    sums = lax.all_to_all(sums, "gx", 0, 0, tiled=True)

    def finish(*refs):
        final_kernel(*refs, voxels=voxels)

    loss, weight_grad, bias_grad, feature_grad = call(
        finish,
        [((1, 1), F32), ((27, 32), F32), ((1, 1), F32), ((32, 4, 8, 128), BF16)],
        sums, parts,
    )
    return (loss.reshape(()), weight_grad, bias_grad.reshape((1,)), feature_grad)


def solution(mesh):
    in_specs = (P(None, None, "gx", "gy"), P(None, "gx", "gy"), P(), P())
    out_specs = (P(), P(), P(), P(None, None, "gx", "gy"))
    return jax.shard_map(local, mesh=mesh, in_specs=in_specs, out_specs=out_specs, check_vma=False)
```

```python
import jax
import jax.numpy as jnp
from jax import lax
from jax.experimental import pallas as pl
from jax.experimental.pallas import tpu as pltpu
from jax.sharding import PartitionSpec as P

ITERS = 5
F32 = jnp.float32
BF16 = jnp.bfloat16
SHARP = 10.0
SOFT = 0.05
EDGE = 16
VMEM_LIMIT = 24 * 1024 * 1024


def iota(shape, dim):
    return lax.broadcasted_iota(jnp.int32, shape, dim)


def dot(a, b, dims, precision=None):
    return lax.dot_general(a, b, (dims, ((), ())), precision=precision, preferred_element_type=F32)


def edge_row(q):
    return jnp.where(q < 8, q, jnp.where(q == 8, 8, jnp.where(q == 15, -1, -100)))


def weight_matrix(w):
    spread = jnp.where((iota((32, 256), 1) >> 3) == iota((32, 256), 0), 1.0, 0.0).astype(BF16)
    by_lane = dot(w, spread, ((1,), (0,))).astype(BF16)
    row = iota((144, 27), 0)
    ad = row >> 4
    base = ad + 6 * (jnp.where(ad >= 3, 1, 0) + jnp.where(ad >= 6, 1, 0))
    col = iota((144, 27), 1)
    offset = (iota((144, 256), 1) & 7) - edge_row(iota((144, 256), 0) & 15) + 1
    matrix = jnp.zeros((144, 256), F32)
    for b in range(3):
        pick = jnp.where(col == base + 3 * b, 1.0, 0.0).astype(BF16)
        matrix = matrix + jnp.where(offset == b, dot(pick, by_lane, ((1,), (0,))), 0.0)
    return matrix.astype(BF16)


def turned(x, s):
    return x if s == 0 else pltpu.roll(x, s % x.shape[0], 0)


def at_end(lane):
    return ((lane & 15) == 0) | ((lane & 15) == 15)


def partial_logits_kernel(
    w_hbm, f_hbm, lab_hbm, a_ref, near_ref, far_ref, f_ref, w_ref, lab_ref, sems
):
    pairs = [(w_hbm, w_ref), (f_hbm, f_ref), (lab_hbm, lab_ref)]
    copies = [pltpu.make_async_copy(x, y, sems.at[n]) for n, (x, y) in enumerate(pairs)]
    for copy in copies:
        copy.start()
    copies[0].wait()
    matrix = weight_matrix(w_ref[...])
    a_ref[...] = matrix
    copies[1].wait()
    lane = iota((16, 128), 1)
    sub = iota((8, 128), 0)
    terms = [
        dot(matrix, f_ref[:, z].reshape(256, 128), ((1,), (0,))).reshape(3, 3, 16, 128)
        for z in range(4)
    ]
    corner = jnp.zeros((16, 128), F32)
    edges = jnp.zeros((8, 128), F32)
    for z in range(4):
        byd = []
        for d in range(3):
            byd.append(sum(terms[z + a - 1][a, d] for a in range(3) if 0 <= z + a - 1 < 4))
        main = byd[1]
        main = main + jnp.where(lane >= 1, pltpu.roll(byd[0], 1, 1), 0.0)
        main = main + jnp.where(lane <= 126, pltpu.roll(byd[2], 127, 1), 0.0)
        near_ref[8 * z : 8 * z + 8] = main[:8]
        far_ref[8 * z : 8 * z + 8] = main[:8]
        edges = jnp.where(sub == z, turned(main[8:], z), edges)
        edges = jnp.where(sub == 7 - z, turned(main[8:], -z), edges)
        low, high = 16 * z, 16 * z + 15
        corner = jnp.where(lane == low, pltpu.roll(byd[0], low + 1, 1), corner)
        corner = jnp.where(lane == high, pltpu.roll(byd[2], high, 1), corner)
    corners = jnp.where(at_end(lane[:8]), corner[:8], pltpu.roll(corner[8:], 2, 1))
    near_ref[32:40] = edges
    far_ref[32:40] = edges
    near_ref[40:48] = corners
    far_ref[40:48] = corners
    copies[2].wait()
    near_ref[48:80] = lab_ref[...].reshape(32, 128).astype(F32)


def rows_kernel(
    own_ref, one_a_ref, one_b_ref, two_a_ref, two_b_ref, main_ref, lab_ref, send_a_ref, send_b_ref
):
    row_block, col_block = lax.axis_index("gx"), lax.axis_index("gy")
    even1 = (row_block & 1) == 0
    even2 = (row_block & 2) == 0
    even_col = (col_block & 1) == 0
    own = own_ref[...]
    one_a, one_b, two_a, two_b = one_a_ref[...], one_b_ref[...], two_a_ref[...], two_b_ref[...]
    before, after = jnp.where(even1, one_b, one_a), jnp.where(even1, one_a, one_b)
    blocks = [jnp.where(even2, two_b, two_a), before, own, after, jnp.where(even2, two_a, two_b)]
    sub = iota((8, 128), 0)
    ends = at_end(iota((8, 128), 1))

    def assemble(tiles, firsts, lasts):
        result = []
        for t in range(5):
            tile = tiles[t]
            if t > 0:
                tile = tile + jnp.where(sub == 0, firsts[t - 1], 0.0)
            if t < 4:
                tile = tile + jnp.where(sub == 7, lasts[t + 1], 0.0)
            result.append(tile)
        return jnp.concatenate(result, axis=0)

    corners = [jnp.where(ends, x[40:48], 0.0) for x in blocks]
    beyond = [jnp.where(ends, pltpu.roll(x[40:48], 126, 1), 0.0) for x in blocks]
    corner = assemble(corners, beyond, beyond)
    main_ref[4] = corner
    lane = iota((40, 128), 1)
    right = jnp.zeros((40, 128), F32)
    left = jnp.zeros((40, 128), F32)
    for z in range(4):
        main = assemble(
            [x[8 * z : 8 * z + 8] for x in blocks],
            [turned(x[32:40], -z) for x in blocks],
            [turned(x[32:40], z) for x in blocks],
        )
        main_ref[z] = main
        lab = jnp.concatenate([x[48 + 8 * z : 56 + 8 * z] for x in (before, own, after)], axis=0)
        lab_ref[z] = lab
        lab = jnp.concatenate([lab, jnp.zeros((16, 128), F32)], axis=0)
        right = jnp.where((lane >> 4) == z, pltpu.roll(main, 16 * z + 16, 1), right)
        right = jnp.where((lane >> 4) == z + 4, pltpu.roll(lab, (16 * z + 80) % 128, 1), right)
        left = jnp.where((lane >> 4) == z, pltpu.roll(main, 16 * z, 1), left)
        left = jnp.where((lane >> 4) == z + 4, pltpu.roll(lab, 16 * z + 64, 1), left)
    right = jnp.where((lane < 64) & ((lane & 15) == 0), corner, right)
    left = jnp.where((lane < 64) & ((lane & 15) == 15), corner, left)
    send_a_ref[...] = jnp.where(even_col, right, left)
    send_b_ref[...] = jnp.where(even_col, left, right)


def shift_rows(x, s):
    return pltpu.roll(x, s % x.shape[0], 0)


def shift_cols(x, s):
    return pltpu.roll(x, s % x.shape[1], 1)


def cross(fields, outside):
    result = []
    for z in range(4):
        x = fields[z]
        around = shift_rows(x, 1) + shift_rows(x, -1) + shift_cols(x, 1) + shift_cols(x, -1)
        before = fields[z - 1] if z > 0 else outside
        after = fields[z + 1] if z < 3 else outside
        result.append((around + (before + after)) * (1.0 / 9.0) + x * (1.0 / 3.0))
    return result


def box(fields, outside, crop):
    result = []
    for z in range(4):
        before = fields[z - 1] if z > 0 else outside
        after = fields[z + 1] if z < 3 else outside
        x = fields[z] + (before + after)
        x = x + shift_rows(x, 1) + shift_rows(x, -1)
        if crop:
            x = x[8:32]
        result.append(x + shift_cols(x, 1) + shift_cols(x, -1))
    return result


def inverse(x):
    return 1.0 / x


def forward(e0, q0, inside, crop, keep):
    def middle(x):
        return x[8:32] if crop else x

    e, q, s = e0, q0, None
    for i in range(ITERS + 1):
        e = [jnp.where(inside, x, 1.0) for x in cross(e, 1.0)]
        q_next = [inverse(x) for x in e]
        mean = box(q_next, 1.0, crop)
        s_next = []
        for z in range(4):
            d_inv = inverse(mean[z] * (1.0 / 27.0))
            qz = middle(q[z])
            ratio = qz * d_inv
            ratio = ratio * ratio
            log_term = jnp.log(1.0 + ratio)
            change = SOFT * log_term
            if i == 0:
                s_next.append(change)
                keep(i, z, qz, d_inv, ratio, None, None, None)
            else:
                rest = 1.0 - s[z]
                power = jnp.exp(log_term * rest)
                s_next.append(s[z] + SOFT * jnp.log(1.0 + power))
                keep(i, z, qz, d_inv, ratio, change, rest, power)
        s, q = s_next, q_next
    return s, q


def skeleton_kernel(
    bias_ref, f_ref, main_ref, lab_ref, got_a_ref, got_b_ref,
    grad_ref, sums_ref,
    qs_ref, ds_ref, rs_ref, gain_ref,
):
    row_ids = lax.axis_index("gx") * 8 - 16 + iota((40, 256), 0)
    lane = iota((40, 256), 1)
    col = jnp.where(lane < 144, lane, lane - 256)
    col_ids = lax.axis_index("gy") * 128 + col
    inside = (row_ids >= 0) & (row_ids < lax.axis_size("gx") * 8)
    inside = inside & (col_ids >= 0) & (col_ids < lax.axis_size("gy") * 128) & (col >= -16)
    inside_f = jnp.where(inside, 1.0, 0.0)
    inner = inside_f[8:32]
    inner_b = inner > 0.5
    bias = bias_ref[0]

    even_col = (lax.axis_index("gy") & 1) == 0
    from_left = jnp.where(even_col, got_b_ref[...], got_a_ref[...])
    from_right = jnp.where(even_col, got_a_ref[...], got_b_ref[...])
    corner = main_ref[4]
    lane40 = iota((40, 128), 1)
    lane24 = lane40[:24]
    e0, q0, slope, probs, labels = [], [], [], [], []
    for z in range(4):
        to_zero, to_last = (128 - 16 * z) % 128, 112 - 16 * z
        left_zero, left_last = pltpu.roll(from_left, to_zero, 1), pltpu.roll(from_left, to_last, 1)
        right_zero, right_last = pltpu.roll(from_right, to_zero, 1), pltpu.roll(from_right, to_last, 1)
        main = main_ref[z]
        main = main + jnp.where(lane40 == 0, left_zero, jnp.where(lane40 == 127, right_last, 0.0))
        tail = jnp.where(lane40 >= 112, left_last, jnp.where(lane40 < 16, right_zero, 0.0))
        own_zero, own_last = pltpu.roll(corner, to_zero, 1), pltpu.roll(corner, to_last, 1)
        tail = tail + jnp.where(lane40 == 0, own_zero, jnp.where(lane40 == 127, own_last, 0.0))
        lab_left = pltpu.roll(from_left[:24], 48 - 16 * z, 1)
        lab_right = pltpu.roll(from_right[:24], 64 - 16 * z, 1)
        lab_tail = jnp.where(lane24 >= 112, lab_left, jnp.where(lane24 < 16, lab_right, 0.0))
        logits = jnp.concatenate([main, tail], axis=1) + bias
        small = jnp.exp(-jnp.abs(logits))
        scale = inverse(1.0 + small)
        prob = jnp.where(logits >= 0.0, scale, small * scale)
        prob = jnp.where(inside, prob, 0.0)
        e = jnp.exp(-SHARP * prob)
        e0.append(e)
        q0.append(inverse(e))
        weight = (small * scale) * scale
        slope.append(((-SHARP) * e * weight)[8:32] * inner)
        probs.append((prob[8:32], weight[8:32]))
        labels.append(jnp.concatenate([lab_ref[z], lab_tail], axis=1))

    low, high = jnp.exp(-SHARP * jnp.ones((24, 256), F32)), jnp.exp(SHARP * jnp.ones((24, 256), F32))
    true_skel, _ = forward(
        [jnp.where(x > 0.5, low, 1.0) for x in labels],
        [jnp.where(x > 0.5, high, 1.0) for x in labels],
        inner_b, False, lambda *factors: None,
    )

    def keep(i, z, qz, d_inv, ratio, change, rest, power):
        qs_ref[i, z] = qz
        ds_ref[i, z] = d_inv
        part = (-2.0 * SOFT) * (ratio * inverse(1.0 + ratio))
        if i > 0:
            share = power * inverse(1.0 + power)
            part = part * (share * rest)
            gain_ref[i, z] = 1.0 - share * change
        rs_ref[i, z] = part

    pred_skel, q_last = forward(e0, q0, inside, True, keep)

    def own(x):
        return x[8:16, :128]

    def total(values):
        acc = values[0] + values[1] + values[2] + values[3]
        return jnp.sum(jnp.sum(acc, axis=1, keepdims=True), axis=0, keepdims=True)

    t0 = total([own(pred_skel[z] * labels[z]) for z in range(4)])
    t1 = total([own(pred_skel[z]) for z in range(4)])
    t2 = total([own(true_skel[z] * probs[z][0]) for z in range(4)])
    t3 = total([own(true_skel[z]) for z in range(4)])

    weights = [labels, [inner] * 4]
    running = [jnp.ones((24, 256), F32)] * 4
    deep = [None, None]
    for i in range(ITERS, -1, -1):
        coefs = []
        for z in range(4):
            coefs.append(rs_ref[i, z] * running[z])
            if i > 0:
                running[z] = running[z] * gain_ref[i, z]
        for f in range(2):
            scaled = [coefs[z] * weights[f][z] for z in range(4)]
            spread = box([scaled[z] * ds_ref[i, z] for z in range(4)], 0.0, False)
            q_of = [q_last[z][8:32] if i == ITERS else qs_ref[i + 1, z] for z in range(4)]
            incoming = []
            for z in range(4):
                value = spread[z] * (q_of[z] * q_of[z]) * (-1.0 / 27.0)
                if deep[f] is not None:
                    value = value + deep[f][z]
                incoming.append(value * inner)
            moved = cross(incoming, 0.0)
            deep[f] = [moved[z] + scaled[z] * qs_ref[i, z] for z in range(4)]
    fields = [
        [deep[0][z] * slope[z] for z in range(4)],
        [deep[1][z] * slope[z] for z in range(4)],
        [true_skel[z] * probs[z][1] * inner for z in range(4)],
    ]
    bias_sums = [total([own(x) for x in field]) for field in fields]

    sub = iota((8, 256), 0)
    stacks = []
    for z in range(4):
        pieces = []
        for f in range(3):
            x = fields[f][z]
            edge = jnp.where(sub == 0, x[16:24], jnp.where(sub == 7, x[0:8], 0.0))
            block = jnp.concatenate([x[8:16], edge], axis=0)
            grad_ref[f, z] = block
            for d in range(3):
                moved = (shift_cols(block, d - 1) if d != 1 else block)[:, :128]
                upper = moved.astype(BF16)
                lower = (moved - upper.astype(F32)).astype(BF16)
                pieces += [upper, lower]
        stacks.append(jnp.concatenate(pieces, axis=0))
    offset = (iota((16, 256), 1) & 7) - edge_row(iota((16, 256), 0)) + 1
    picked = {}
    for a in range(3):
        moments = jnp.zeros((288, 256), F32)
        for z in range(4):
            if 0 <= z + a - 1 < 4:
                feats = f_ref[:, z + a - 1].reshape(256, 128)
                moments = moments + dot(stacks[z], feats, ((1,), (1,)))
        for f in range(3):
            for d in range(3):
                start = (f * 3 + d) * 32
                pair = moments[start : start + 16] + moments[start + 16 : start + 32]
                for b in range(3):
                    chosen = jnp.where(offset == b, pair, 0.0)
                    picked[b, f, a, d] = jnp.sum(chosen, axis=0, keepdims=True)
    order = [(f, a, d) for f in range(3) for a in range(3) for d in range(3)]
    groups = [[picked[(b,) + at] for at in order[:24]] for b in range(3)]
    rest = [picked[(b,) + at] for b in range(3) for at in order[24:]]
    groups.append(rest + [jnp.zeros((15, 256), F32)])
    result = jnp.zeros((24, 128), F32)
    for b in range(4):
        stacked = jnp.concatenate(groups[b], axis=0)
        collect = jnp.where((iota((256, 128), 0) >> 3) + 32 * b == iota((256, 128), 1), 1.0, 0.0)
        result = result + dot(stacked, collect, ((1,), (0,)), precision=lax.Precision.HIGHEST)
    row24, lane_of = iota((24, 128), 0), iota((24, 128), 1)
    for k, value in enumerate([t0, t1, t2, t3] + bias_sums):
        result = jnp.where(((row24 == 11) | (row24 == 23)) & (lane_of == 96 + k), value, result)
    for n in range(sums_ref.shape[0]):
        sums_ref[n] = result


def half_kernel(in_ref, out_ref):
    acc = in_ref[0]
    for n in range(1, in_ref.shape[0]):
        acc = acc + in_ref[n]
    half = jnp.where((lax.axis_index("gy") & 1) == 0, acc[:12], acc[12:])
    for n in range(out_ref.shape[0]):
        out_ref[n] = half[4 * (n % 3) : 4 * (n % 3) + 4]


def add_kernel(in_ref, out_ref):
    for part in range(3):
        acc = in_ref[part]
        for n in range(part + 3, in_ref.shape[0], 3):
            acc = acc + in_ref[n]
        out_ref[part] = acc


def loss_and_slopes(row):
    sums = [row[:, 96 + k : 97 + k] for k in range(7)]
    precision = (sums[0] + 1.0) / (sums[1] + 1.0)
    sensitivity = (sums[2] + 1.0) / (sums[3] + 1.0)
    both = precision + sensitivity
    loss = 1.0 - 2.0 * precision * sensitivity / both
    by_precision = -2.0 * (sensitivity / both) * (sensitivity / both)
    by_sensitivity = -2.0 * (precision / both) * (precision / both)
    slopes = [
        by_precision / (sums[1] + 1.0),
        -by_precision * precision / (sums[1] + 1.0),
        by_sensitivity / (sums[3] + 1.0),
    ]
    return loss, slopes, sums[4:]


def weight_kernel(own_ref, got_ref, loss_ref, weight_ref, bias_ref):
    even = (lax.axis_index("gy") & 1) == 0
    own, got = own_ref[...], got_ref[...]
    first, second = jnp.where(even, own, got), jnp.where(even, got, own)
    acc = jnp.concatenate([x[part] for x in (first, second) for part in range(3)], axis=0)
    loss, slopes, bias_sums = loss_and_slopes(acc[11:12])
    loss_ref[...] = loss
    bias_ref[...] = sum(slopes[f] * bias_sums[f] for f in range(3))
    group = iota((3, 128), 1) >> 5
    last = acc[18:21]
    for b in range(3):
        last = jnp.where(group == b, pltpu.roll(acc[3 * b : 3 * b + 3], (32 * b + 32) % 128, 1), last)
    third = jnp.concatenate([acc[18:24], last], axis=0)
    weight = slopes[0] * acc[0:9] + slopes[1] * acc[9:18] + slopes[2] * third
    for b in range(3):
        part = weight if b == 0 else pltpu.roll(weight, 128 - 32 * b, 1)
        for a in range(3):
            weight_ref[9 * a + 3 * b : 9 * a + 3 * b + 3] = part[3 * a : 3 * a + 3, :32]


def feature_kernel(sums_ref, grad_ref, a_ref, out_ref, *, voxels):
    _, slopes, _ = loss_and_slopes(sums_ref[2, 3:4])
    matrix = a_ref[...]
    parts = []
    for z in range(4):
        block = slopes[0] * grad_ref[0, z] + slopes[1] * grad_ref[1, z] + slopes[2] * grad_ref[2, z]
        block = block * voxels
        byd = []
        for d in range(3):
            moved = (shift_cols(block, d - 1) if d != 1 else block)[:, :128]
            upper = moved.astype(BF16)
            byd.append((upper, (moved - upper.astype(F32)).astype(BF16)))
        parts.append(byd)
    none = jnp.zeros((16, 128), BF16)
    for z in range(4):
        acc_z = None
        for level in range(2):
            stack = []
            for a in range(3):
                for d in range(3):
                    at = z - a + 1
                    stack.append(parts[at][d][level] if 0 <= at < 4 else none)
            term = dot(matrix, jnp.concatenate(stack, axis=0), ((0,), (0,)))
            acc_z = term if acc_z is None else acc_z + term
        out_ref[:, z] = acc_z.reshape(32, 8, 128).astype(BF16)


def call(kernel, out_shapes, *args, scratch=(), spaces={}):
    spec = pl.BlockSpec(memory_space=pltpu.VMEM)
    in_specs = [pl.BlockSpec(memory_space=spaces.get(n, pltpu.VMEM)) for n in range(len(args))]
    return pl.pallas_call(
        kernel,
        out_shape=[jax.ShapeDtypeStruct(shape, dtype) for shape, dtype in out_shapes],
        in_specs=in_specs,
        out_specs=[spec] * len(out_shapes),
        scratch_shapes=list(scratch),
        compiler_params=pltpu.CompilerParams(vmem_limit_bytes=VMEM_LIMIT),
    )(*args)


def swapped(x, axis, step, phase):
    count = lax.axis_size(axis)
    pairs = []
    for n in range(count - step):
        if (n // step) % 2 == phase:
            pairs += [(n, n + step), (n + step, n)]
    return lax.ppermute(x, axis, pairs)


def local(features, vessel_label, conv_weight, conv_bias):
    gx, gy = lax.axis_size("gx"), lax.axis_size("gy")
    voxels = float(4 * 8 * gx * 128 * gy)
    matrix, near, far, features = call(
        partial_logits_kernel,
        [((144, 256), BF16), ((80, 128), F32), ((48, 128), F32), (features.shape, BF16)],
        *[pltpu.with_memory_space_constraint(x, pltpu.HBM) for x in (conv_weight, features, vessel_label)],
        scratch=[
            pltpu.VMEM((27, 32), BF16),
            pltpu.VMEM((4, 8, 128), jnp.int32),
            pltpu.SemaphoreType.DMA((3,)),
        ],
        spaces={0: pltpu.HBM, 1: pltpu.HBM, 2: pltpu.HBM},
    )
    two = [swapped(far, "gx", 2, phase) for phase in range(2)]
    one = [swapped(near, "gx", 1, phase) for phase in range(2)]
    main, labels, send_a, send_b = call(
        rows_kernel,
        [((5, 40, 128), F32), ((4, 24, 128), F32), ((40, 128), F32), ((40, 128), F32)],
        near, *one, *two,
    )
    got = [swapped(send_a, "gy", 1, 0), swapped(send_b, "gy", 1, 1)]
    field = pltpu.VMEM((ITERS + 1, 4, 24, 256), F32)
    grads, sums = call(
        skeleton_kernel,
        [((3, 4, 16, 256), F32), ((gy, 24, 128), F32)],
        conv_bias, features, main, labels, *got,
        scratch=[field] * 4, spaces={0: pltpu.SMEM},
    )
    sums = lax.all_to_all(sums, "gy", 0, 0, tiled=True)
    sums = call(half_kernel, [((3 * gx, 4, 128), F32)], sums)[0]
    sums = lax.all_to_all(sums, "gx", 0, 0, tiled=True)
    sums = call(add_kernel, [((3, 4, 128), F32)], sums)[0]
    other = swapped(sums, "gy", 1, 0)

    def feature_part(*refs):
        feature_kernel(*refs, voxels=voxels)

    feature_grad = call(feature_part, [((32, 4, 8, 128), BF16)], sums, grads, matrix)[0]
    loss, weight_grad, bias_grad = call(
        weight_kernel, [((1, 1), F32), ((27, 32), F32), ((1, 1), F32)], sums, other
    )
    return (loss.reshape(()), weight_grad, bias_grad.reshape((1,)), feature_grad)


def solution(mesh):
    in_specs = (P(None, None, "gx", "gy"), P(None, "gx", "gy"), P(), P())
    out_specs = (P(), P(), P(), P(None, None, "gx", "gy"))
    return jax.shard_map(local, mesh=mesh, in_specs=in_specs, out_specs=out_specs, check_vma=False)
```

```python
import jax
import jax.numpy as jnp
from jax import lax
from jax.experimental import pallas as pl
from jax.experimental.pallas import tpu as pltpu
from jax.sharding import PartitionSpec as P

ITERS = 5
F32 = jnp.float32
BF16 = jnp.bfloat16
SHARP = 10.0
SOFT = 0.05
EDGE = 16
VMEM_LIMIT = 24 * 1024 * 1024


def iota(shape, dim):
    return lax.broadcasted_iota(jnp.int32, shape, dim)


def dot(a, b, dims, precision=None):
    return lax.dot_general(a, b, (dims, ((), ())), precision=precision, preferred_element_type=F32)


def edge_row(q):
    return jnp.where(q < 8, q, jnp.where(q == 8, 8, jnp.where(q == 15, -1, -100)))


def weight_matrix(w):
    spread = jnp.where((iota((32, 256), 1) >> 3) == iota((32, 256), 0), 1.0, 0.0).astype(BF16)
    by_lane = dot(w, spread, ((1,), (0,))).astype(BF16)
    row = iota((144, 27), 0)
    ad = row >> 4
    base = ad + 6 * (jnp.where(ad >= 3, 1, 0) + jnp.where(ad >= 6, 1, 0))
    col = iota((144, 27), 1)
    offset = (iota((144, 256), 1) & 7) - edge_row(iota((144, 256), 0) & 15) + 1
    matrix = jnp.zeros((144, 256), F32)
    for b in range(3):
        pick = jnp.where(col == base + 3 * b, 1.0, 0.0).astype(BF16)
        matrix = matrix + jnp.where(offset == b, dot(pick, by_lane, ((1,), (0,))), 0.0)
    return matrix.astype(BF16)


def turned(x, s):
    return x if s == 0 else pltpu.roll(x, s % x.shape[0], 0)


def at_end(lane):
    return ((lane & 15) == 0) | ((lane & 15) == 15)


def partial_logits_kernel(
    w_hbm, f_hbm, lab_hbm, a_ref, near_ref, far_ref, f_ref, w_ref, lab_ref, sems
):
    pairs = [(w_hbm, w_ref), (f_hbm, f_ref), (lab_hbm, lab_ref)]
    copies = [pltpu.make_async_copy(x, y, sems.at[n]) for n, (x, y) in enumerate(pairs)]
    for copy in copies:
        copy.start()
    copies[0].wait()
    matrix = weight_matrix(w_ref[...])
    a_ref[...] = matrix
    copies[1].wait()
    lane = iota((16, 128), 1)
    sub = iota((8, 128), 0)
    terms = [
        dot(matrix, f_ref[:, z].reshape(256, 128), ((1,), (0,))).reshape(3, 3, 16, 128)
        for z in range(4)
    ]
    corner = jnp.zeros((16, 128), F32)
    edges = jnp.zeros((8, 128), F32)
    for z in range(4):
        byd = []
        for d in range(3):
            byd.append(sum(terms[z + a - 1][a, d] for a in range(3) if 0 <= z + a - 1 < 4))
        main = byd[1]
        main = main + jnp.where(lane >= 1, pltpu.roll(byd[0], 1, 1), 0.0)
        main = main + jnp.where(lane <= 126, pltpu.roll(byd[2], 127, 1), 0.0)
        near_ref[8 * z : 8 * z + 8] = main[:8]
        far_ref[8 * z : 8 * z + 8] = main[:8]
        edges = jnp.where(sub == z, turned(main[8:], z), edges)
        edges = jnp.where(sub == 7 - z, turned(main[8:], -z), edges)
        low, high = 16 * z, 16 * z + 15
        corner = jnp.where(lane == low, pltpu.roll(byd[0], low + 1, 1), corner)
        corner = jnp.where(lane == high, pltpu.roll(byd[2], high, 1), corner)
    corners = jnp.where(at_end(lane[:8]), corner[:8], pltpu.roll(corner[8:], 2, 1))
    near_ref[32:40] = edges
    far_ref[32:40] = edges
    near_ref[40:48] = corners
    far_ref[40:48] = corners
    copies[2].wait()
    near_ref[48:80] = lab_ref[...].reshape(32, 128).astype(F32)


def rows_kernel(
    own_ref, one_a_ref, one_b_ref, two_a_ref, two_b_ref, main_ref, lab_ref, send_a_ref, send_b_ref
):
    row_block, col_block = lax.axis_index("gx"), lax.axis_index("gy")
    even1 = (row_block & 1) == 0
    even2 = (row_block & 2) == 0
    even_col = (col_block & 1) == 0
    own = own_ref[...]
    one_a, one_b, two_a, two_b = one_a_ref[...], one_b_ref[...], two_a_ref[...], two_b_ref[...]
    before, after = jnp.where(even1, one_b, one_a), jnp.where(even1, one_a, one_b)
    blocks = [jnp.where(even2, two_b, two_a), before, own, after, jnp.where(even2, two_a, two_b)]
    sub = iota((8, 128), 0)
    ends = at_end(iota((8, 128), 1))

    def assemble(tiles, firsts, lasts):
        result = []
        for t in range(5):
            tile = tiles[t]
            if t > 0:
                tile = tile + jnp.where(sub == 0, firsts[t - 1], 0.0)
            if t < 4:
                tile = tile + jnp.where(sub == 7, lasts[t + 1], 0.0)
            result.append(tile)
        return jnp.concatenate(result, axis=0)

    corners = [jnp.where(ends, x[40:48], 0.0) for x in blocks]
    beyond = [jnp.where(ends, pltpu.roll(x[40:48], 126, 1), 0.0) for x in blocks]
    corner = assemble(corners, beyond, beyond)
    main_ref[4] = corner
    lane = iota((40, 128), 1)
    right = jnp.zeros((40, 128), F32)
    left = jnp.zeros((40, 128), F32)
    for z in range(4):
        main = assemble(
            [x[8 * z : 8 * z + 8] for x in blocks],
            [turned(x[32:40], -z) for x in blocks],
            [turned(x[32:40], z) for x in blocks],
        )
        main_ref[z] = main
        lab = jnp.concatenate([x[48 + 8 * z : 56 + 8 * z] for x in (before, own, after)], axis=0)
        lab_ref[z] = lab
        lab = jnp.concatenate([lab, jnp.zeros((16, 128), F32)], axis=0)
        right = jnp.where((lane >> 4) == z, pltpu.roll(main, 16 * z + 16, 1), right)
        right = jnp.where((lane >> 4) == z + 4, pltpu.roll(lab, (16 * z + 80) % 128, 1), right)
        left = jnp.where((lane >> 4) == z, pltpu.roll(main, 16 * z, 1), left)
        left = jnp.where((lane >> 4) == z + 4, pltpu.roll(lab, 16 * z + 64, 1), left)
    right = jnp.where((lane < 64) & ((lane & 15) == 0), corner, right)
    left = jnp.where((lane < 64) & ((lane & 15) == 15), corner, left)
    send_a_ref[...] = jnp.where(even_col, right, left)
    send_b_ref[...] = jnp.where(even_col, left, right)


def shift_rows(x, s):
    return pltpu.roll(x, s % x.shape[0], 0)


def shift_cols(x, s):
    return pltpu.roll(x, s % x.shape[1], 1)


def cross(fields, outside):
    result = []
    for z in range(4):
        x = fields[z]
        around = shift_rows(x, 1) + shift_rows(x, -1) + shift_cols(x, 1) + shift_cols(x, -1)
        before = fields[z - 1] if z > 0 else outside
        after = fields[z + 1] if z < 3 else outside
        result.append((around + (before + after)) * (1.0 / 9.0) + x * (1.0 / 3.0))
    return result


def box(fields, outside, crop):
    result = []
    for z in range(4):
        before = fields[z - 1] if z > 0 else outside
        after = fields[z + 1] if z < 3 else outside
        x = fields[z] + (before + after)
        x = x + shift_rows(x, 1) + shift_rows(x, -1)
        if crop:
            x = x[8:32]
        result.append(x + shift_cols(x, 1) + shift_cols(x, -1))
    return result


def inverse(x):
    return 1.0 / x


def forward(e0, q0, inside, crop, keep):
    def middle(x):
        return x[8:32] if crop else x

    e, q, s = e0, q0, None
    for i in range(ITERS + 1):
        e = [jnp.where(inside, x, 1.0) for x in cross(e, 1.0)]
        q_next = [inverse(x) for x in e]
        mean = box(q_next, 1.0, crop)
        s_next = []
        for z in range(4):
            d_inv = inverse(mean[z] * (1.0 / 27.0))
            qz = middle(q[z])
            ratio = qz * d_inv
            ratio = ratio * ratio
            log_term = jnp.log(1.0 + ratio)
            change = SOFT * log_term
            if i == 0:
                s_next.append(change)
                keep(i, z, qz, d_inv, ratio, None, None, None)
            else:
                rest = 1.0 - s[z]
                power = jnp.exp(log_term * rest)
                s_next.append(s[z] + SOFT * jnp.log(1.0 + power))
                keep(i, z, qz, d_inv, ratio, change, rest, power)
        s, q = s_next, q_next
    return s, q


def skeleton_kernel(
    bias_ref, f_ref, main_ref, lab_ref, got_b_ref, got_a_ref,
    grad_ref, sums_ref,
    qs_ref, ds_ref, rs_ref, gain_ref,
):
    row_ids = lax.axis_index("gx") * 8 - 16 + iota((40, 256), 0)
    lane = iota((40, 256), 1)
    col = jnp.where(lane < 144, lane, lane - 256)
    col_ids = lax.axis_index("gy") * 128 + col
    inside = (row_ids >= 0) & (row_ids < lax.axis_size("gx") * 8)
    inside = inside & (col_ids >= 0) & (col_ids < lax.axis_size("gy") * 128) & (col >= -16)
    inside_f = jnp.where(inside, 1.0, 0.0)
    inner = inside_f[8:32]
    inner_b = inner > 0.5
    bias = bias_ref[0]

    even_col = (lax.axis_index("gy") & 1) == 0
    from_left = jnp.where(even_col, got_b_ref[...], got_a_ref[...])
    from_right = jnp.where(even_col, got_a_ref[...], got_b_ref[...])
    corner = main_ref[4]
    lane40 = iota((40, 128), 1)
    lane24 = lane40[:24]
    e0, q0, slope, probs, labels = [], [], [], [], []
    for z in range(4):
        to_zero, to_last = (128 - 16 * z) % 128, 112 - 16 * z
        left_zero, left_last = pltpu.roll(from_left, to_zero, 1), pltpu.roll(from_left, to_last, 1)
        right_zero, right_last = pltpu.roll(from_right, to_zero, 1), pltpu.roll(from_right, to_last, 1)
        main = main_ref[z]
        main = main + jnp.where(lane40 == 0, left_zero, jnp.where(lane40 == 127, right_last, 0.0))
        tail = jnp.where(lane40 >= 112, left_last, jnp.where(lane40 < 16, right_zero, 0.0))
        own_zero, own_last = pltpu.roll(corner, to_zero, 1), pltpu.roll(corner, to_last, 1)
        tail = tail + jnp.where(lane40 == 0, own_zero, jnp.where(lane40 == 127, own_last, 0.0))
        lab_left = pltpu.roll(from_left[:24], 48 - 16 * z, 1)
        lab_right = pltpu.roll(from_right[:24], 64 - 16 * z, 1)
        lab_tail = jnp.where(lane24 >= 112, lab_left, jnp.where(lane24 < 16, lab_right, 0.0))
        logits = jnp.concatenate([main, tail], axis=1) + bias
        small = jnp.exp(-jnp.abs(logits))
        scale = inverse(1.0 + small)
        prob = jnp.where(logits >= 0.0, scale, small * scale)
        prob = jnp.where(inside, prob, 0.0)
        e = jnp.exp(-SHARP * prob)
        e0.append(e)
        q0.append(inverse(e))
        weight = (small * scale) * scale
        slope.append(((-SHARP) * e * weight)[8:32] * inner)
        probs.append((prob[8:32], weight[8:32]))
        labels.append(jnp.concatenate([lab_ref[z], lab_tail], axis=1))

    low, high = jnp.exp(-SHARP * jnp.ones((24, 256), F32)), jnp.exp(SHARP * jnp.ones((24, 256), F32))
    true_skel, _ = forward(
        [jnp.where(x > 0.5, low, 1.0) for x in labels],
        [jnp.where(x > 0.5, high, 1.0) for x in labels],
        inner_b, False, lambda *factors: None,
    )

    def keep(i, z, qz, d_inv, ratio, change, rest, power):
        qs_ref[i, z] = qz
        ds_ref[i, z] = d_inv
        part = (-2.0 * SOFT) * (ratio * inverse(1.0 + ratio))
        if i > 0:
            share = power * inverse(1.0 + power)
            part = part * (share * rest)
            gain_ref[i, z] = 1.0 - share * change
        rs_ref[i, z] = part

    pred_skel, q_last = forward(e0, q0, inside, True, keep)

    def own(x):
        return x[8:16, :128]

    def total(values):
        acc = values[0] + values[1] + values[2] + values[3]
        return jnp.sum(jnp.sum(acc, axis=1, keepdims=True), axis=0, keepdims=True)

    t0 = total([own(pred_skel[z] * labels[z]) for z in range(4)])
    t1 = total([own(pred_skel[z]) for z in range(4)])
    t2 = total([own(true_skel[z] * probs[z][0]) for z in range(4)])
    t3 = total([own(true_skel[z]) for z in range(4)])

    weights = [labels, [inner] * 4]
    running = [jnp.ones((24, 256), F32)] * 4
    deep = [None, None]
    for i in range(ITERS, -1, -1):
        coefs = []
        for z in range(4):
            coefs.append(rs_ref[i, z] * running[z])
            if i > 0:
                running[z] = running[z] * gain_ref[i, z]
        for f in range(2):
            scaled = [coefs[z] * weights[f][z] for z in range(4)]
            spread = box([scaled[z] * ds_ref[i, z] for z in range(4)], 0.0, False)
            q_of = [q_last[z][8:32] if i == ITERS else qs_ref[i + 1, z] for z in range(4)]
            incoming = []
            for z in range(4):
                value = spread[z] * (q_of[z] * q_of[z]) * (-1.0 / 27.0)
                if deep[f] is not None:
                    value = value + deep[f][z]
                incoming.append(value * inner)
            moved = cross(incoming, 0.0)
            deep[f] = [moved[z] + scaled[z] * qs_ref[i, z] for z in range(4)]
    fields = [
        [deep[0][z] * slope[z] for z in range(4)],
        [deep[1][z] * slope[z] for z in range(4)],
        [true_skel[z] * probs[z][1] * inner for z in range(4)],
    ]
    bias_sums = [total([own(x) for x in field]) for field in fields]

    sub = iota((8, 256), 0)
    stacks = []
    for z in range(4):
        pieces = []
        for f in range(3):
            x = fields[f][z]
            edge = jnp.where(sub == 0, x[16:24], jnp.where(sub == 7, x[0:8], 0.0))
            block = jnp.concatenate([x[8:16], edge], axis=0)
            grad_ref[f, z] = block
            for d in range(3):
                moved = (shift_cols(block, d - 1) if d != 1 else block)[:, :128]
                upper = moved.astype(BF16)
                lower = (moved - upper.astype(F32)).astype(BF16)
                pieces += [upper, lower]
        stacks.append(jnp.concatenate(pieces, axis=0))
    offset = (iota((16, 256), 1) & 7) - edge_row(iota((16, 256), 0)) + 1
    picked = {}
    for a in range(3):
        moments = jnp.zeros((288, 256), F32)
        for z in range(4):
            if 0 <= z + a - 1 < 4:
                feats = f_ref[:, z + a - 1].reshape(256, 128)
                moments = moments + dot(stacks[z], feats, ((1,), (1,)))
        for f in range(3):
            for d in range(3):
                start = (f * 3 + d) * 32
                pair = moments[start : start + 16] + moments[start + 16 : start + 32]
                for b in range(3):
                    chosen = jnp.where(offset == b, pair, 0.0)
                    picked[b, f, a, d] = jnp.sum(chosen, axis=0, keepdims=True)
    order = [(f, a, d) for f in range(3) for a in range(3) for d in range(3)]
    groups = [[picked[(b,) + at] for at in order[:24]] for b in range(3)]
    rest = [picked[(b,) + at] for b in range(3) for at in order[24:]]
    groups.append(rest + [jnp.zeros((15, 256), F32)])
    result = jnp.zeros((24, 128), F32)
    for b in range(4):
        stacked = jnp.concatenate(groups[b], axis=0)
        collect = jnp.where((iota((256, 128), 0) >> 3) + 32 * b == iota((256, 128), 1), 1.0, 0.0)
        result = result + dot(stacked, collect, ((1,), (0,)), precision=lax.Precision.HIGHEST)
    row24, lane_of = iota((24, 128), 0), iota((24, 128), 1)
    for k, value in enumerate([t0, t1, t2, t3] + bias_sums):
        result = jnp.where(((row24 == 11) | (row24 == 23)) & (lane_of == 96 + k), value, result)
    for n in range(sums_ref.shape[0]):
        sums_ref[n] = result


def half_kernel(in_ref, out_ref):
    acc = in_ref[0]
    for n in range(1, in_ref.shape[0]):
        acc = acc + in_ref[n]
    half = jnp.where((lax.axis_index("gy") & 1) == 0, acc[:12], acc[12:])
    for n in range(out_ref.shape[0]):
        out_ref[n] = half[4 * (n % 3) : 4 * (n % 3) + 4]


def add_kernel(in_ref, out_ref):
    for part in range(3):
        acc = in_ref[part]
        for n in range(part + 3, in_ref.shape[0], 3):
            acc = acc + in_ref[n]
        out_ref[part] = acc


def loss_and_slopes(row):
    sums = [row[:, 96 + k : 97 + k] for k in range(7)]
    precision = (sums[0] + 1.0) / (sums[1] + 1.0)
    sensitivity = (sums[2] + 1.0) / (sums[3] + 1.0)
    both = precision + sensitivity
    loss = 1.0 - 2.0 * precision * sensitivity / both
    by_precision = -2.0 * (sensitivity / both) * (sensitivity / both)
    by_sensitivity = -2.0 * (precision / both) * (precision / both)
    slopes = [
        by_precision / (sums[1] + 1.0),
        -by_precision * precision / (sums[1] + 1.0),
        by_sensitivity / (sums[3] + 1.0),
    ]
    return loss, slopes, sums[4:]


def weight_kernel(
    own_ref, got_ref, feature_ref, loss_ref, weight_ref, bias_ref, feature_out_ref, sem
):
    copy = pltpu.make_async_copy(feature_ref, feature_out_ref, sem)
    copy.start()
    even = (lax.axis_index("gy") & 1) == 0
    own, got = own_ref[...], got_ref[...]
    first, second = jnp.where(even, own, got), jnp.where(even, got, own)
    acc = jnp.concatenate([x[part] for x in (first, second) for part in range(3)], axis=0)
    loss, slopes, bias_sums = loss_and_slopes(acc[11:12])
    loss_ref[...] = loss
    bias_ref[...] = sum(slopes[f] * bias_sums[f] for f in range(3))
    group = iota((3, 128), 1) >> 5
    last = acc[18:21]
    for b in range(3):
        last = jnp.where(group == b, pltpu.roll(acc[3 * b : 3 * b + 3], (32 * b + 32) % 128, 1), last)
    third = jnp.concatenate([acc[18:24], last], axis=0)
    weight = slopes[0] * acc[0:9] + slopes[1] * acc[9:18] + slopes[2] * third
    for b in range(3):
        part = weight if b == 0 else pltpu.roll(weight, 128 - 32 * b, 1)
        for a in range(3):
            weight_ref[9 * a + 3 * b : 9 * a + 3 * b + 3] = part[3 * a : 3 * a + 3, :32]
    copy.wait()


def feature_kernel(sums_ref, grad_ref, a_ref, out_ref, *, voxels):
    _, slopes, _ = loss_and_slopes(sums_ref[2, 3:4])
    matrix = a_ref[...]
    parts = []
    for z in range(4):
        block = slopes[0] * grad_ref[0, z] + slopes[1] * grad_ref[1, z] + slopes[2] * grad_ref[2, z]
        block = block * voxels
        byd = []
        for d in range(3):
            moved = (shift_cols(block, d - 1) if d != 1 else block)[:, :128]
            upper = moved.astype(BF16)
            byd.append((upper, (moved - upper.astype(F32)).astype(BF16)))
        parts.append(byd)
    none = jnp.zeros((16, 128), BF16)
    for z in range(4):
        acc_z = None
        for level in range(2):
            stack = []
            for a in range(3):
                for d in range(3):
                    at = z - a + 1
                    stack.append(parts[at][d][level] if 0 <= at < 4 else none)
            term = dot(matrix, jnp.concatenate(stack, axis=0), ((0,), (0,)))
            acc_z = term if acc_z is None else acc_z + term
        out_ref[:, z] = acc_z.reshape(32, 8, 128).astype(BF16)


def call(kernel, out_shapes, *args, scratch=(), spaces={}, out_spaces={}):
    in_specs = [pl.BlockSpec(memory_space=spaces.get(n, pltpu.VMEM)) for n in range(len(args))]
    return pl.pallas_call(
        kernel,
        out_shape=[jax.ShapeDtypeStruct(shape, dtype) for shape, dtype in out_shapes],
        in_specs=in_specs,
        out_specs=[
            pl.BlockSpec(memory_space=out_spaces.get(n, pltpu.VMEM)) for n in range(len(out_shapes))
        ],
        scratch_shapes=list(scratch),
        compiler_params=pltpu.CompilerParams(vmem_limit_bytes=VMEM_LIMIT),
    )(*args)


def swapped(x, axis, step, phase):
    count = lax.axis_size(axis)
    pairs = []
    for n in range(count - step):
        if (n // step) % 2 == phase:
            pairs += [(n, n + step), (n + step, n)]
    return lax.ppermute(x, axis, pairs)


def local(features, vessel_label, conv_weight, conv_bias):
    gx, gy = lax.axis_size("gx"), lax.axis_size("gy")
    voxels = float(4 * 8 * gx * 128 * gy)
    matrix, near, far, features = call(
        partial_logits_kernel,
        [((144, 256), BF16), ((80, 128), F32), ((48, 128), F32), (features.shape, BF16)],
        *[pltpu.with_memory_space_constraint(x, pltpu.HBM) for x in (conv_weight, features, vessel_label)],
        scratch=[
            pltpu.VMEM((27, 32), BF16),
            pltpu.VMEM((4, 8, 128), jnp.int32),
            pltpu.SemaphoreType.DMA((3,)),
        ],
        spaces={0: pltpu.HBM, 1: pltpu.HBM, 2: pltpu.HBM},
    )
    two = [swapped(far, "gx", 2, phase) for phase in range(2)]
    one = [swapped(near, "gx", 1, phase) for phase in range(2)]
    main, labels, send_a, send_b = call(
        rows_kernel,
        [((5, 40, 128), F32), ((4, 24, 128), F32), ((40, 128), F32), ((40, 128), F32)],
        near, *one, *two,
    )
    got_b = swapped(send_b, "gy", 1, 1)
    got_a = swapped(send_a, "gy", 1, 0)
    field = pltpu.VMEM((ITERS + 1, 4, 24, 256), F32)
    grads, sums = call(
        skeleton_kernel,
        [((3, 4, 16, 256), F32), ((gy, 24, 128), F32)],
        conv_bias, features, main, labels, got_b, got_a,
        scratch=[field] * 4, spaces={0: pltpu.SMEM},
    )
    sums = lax.all_to_all(sums, "gy", 0, 0, tiled=True)
    sums = call(half_kernel, [((3 * gx, 4, 128), F32)], sums)[0]
    sums = lax.all_to_all(sums, "gx", 0, 0, tiled=True)
    sums = call(add_kernel, [((3, 4, 128), F32)], sums)[0]
    other = swapped(sums, "gy", 1, 0)

    def feature_part(*refs):
        feature_kernel(*refs, voxels=voxels)

    feature_grad = call(feature_part, [((32, 4, 8, 128), BF16)], sums, grads, matrix)[0]
    loss, weight_grad, bias_grad, feature_grad = call(
        weight_kernel,
        [((1, 1), F32), ((27, 32), F32), ((1, 1), F32), ((32, 4, 8, 128), BF16)],
        sums, other, feature_grad,
        scratch=[pltpu.SemaphoreType.DMA(())],
        out_spaces={3: pltpu.HBM},
    )
    return (loss.reshape(()), weight_grad, bias_grad.reshape((1,)), feature_grad)


def solution(mesh):
    in_specs = (P(None, None, "gx", "gy"), P(None, "gx", "gy"), P(), P())
    out_specs = (P(), P(), P(), P(None, None, "gx", "gy"))
    return jax.shard_map(local, mesh=mesh, in_specs=in_specs, out_specs=out_specs, check_vma=False)
```

```python
import jax
import jax.numpy as jnp
from jax import lax
from jax.experimental import pallas as pl
from jax.experimental.pallas import tpu as pltpu
from jax.sharding import PartitionSpec as P

ITERS = 5
F32 = jnp.float32
BF16 = jnp.bfloat16
SHARP = 10.0
SOFT = 0.05
EDGE = 16
VMEM_LIMIT = 24 * 1024 * 1024


def iota(shape, dim):
    return lax.broadcasted_iota(jnp.int32, shape, dim)


def dot(a, b, dims, precision=None):
    return lax.dot_general(a, b, (dims, ((), ())), precision=precision, preferred_element_type=F32)


def edge_row(q):
    return jnp.where(q < 8, q, jnp.where(q == 8, 8, jnp.where(q == 15, -1, -100)))


def weight_matrix(w):
    spread = jnp.where((iota((32, 256), 1) >> 3) == iota((32, 256), 0), 1.0, 0.0).astype(BF16)
    by_lane = dot(w, spread, ((1,), (0,))).astype(BF16)
    row = iota((144, 27), 0)
    ad = row >> 4
    base = ad + 6 * (jnp.where(ad >= 3, 1, 0) + jnp.where(ad >= 6, 1, 0))
    col = iota((144, 27), 1)
    offset = (iota((144, 256), 1) & 7) - edge_row(iota((144, 256), 0) & 15) + 1
    matrix = jnp.zeros((144, 256), F32)
    for b in range(3):
        pick = jnp.where(col == base + 3 * b, 1.0, 0.0).astype(BF16)
        matrix = matrix + jnp.where(offset == b, dot(pick, by_lane, ((1,), (0,))), 0.0)
    return matrix.astype(BF16)


def turned(x, s):
    return x if s == 0 else pltpu.roll(x, s % x.shape[0], 0)


def at_end(lane):
    return ((lane & 15) == 0) | ((lane & 15) == 15)


def partial_logits_kernel(
    w_hbm, f_hbm, lab_hbm, a_ref, near_ref, far_ref, f_ref, w_ref, lab_ref, sems
):
    pairs = [(w_hbm, w_ref), (f_hbm, f_ref), (lab_hbm, lab_ref)]
    copies = [pltpu.make_async_copy(x, y, sems.at[n]) for n, (x, y) in enumerate(pairs)]
    for copy in copies:
        copy.start()
    copies[0].wait()
    matrix = weight_matrix(w_ref[...])
    a_ref[...] = matrix
    copies[1].wait()
    lane = iota((16, 128), 1)
    sub = iota((8, 128), 0)
    terms = [
        dot(matrix, f_ref[:, z].reshape(256, 128), ((1,), (0,))).reshape(3, 3, 16, 128)
        for z in range(4)
    ]
    corner = jnp.zeros((16, 128), F32)
    edges = jnp.zeros((8, 128), F32)
    for z in range(4):
        byd = []
        for d in range(3):
            byd.append(sum(terms[z + a - 1][a, d] for a in range(3) if 0 <= z + a - 1 < 4))
        main = byd[1]
        main = main + jnp.where(lane >= 1, pltpu.roll(byd[0], 1, 1), 0.0)
        main = main + jnp.where(lane <= 126, pltpu.roll(byd[2], 127, 1), 0.0)
        near_ref[8 * z : 8 * z + 8] = main[:8]
        far_ref[8 * z : 8 * z + 8] = main[:8]
        edges = jnp.where(sub == z, turned(main[8:], z), edges)
        edges = jnp.where(sub == 7 - z, turned(main[8:], -z), edges)
        low, high = 16 * z, 16 * z + 15
        corner = jnp.where(lane == low, pltpu.roll(byd[0], low + 1, 1), corner)
        corner = jnp.where(lane == high, pltpu.roll(byd[2], high, 1), corner)
    corners = jnp.where(at_end(lane[:8]), corner[:8], pltpu.roll(corner[8:], 2, 1))
    near_ref[32:40] = edges
    far_ref[32:40] = edges
    near_ref[40:48] = corners
    far_ref[40:48] = corners
    copies[2].wait()
    near_ref[48:80] = lab_ref[...].reshape(32, 128).astype(F32)


def rows_kernel(
    own_ref, two_b_ref, two_a_ref, one_b_ref, one_a_ref, main_ref, lab_ref, send_a_ref, send_b_ref
):
    row_block, col_block = lax.axis_index("gx"), lax.axis_index("gy")
    even1 = (row_block & 1) == 0
    even2 = (row_block & 2) == 0
    even_col = (col_block & 1) == 0
    own = own_ref[...]
    one_a, one_b, two_a, two_b = one_a_ref[...], one_b_ref[...], two_a_ref[...], two_b_ref[...]
    before, after = jnp.where(even1, one_b, one_a), jnp.where(even1, one_a, one_b)
    blocks = [jnp.where(even2, two_b, two_a), before, own, after, jnp.where(even2, two_a, two_b)]
    sub = iota((8, 128), 0)
    ends = at_end(iota((8, 128), 1))

    def assemble(tiles, firsts, lasts):
        result = []
        for t in range(5):
            tile = tiles[t]
            if t > 0:
                tile = tile + jnp.where(sub == 0, firsts[t - 1], 0.0)
            if t < 4:
                tile = tile + jnp.where(sub == 7, lasts[t + 1], 0.0)
            result.append(tile)
        return jnp.concatenate(result, axis=0)

    corners = [jnp.where(ends, x[40:48], 0.0) for x in blocks]
    beyond = [jnp.where(ends, pltpu.roll(x[40:48], 126, 1), 0.0) for x in blocks]
    corner = assemble(corners, beyond, beyond)
    main_ref[4] = corner
    lane = iota((40, 128), 1)
    right = jnp.zeros((40, 128), F32)
    left = jnp.zeros((40, 128), F32)
    for z in range(4):
        main = assemble(
            [x[8 * z : 8 * z + 8] for x in blocks],
            [turned(x[32:40], -z) for x in blocks],
            [turned(x[32:40], z) for x in blocks],
        )
        main_ref[z] = main
        lab = jnp.concatenate([x[48 + 8 * z : 56 + 8 * z] for x in (before, own, after)], axis=0)
        lab_ref[z] = lab
        lab = jnp.concatenate([lab, jnp.zeros((16, 128), F32)], axis=0)
        right = jnp.where((lane >> 4) == z, pltpu.roll(main, 16 * z + 16, 1), right)
        right = jnp.where((lane >> 4) == z + 4, pltpu.roll(lab, (16 * z + 80) % 128, 1), right)
        left = jnp.where((lane >> 4) == z, pltpu.roll(main, 16 * z, 1), left)
        left = jnp.where((lane >> 4) == z + 4, pltpu.roll(lab, 16 * z + 64, 1), left)
    right = jnp.where((lane < 64) & ((lane & 15) == 0), corner, right)
    left = jnp.where((lane < 64) & ((lane & 15) == 15), corner, left)
    send_a_ref[...] = jnp.where(even_col, right, left)
    send_b_ref[...] = jnp.where(even_col, left, right)


def shift_rows(x, s):
    return pltpu.roll(x, s % x.shape[0], 0)


def shift_cols(x, s):
    return pltpu.roll(x, s % x.shape[1], 1)


def cross(fields, outside):
    result = []
    for z in range(4):
        x = fields[z]
        around = shift_rows(x, 1) + shift_rows(x, -1) + shift_cols(x, 1) + shift_cols(x, -1)
        before = fields[z - 1] if z > 0 else outside
        after = fields[z + 1] if z < 3 else outside
        result.append((around + (before + after)) * (1.0 / 9.0) + x * (1.0 / 3.0))
    return result


def box(fields, outside, crop):
    result = []
    for z in range(4):
        before = fields[z - 1] if z > 0 else outside
        after = fields[z + 1] if z < 3 else outside
        x = fields[z] + (before + after)
        x = x + shift_rows(x, 1) + shift_rows(x, -1)
        if crop:
            x = x[8:32]
        result.append(x + shift_cols(x, 1) + shift_cols(x, -1))
    return result


def inverse(x):
    return 1.0 / x


def forward(e0, q0, inside, crop, keep):
    def middle(x):
        return x[8:32] if crop else x

    e, q, s = e0, q0, None
    for i in range(ITERS + 1):
        e = [jnp.where(inside, x, 1.0) for x in cross(e, 1.0)]
        q_next = [inverse(x) for x in e]
        mean = box(q_next, 1.0, crop)
        s_next = []
        for z in range(4):
            d_inv = inverse(mean[z] * (1.0 / 27.0))
            qz = middle(q[z])
            ratio = qz * d_inv
            ratio = ratio * ratio
            log_term = jnp.log(1.0 + ratio)
            change = SOFT * log_term
            if i == 0:
                s_next.append(change)
                keep(i, z, qz, d_inv, ratio, None, None, None)
            else:
                rest = 1.0 - s[z]
                power = jnp.exp(log_term * rest)
                s_next.append(s[z] + SOFT * jnp.log(1.0 + power))
                keep(i, z, qz, d_inv, ratio, change, rest, power)
        s, q = s_next, q_next
    return s, q


def skeleton_kernel(
    bias_ref, f_ref, main_ref, lab_ref, got_b_ref, got_a_ref,
    grad_ref, sums_ref,
    qs_ref, ds_ref, rs_ref, gain_ref,
):
    row_ids = lax.axis_index("gx") * 8 - 16 + iota((40, 256), 0)
    lane = iota((40, 256), 1)
    col = jnp.where(lane < 144, lane, lane - 256)
    col_ids = lax.axis_index("gy") * 128 + col
    inside = (row_ids >= 0) & (row_ids < lax.axis_size("gx") * 8)
    inside = inside & (col_ids >= 0) & (col_ids < lax.axis_size("gy") * 128) & (col >= -16)
    inside_f = jnp.where(inside, 1.0, 0.0)
    inner = inside_f[8:32]
    inner_b = inner > 0.5
    bias = bias_ref[0]

    even_col = (lax.axis_index("gy") & 1) == 0
    from_left = jnp.where(even_col, got_b_ref[...], got_a_ref[...])
    from_right = jnp.where(even_col, got_a_ref[...], got_b_ref[...])
    corner = main_ref[4]
    lane40 = iota((40, 128), 1)
    lane24 = lane40[:24]
    e0, q0, slope, probs, labels = [], [], [], [], []
    for z in range(4):
        to_zero, to_last = (128 - 16 * z) % 128, 112 - 16 * z
        left_zero, left_last = pltpu.roll(from_left, to_zero, 1), pltpu.roll(from_left, to_last, 1)
        right_zero, right_last = pltpu.roll(from_right, to_zero, 1), pltpu.roll(from_right, to_last, 1)
        main = main_ref[z]
        main = main + jnp.where(lane40 == 0, left_zero, jnp.where(lane40 == 127, right_last, 0.0))
        tail = jnp.where(lane40 >= 112, left_last, jnp.where(lane40 < 16, right_zero, 0.0))
        own_zero, own_last = pltpu.roll(corner, to_zero, 1), pltpu.roll(corner, to_last, 1)
        tail = tail + jnp.where(lane40 == 0, own_zero, jnp.where(lane40 == 127, own_last, 0.0))
        lab_left = pltpu.roll(from_left[:24], 48 - 16 * z, 1)
        lab_right = pltpu.roll(from_right[:24], 64 - 16 * z, 1)
        lab_tail = jnp.where(lane24 >= 112, lab_left, jnp.where(lane24 < 16, lab_right, 0.0))
        logits = jnp.concatenate([main, tail], axis=1) + bias
        small = jnp.exp(-jnp.abs(logits))
        scale = inverse(1.0 + small)
        prob = jnp.where(logits >= 0.0, scale, small * scale)
        prob = jnp.where(inside, prob, 0.0)
        e = jnp.exp(-SHARP * prob)
        e0.append(e)
        q0.append(inverse(e))
        weight = (small * scale) * scale
        slope.append(((-SHARP) * e * weight)[8:32] * inner)
        probs.append((prob[8:32], weight[8:32]))
        labels.append(jnp.concatenate([lab_ref[z], lab_tail], axis=1))

    low, high = jnp.exp(-SHARP * jnp.ones((24, 256), F32)), jnp.exp(SHARP * jnp.ones((24, 256), F32))
    true_skel, _ = forward(
        [jnp.where(x > 0.5, low, 1.0) for x in labels],
        [jnp.where(x > 0.5, high, 1.0) for x in labels],
        inner_b, False, lambda *factors: None,
    )

    def keep(i, z, qz, d_inv, ratio, change, rest, power):
        qs_ref[i, z] = qz
        ds_ref[i, z] = d_inv
        part = (-2.0 * SOFT) * (ratio * inverse(1.0 + ratio))
        if i > 0:
            share = power * inverse(1.0 + power)
            part = part * (share * rest)
            gain_ref[i, z] = 1.0 - share * change
        rs_ref[i, z] = part

    pred_skel, q_last = forward(e0, q0, inside, True, keep)

    def own(x):
        return x[8:16, :128]

    def total(values):
        acc = values[0] + values[1] + values[2] + values[3]
        return jnp.sum(jnp.sum(acc, axis=1, keepdims=True), axis=0, keepdims=True)

    t0 = total([own(pred_skel[z] * labels[z]) for z in range(4)])
    t1 = total([own(pred_skel[z]) for z in range(4)])
    t2 = total([own(true_skel[z] * probs[z][0]) for z in range(4)])
    t3 = total([own(true_skel[z]) for z in range(4)])

    weights = [labels, [inner] * 4]
    running = [jnp.ones((24, 256), F32)] * 4
    deep = [None, None]
    for i in range(ITERS, -1, -1):
        coefs = []
        for z in range(4):
            coefs.append(rs_ref[i, z] * running[z])
            if i > 0:
                running[z] = running[z] * gain_ref[i, z]
        for f in range(2):
            scaled = [coefs[z] * weights[f][z] for z in range(4)]
            spread = box([scaled[z] * ds_ref[i, z] for z in range(4)], 0.0, False)
            q_of = [q_last[z][8:32] if i == ITERS else qs_ref[i + 1, z] for z in range(4)]
            incoming = []
            for z in range(4):
                value = spread[z] * (q_of[z] * q_of[z]) * (-1.0 / 27.0)
                if deep[f] is not None:
                    value = value + deep[f][z]
                incoming.append(value * inner)
            moved = cross(incoming, 0.0)
            deep[f] = [moved[z] + scaled[z] * qs_ref[i, z] for z in range(4)]
    fields = [
        [deep[0][z] * slope[z] for z in range(4)],
        [deep[1][z] * slope[z] for z in range(4)],
        [true_skel[z] * probs[z][1] * inner for z in range(4)],
    ]
    bias_sums = [total([own(x) for x in field]) for field in fields]

    sub = iota((8, 256), 0)
    stacks = []
    for z in range(4):
        pieces = []
        for f in range(3):
            x = fields[f][z]
            edge = jnp.where(sub == 0, x[16:24], jnp.where(sub == 7, x[0:8], 0.0))
            block = jnp.concatenate([x[8:16], edge], axis=0)
            grad_ref[f, z] = block
            for d in range(3):
                moved = (shift_cols(block, d - 1) if d != 1 else block)[:, :128]
                upper = moved.astype(BF16)
                lower = (moved - upper.astype(F32)).astype(BF16)
                pieces += [upper, lower]
        stacks.append(jnp.concatenate(pieces, axis=0))
    offset = (iota((16, 256), 1) & 7) - edge_row(iota((16, 256), 0)) + 1
    picked = {}
    for a in range(3):
        moments = jnp.zeros((288, 256), F32)
        for z in range(4):
            if 0 <= z + a - 1 < 4:
                feats = f_ref[:, z + a - 1].reshape(256, 128)
                moments = moments + dot(stacks[z], feats, ((1,), (1,)))
        for f in range(3):
            for d in range(3):
                start = (f * 3 + d) * 32
                pair = moments[start : start + 16] + moments[start + 16 : start + 32]
                for b in range(3):
                    chosen = jnp.where(offset == b, pair, 0.0)
                    picked[b, f, a, d] = jnp.sum(chosen, axis=0, keepdims=True)
    order = [(f, a, d) for f in range(3) for a in range(3) for d in range(3)]
    groups = [[picked[(b,) + at] for at in order[:24]] for b in range(3)]
    rest = [picked[(b,) + at] for b in range(3) for at in order[24:]]
    groups.append(rest + [jnp.zeros((15, 256), F32)])
    result = jnp.zeros((24, 128), F32)
    for b in range(4):
        stacked = jnp.concatenate(groups[b], axis=0)
        collect = jnp.where((iota((256, 128), 0) >> 3) + 32 * b == iota((256, 128), 1), 1.0, 0.0)
        result = result + dot(stacked, collect, ((1,), (0,)), precision=lax.Precision.HIGHEST)
    row24, lane_of = iota((24, 128), 0), iota((24, 128), 1)
    for k, value in enumerate([t0, t1, t2, t3] + bias_sums):
        result = jnp.where(((row24 == 11) | (row24 == 23)) & (lane_of == 96 + k), value, result)
    for n in range(sums_ref.shape[0]):
        sums_ref[n] = result


def half_kernel(in_ref, out_ref):
    acc = in_ref[0]
    for n in range(1, in_ref.shape[0]):
        acc = acc + in_ref[n]
    half = jnp.where((lax.axis_index("gy") & 1) == 0, acc[:12], acc[12:])
    for n in range(out_ref.shape[0]):
        out_ref[n] = half[4 * (n % 3) : 4 * (n % 3) + 4]


def add_kernel(in_ref, out_ref):
    for part in range(3):
        acc = in_ref[part]
        for n in range(part + 3, in_ref.shape[0], 3):
            acc = acc + in_ref[n]
        out_ref[part] = acc


def loss_and_slopes(row):
    sums = [row[:, 96 + k : 97 + k] for k in range(7)]
    precision = (sums[0] + 1.0) / (sums[1] + 1.0)
    sensitivity = (sums[2] + 1.0) / (sums[3] + 1.0)
    both = precision + sensitivity
    loss = 1.0 - 2.0 * precision * sensitivity / both
    by_precision = -2.0 * (sensitivity / both) * (sensitivity / both)
    by_sensitivity = -2.0 * (precision / both) * (precision / both)
    slopes = [
        by_precision / (sums[1] + 1.0),
        -by_precision * precision / (sums[1] + 1.0),
        by_sensitivity / (sums[3] + 1.0),
    ]
    return loss, slopes, sums[4:]


def weight_kernel(
    own_ref, got_ref, feature_ref,
    loss_out_ref, weight_out_ref, bias_out_ref, feature_out_ref,
    loss_ref, weight_ref, bias_ref, sems,
):
    pairs = [
        (feature_ref, feature_out_ref), (loss_ref, loss_out_ref),
        (bias_ref, bias_out_ref), (weight_ref, weight_out_ref),
    ]
    copies = [pltpu.make_async_copy(x, y, sems.at[n]) for n, (x, y) in enumerate(pairs)]
    copies[0].start()
    even = (lax.axis_index("gy") & 1) == 0
    own, got = own_ref[...], got_ref[...]
    first, second = jnp.where(even, own, got), jnp.where(even, got, own)
    acc = jnp.concatenate([x[part] for x in (first, second) for part in range(3)], axis=0)
    loss, slopes, bias_sums = loss_and_slopes(acc[11:12])
    loss_ref[...] = loss
    bias_ref[...] = sum(slopes[f] * bias_sums[f] for f in range(3))
    copies[1].start()
    copies[2].start()
    group = iota((3, 128), 1) >> 5
    last = acc[18:21]
    for b in range(3):
        last = jnp.where(group == b, pltpu.roll(acc[3 * b : 3 * b + 3], (32 * b + 32) % 128, 1), last)
    third = jnp.concatenate([acc[18:24], last], axis=0)
    weight = slopes[0] * acc[0:9] + slopes[1] * acc[9:18] + slopes[2] * third
    for b in range(3):
        part = weight if b == 0 else pltpu.roll(weight, 128 - 32 * b, 1)
        for a in range(3):
            weight_ref[9 * a + 3 * b : 9 * a + 3 * b + 3] = part[3 * a : 3 * a + 3, :32]
    copies[3].start()
    for copy in copies:
        copy.wait()


def feature_kernel(sums_ref, grad_ref, a_ref, out_ref, *, voxels):
    _, slopes, _ = loss_and_slopes(sums_ref[2, 3:4])
    matrix = a_ref[...]
    parts = []
    for z in range(4):
        block = slopes[0] * grad_ref[0, z] + slopes[1] * grad_ref[1, z] + slopes[2] * grad_ref[2, z]
        block = block * voxels
        byd = []
        for d in range(3):
            moved = (shift_cols(block, d - 1) if d != 1 else block)[:, :128]
            upper = moved.astype(BF16)
            byd.append((upper, (moved - upper.astype(F32)).astype(BF16)))
        parts.append(byd)
    none = jnp.zeros((16, 128), BF16)
    for z in range(4):
        acc_z = None
        for level in range(2):
            stack = []
            for a in range(3):
                for d in range(3):
                    at = z - a + 1
                    stack.append(parts[at][d][level] if 0 <= at < 4 else none)
            term = dot(matrix, jnp.concatenate(stack, axis=0), ((0,), (0,)))
            acc_z = term if acc_z is None else acc_z + term
        out_ref[:, z] = acc_z.reshape(32, 8, 128).astype(BF16)


def call(kernel, out_shapes, *args, scratch=(), spaces={}, out_spaces={}):
    in_specs = [pl.BlockSpec(memory_space=spaces.get(n, pltpu.VMEM)) for n in range(len(args))]
    return pl.pallas_call(
        kernel,
        out_shape=[jax.ShapeDtypeStruct(shape, dtype) for shape, dtype in out_shapes],
        in_specs=in_specs,
        out_specs=[
            pl.BlockSpec(memory_space=out_spaces.get(n, pltpu.VMEM)) for n in range(len(out_shapes))
        ],
        scratch_shapes=list(scratch),
        compiler_params=pltpu.CompilerParams(vmem_limit_bytes=VMEM_LIMIT),
    )(*args)


def swapped(x, axis, step, phase):
    count = lax.axis_size(axis)
    pairs = []
    for n in range(count - step):
        if (n // step) % 2 == phase:
            pairs += [(n, n + step), (n + step, n)]
    return lax.ppermute(x, axis, pairs)


def local(features, vessel_label, conv_weight, conv_bias):
    gx, gy = lax.axis_size("gx"), lax.axis_size("gy")
    voxels = float(4 * 8 * gx * 128 * gy)
    matrix, near, far, features = call(
        partial_logits_kernel,
        [((144, 256), BF16), ((80, 128), F32), ((48, 128), F32), (features.shape, BF16)],
        *[pltpu.with_memory_space_constraint(x, pltpu.HBM) for x in (conv_weight, features, vessel_label)],
        scratch=[
            pltpu.VMEM((27, 32), BF16),
            pltpu.VMEM((4, 8, 128), jnp.int32),
            pltpu.SemaphoreType.DMA((3,)),
        ],
        spaces={0: pltpu.HBM, 1: pltpu.HBM, 2: pltpu.HBM},
    )
    two = [swapped(far, "gx", 2, phase) for phase in range(2)]
    one = [swapped(near, "gx", 1, phase) for phase in range(2)]
    main, labels, send_a, send_b = call(
        rows_kernel,
        [((5, 40, 128), F32), ((4, 24, 128), F32), ((40, 128), F32), ((40, 128), F32)],
        near, *two[::-1], *one[::-1],
    )
    got_b = swapped(send_b, "gy", 1, 1)
    got_a = swapped(send_a, "gy", 1, 0)
    field = pltpu.VMEM((ITERS + 1, 4, 24, 256), F32)
    grads, sums = call(
        skeleton_kernel,
        [((3, 4, 16, 256), F32), ((gy, 24, 128), F32)],
        conv_bias, features, main, labels, got_b, got_a,
        scratch=[field] * 4, spaces={0: pltpu.SMEM},
    )
    sums = lax.all_to_all(sums, "gy", 0, 0, tiled=True)
    sums = call(half_kernel, [((3 * gx, 4, 128), F32)], sums)[0]
    sums = lax.all_to_all(sums, "gx", 0, 0, tiled=True)
    sums = call(add_kernel, [((3, 4, 128), F32)], sums)[0]
    other = swapped(sums, "gy", 1, 0)

    def feature_part(*refs):
        feature_kernel(*refs, voxels=voxels)

    feature_grad = call(feature_part, [((32, 4, 8, 128), BF16)], sums, grads, matrix)[0]
    loss, weight_grad, bias_grad, feature_grad = call(
        weight_kernel,
        [((1, 1), F32), ((27, 32), F32), ((1, 1), F32), ((32, 4, 8, 128), BF16)],
        sums, other, feature_grad,
        scratch=[
            pltpu.VMEM((1, 1), F32),
            pltpu.VMEM((27, 32), F32),
            pltpu.VMEM((1, 1), F32),
            pltpu.SemaphoreType.DMA((4,)),
        ],
        out_spaces={n: pltpu.HBM for n in range(4)},
    )
    return (loss.reshape(()), weight_grad, bias_grad.reshape((1,)), feature_grad)


def solution(mesh):
    in_specs = (P(None, None, "gx", "gy"), P(None, "gx", "gy"), P(), P())
    out_specs = (P(), P(), P(), P(None, None, "gx", "gy"))
    return jax.shard_map(local, mesh=mesh, in_specs=in_specs, out_specs=out_specs, check_vma=False)
```

```python
import jax
import jax.numpy as jnp
from jax import lax
from jax.experimental import pallas as pl
from jax.experimental.pallas import tpu as pltpu
from jax.sharding import PartitionSpec as P

ITERS = 5
F32 = jnp.float32
BF16 = jnp.bfloat16
SHARP = 10.0
SOFT = 0.05
EDGE = 16
VMEM_LIMIT = 24 * 1024 * 1024


def iota(shape, dim):
    return lax.broadcasted_iota(jnp.int32, shape, dim)


def dot(a, b, dims, precision=None):
    return lax.dot_general(a, b, (dims, ((), ())), precision=precision, preferred_element_type=F32)


def edge_row(q):
    return jnp.where(q < 8, q, jnp.where(q == 8, 8, jnp.where(q == 15, -1, -100)))


def weight_matrix(w):
    spread = jnp.where((iota((32, 256), 1) >> 3) == iota((32, 256), 0), 1.0, 0.0).astype(BF16)
    by_lane = dot(w, spread, ((1,), (0,))).astype(BF16)
    row = iota((144, 27), 0)
    ad = row >> 4
    base = ad + 6 * (jnp.where(ad >= 3, 1, 0) + jnp.where(ad >= 6, 1, 0))
    col = iota((144, 27), 1)
    offset = (iota((144, 256), 1) & 7) - edge_row(iota((144, 256), 0) & 15) + 1
    matrix = jnp.zeros((144, 256), F32)
    for b in range(3):
        pick = jnp.where(col == base + 3 * b, 1.0, 0.0).astype(BF16)
        matrix = matrix + jnp.where(offset == b, dot(pick, by_lane, ((1,), (0,))), 0.0)
    return matrix.astype(BF16)


def turned(x, s):
    return x if s == 0 else pltpu.roll(x, s % x.shape[0], 0)


def at_end(lane):
    return ((lane & 15) == 0) | ((lane & 15) == 15)


def partial_logits_kernel(
    w_hbm, f_hbm, lab_hbm, a_ref, near_ref, far_ref, f_ref, w_ref, lab_ref, sems
):
    pairs = [(w_hbm, w_ref), (f_hbm, f_ref), (lab_hbm, lab_ref)]
    copies = [pltpu.make_async_copy(x, y, sems.at[n]) for n, (x, y) in enumerate(pairs)]
    for copy in copies:
        copy.start()
    copies[0].wait()
    matrix = weight_matrix(w_ref[...])
    a_ref[...] = matrix
    copies[1].wait()
    lane = iota((16, 128), 1)
    sub = iota((8, 128), 0)
    terms = [
        dot(matrix, f_ref[:, z].reshape(256, 128), ((1,), (0,))).reshape(3, 3, 16, 128)
        for z in range(4)
    ]
    corner = jnp.zeros((16, 128), F32)
    edges = jnp.zeros((8, 128), F32)
    for z in range(4):
        byd = []
        for d in range(3):
            byd.append(sum(terms[z + a - 1][a, d] for a in range(3) if 0 <= z + a - 1 < 4))
        main = byd[1]
        main = main + jnp.where(lane >= 1, pltpu.roll(byd[0], 1, 1), 0.0)
        main = main + jnp.where(lane <= 126, pltpu.roll(byd[2], 127, 1), 0.0)
        near_ref[8 * z : 8 * z + 8] = main[:8]
        far_ref[8 * z : 8 * z + 8] = main[:8]
        edges = jnp.where(sub == z, turned(main[8:], z), edges)
        edges = jnp.where(sub == 7 - z, turned(main[8:], -z), edges)
        low, high = 16 * z, 16 * z + 15
        corner = jnp.where(lane == low, pltpu.roll(byd[0], low + 1, 1), corner)
        corner = jnp.where(lane == high, pltpu.roll(byd[2], high, 1), corner)
    corners = jnp.where(at_end(lane[:8]), corner[:8], pltpu.roll(corner[8:], 2, 1))
    near_ref[32:40] = edges
    far_ref[32:40] = edges
    near_ref[40:48] = corners
    far_ref[40:48] = corners
    far_ref[48:88] = jnp.zeros((40, 128), F32)
    copies[2].wait()
    near_ref[48:80] = lab_ref[...].reshape(32, 128).astype(F32)


def rows_kernel(
    own_ref, two_b_ref, two_a_ref, one_b_ref, one_a_ref, main_ref, lab_ref, send_a_ref, send_b_ref
):
    row_block, col_block = lax.axis_index("gx"), lax.axis_index("gy")
    even1 = (row_block & 1) == 0
    even2 = (row_block & 2) == 0
    even_col = (col_block & 1) == 0
    own = own_ref[...]
    one_a, one_b, two_a, two_b = one_a_ref[...], one_b_ref[...], two_a_ref[...], two_b_ref[...]
    before, after = jnp.where(even1, one_b, one_a), jnp.where(even1, one_a, one_b)
    two_a, two_b = two_a[:48], two_b[:48]
    blocks = [jnp.where(even2, two_b, two_a), before, own, after, jnp.where(even2, two_a, two_b)]
    sub = iota((8, 128), 0)
    ends = at_end(iota((8, 128), 1))

    def assemble(tiles, firsts, lasts):
        result = []
        for t in range(5):
            tile = tiles[t]
            if t > 0:
                tile = tile + jnp.where(sub == 0, firsts[t - 1], 0.0)
            if t < 4:
                tile = tile + jnp.where(sub == 7, lasts[t + 1], 0.0)
            result.append(tile)
        return jnp.concatenate(result, axis=0)

    corners = [jnp.where(ends, x[40:48], 0.0) for x in blocks]
    beyond = [jnp.where(ends, pltpu.roll(x[40:48], 126, 1), 0.0) for x in blocks]
    corner = assemble(corners, beyond, beyond)
    main_ref[4] = corner
    lane = iota((40, 128), 1)
    right = jnp.zeros((40, 128), F32)
    left = jnp.zeros((40, 128), F32)
    for z in range(4):
        main = assemble(
            [x[8 * z : 8 * z + 8] for x in blocks],
            [turned(x[32:40], -z) for x in blocks],
            [turned(x[32:40], z) for x in blocks],
        )
        main_ref[z] = main
        lab = jnp.concatenate([x[48 + 8 * z : 56 + 8 * z] for x in (before, own, after)], axis=0)
        lab_ref[z] = lab
        lab = jnp.concatenate([lab, jnp.zeros((16, 128), F32)], axis=0)
        right = jnp.where((lane >> 4) == z, pltpu.roll(main, 16 * z + 16, 1), right)
        right = jnp.where((lane >> 4) == z + 4, pltpu.roll(lab, (16 * z + 80) % 128, 1), right)
        left = jnp.where((lane >> 4) == z, pltpu.roll(main, 16 * z, 1), left)
        left = jnp.where((lane >> 4) == z + 4, pltpu.roll(lab, 16 * z + 64, 1), left)
    right = jnp.where((lane < 64) & ((lane & 15) == 0), corner, right)
    left = jnp.where((lane < 64) & ((lane & 15) == 15), corner, left)
    send_a_ref[...] = jnp.where(even_col, right, left)
    send_b_ref[...] = jnp.where(even_col, left, right)


def shift_rows(x, s):
    return pltpu.roll(x, s % x.shape[0], 0)


def shift_cols(x, s):
    return pltpu.roll(x, s % x.shape[1], 1)


def cross(fields, outside):
    result = []
    for z in range(4):
        x = fields[z]
        around = shift_rows(x, 1) + shift_rows(x, -1) + shift_cols(x, 1) + shift_cols(x, -1)
        before = fields[z - 1] if z > 0 else outside
        after = fields[z + 1] if z < 3 else outside
        result.append((around + (before + after)) * (1.0 / 9.0) + x * (1.0 / 3.0))
    return result


def box(fields, outside, crop):
    result = []
    for z in range(4):
        before = fields[z - 1] if z > 0 else outside
        after = fields[z + 1] if z < 3 else outside
        x = fields[z] + (before + after)
        x = x + shift_rows(x, 1) + shift_rows(x, -1)
        if crop:
            x = x[8:32]
        result.append(x + shift_cols(x, 1) + shift_cols(x, -1))
    return result


def inverse(x):
    return 1.0 / x


def forward(e0, q0, inside, crop, keep):
    def middle(x):
        return x[8:32] if crop else x

    e, q, s = e0, q0, None
    for i in range(ITERS + 1):
        e = [jnp.where(inside, x, 1.0) for x in cross(e, 1.0)]
        q_next = [inverse(x) for x in e]
        mean = box(q_next, 1.0, crop)
        s_next = []
        for z in range(4):
            d_inv = inverse(mean[z] * (1.0 / 27.0))
            qz = middle(q[z])
            ratio = qz * d_inv
            ratio = ratio * ratio
            log_term = jnp.log(1.0 + ratio)
            change = SOFT * log_term
            if i == 0:
                s_next.append(change)
                keep(i, z, qz, d_inv, ratio, None, None, None)
            else:
                rest = 1.0 - s[z]
                power = jnp.exp(log_term * rest)
                s_next.append(s[z] + SOFT * jnp.log(1.0 + power))
                keep(i, z, qz, d_inv, ratio, change, rest, power)
        s, q = s_next, q_next
    return s, q


def skeleton_kernel(
    bias_ref, f_ref, main_ref, lab_ref, got_b_ref, got_a_ref,
    grad_ref, keep_ref, send_ref,
    qs_ref, ds_ref, rs_ref, gain_ref,
):
    row_ids = lax.axis_index("gx") * 8 - 16 + iota((40, 256), 0)
    lane = iota((40, 256), 1)
    col = jnp.where(lane < 144, lane, lane - 256)
    col_ids = lax.axis_index("gy") * 128 + col
    inside = (row_ids >= 0) & (row_ids < lax.axis_size("gx") * 8)
    inside = inside & (col_ids >= 0) & (col_ids < lax.axis_size("gy") * 128) & (col >= -16)
    inside_f = jnp.where(inside, 1.0, 0.0)
    inner = inside_f[8:32]
    inner_b = inner > 0.5
    bias = bias_ref[0]

    even_col = (lax.axis_index("gy") & 1) == 0
    from_left = jnp.where(even_col, got_b_ref[...], got_a_ref[...])
    from_right = jnp.where(even_col, got_a_ref[...], got_b_ref[...])
    corner = main_ref[4]
    lane40 = iota((40, 128), 1)
    lane24 = lane40[:24]
    e0, q0, slope, probs, labels = [], [], [], [], []
    for z in range(4):
        to_zero, to_last = (128 - 16 * z) % 128, 112 - 16 * z
        left_zero, left_last = pltpu.roll(from_left, to_zero, 1), pltpu.roll(from_left, to_last, 1)
        right_zero, right_last = pltpu.roll(from_right, to_zero, 1), pltpu.roll(from_right, to_last, 1)
        main = main_ref[z]
        main = main + jnp.where(lane40 == 0, left_zero, jnp.where(lane40 == 127, right_last, 0.0))
        tail = jnp.where(lane40 >= 112, left_last, jnp.where(lane40 < 16, right_zero, 0.0))
        own_zero, own_last = pltpu.roll(corner, to_zero, 1), pltpu.roll(corner, to_last, 1)
        tail = tail + jnp.where(lane40 == 0, own_zero, jnp.where(lane40 == 127, own_last, 0.0))
        lab_left = pltpu.roll(from_left[:24], 48 - 16 * z, 1)
        lab_right = pltpu.roll(from_right[:24], 64 - 16 * z, 1)
        lab_tail = jnp.where(lane24 >= 112, lab_left, jnp.where(lane24 < 16, lab_right, 0.0))
        logits = jnp.concatenate([main, tail], axis=1) + bias
        small = jnp.exp(-jnp.abs(logits))
        scale = inverse(1.0 + small)
        prob = jnp.where(logits >= 0.0, scale, small * scale)
        prob = jnp.where(inside, prob, 0.0)
        e = jnp.exp(-SHARP * prob)
        e0.append(e)
        q0.append(inverse(e))
        weight = (small * scale) * scale
        slope.append(((-SHARP) * e * weight)[8:32] * inner)
        probs.append((prob[8:32], weight[8:32]))
        labels.append(jnp.concatenate([lab_ref[z], lab_tail], axis=1))

    low, high = jnp.exp(-SHARP * jnp.ones((24, 256), F32)), jnp.exp(SHARP * jnp.ones((24, 256), F32))
    true_skel, _ = forward(
        [jnp.where(x > 0.5, low, 1.0) for x in labels],
        [jnp.where(x > 0.5, high, 1.0) for x in labels],
        inner_b, False, lambda *factors: None,
    )

    def keep(i, z, qz, d_inv, ratio, change, rest, power):
        qs_ref[i, z] = qz
        ds_ref[i, z] = d_inv
        part = (-2.0 * SOFT) * (ratio * inverse(1.0 + ratio))
        if i > 0:
            share = power * inverse(1.0 + power)
            part = part * (share * rest)
            gain_ref[i, z] = 1.0 - share * change
        rs_ref[i, z] = part

    pred_skel, q_last = forward(e0, q0, inside, True, keep)

    def own(x):
        return x[8:16, :128]

    def total(values):
        acc = values[0] + values[1] + values[2] + values[3]
        return jnp.sum(jnp.sum(acc, axis=1, keepdims=True), axis=0, keepdims=True)

    t0 = total([own(pred_skel[z] * labels[z]) for z in range(4)])
    t1 = total([own(pred_skel[z]) for z in range(4)])
    t2 = total([own(true_skel[z] * probs[z][0]) for z in range(4)])
    t3 = total([own(true_skel[z]) for z in range(4)])

    weights = [labels, [inner] * 4]
    running = [jnp.ones((24, 256), F32)] * 4
    deep = [None, None]
    for i in range(ITERS, -1, -1):
        coefs = []
        for z in range(4):
            coefs.append(rs_ref[i, z] * running[z])
            if i > 0:
                running[z] = running[z] * gain_ref[i, z]
        for f in range(2):
            scaled = [coefs[z] * weights[f][z] for z in range(4)]
            spread = box([scaled[z] * ds_ref[i, z] for z in range(4)], 0.0, False)
            q_of = [q_last[z][8:32] if i == ITERS else qs_ref[i + 1, z] for z in range(4)]
            incoming = []
            for z in range(4):
                value = spread[z] * (q_of[z] * q_of[z]) * (-1.0 / 27.0)
                if deep[f] is not None:
                    value = value + deep[f][z]
                incoming.append(value * inner)
            moved = cross(incoming, 0.0)
            deep[f] = [moved[z] + scaled[z] * qs_ref[i, z] for z in range(4)]
    fields = [
        [deep[0][z] * slope[z] for z in range(4)],
        [deep[1][z] * slope[z] for z in range(4)],
        [true_skel[z] * probs[z][1] * inner for z in range(4)],
    ]
    bias_sums = [total([own(x) for x in field]) for field in fields]

    sub = iota((8, 256), 0)
    stacks = []
    for z in range(4):
        pieces = []
        for f in range(3):
            x = fields[f][z]
            edge = jnp.where(sub == 0, x[16:24], jnp.where(sub == 7, x[0:8], 0.0))
            block = jnp.concatenate([x[8:16], edge], axis=0)
            grad_ref[f, z] = block
            for d in range(3):
                moved = (shift_cols(block, d - 1) if d != 1 else block)[:, :128]
                upper = moved.astype(BF16)
                lower = (moved - upper.astype(F32)).astype(BF16)
                pieces += [upper, lower]
        stacks.append(jnp.concatenate(pieces, axis=0))
    offset = (iota((16, 256), 1) & 7) - edge_row(iota((16, 256), 0)) + 1
    picked = {}
    for a in range(3):
        moments = jnp.zeros((288, 256), F32)
        for z in range(4):
            if 0 <= z + a - 1 < 4:
                feats = f_ref[:, z + a - 1].reshape(256, 128)
                moments = moments + dot(stacks[z], feats, ((1,), (1,)))
        for f in range(3):
            for d in range(3):
                start = (f * 3 + d) * 32
                pair = moments[start : start + 16] + moments[start + 16 : start + 32]
                for b in range(3):
                    chosen = jnp.where(offset == b, pair, 0.0)
                    picked[b, f, a, d] = jnp.sum(chosen, axis=0, keepdims=True)
    order = [(f, a, d) for f in range(3) for a in range(3) for d in range(3)]
    groups = [[picked[(b,) + at] for at in order[:24]] for b in range(3)]
    rest = [picked[(b,) + at] for b in range(3) for at in order[24:]]
    groups.append(rest + [jnp.zeros((15, 256), F32)])
    result = jnp.zeros((24, 128), F32)
    for b in range(4):
        stacked = jnp.concatenate(groups[b], axis=0)
        collect = jnp.where((iota((256, 128), 0) >> 3) + 32 * b == iota((256, 128), 1), 1.0, 0.0)
        result = result + dot(stacked, collect, ((1,), (0,)), precision=lax.Precision.HIGHEST)
    row24, lane_of = iota((24, 128), 0), iota((24, 128), 1)
    for k, value in enumerate([t0, t1, t2, t3] + bias_sums):
        result = jnp.where(((row24 == 11) | (row24 == 23)) & (lane_of == 96 + k), value, result)
    keep_ref[...] = jnp.where(even_col, result[:12], result[12:])
    send_ref[...] = jnp.where(even_col, result[12:], result[:12])


def pair_kernel(own_ref, got_ref, out_ref):
    out_ref[...] = own_ref[...] + got_ref[...]


def four_kernel(own_ref, one_ref, two_ref, three_ref, out_ref):
    half = (own_ref[...] + one_ref[...]) + (two_ref[...] + three_ref[...])
    for n in range(out_ref.shape[0]):
        out_ref[n] = half[4 * (n % 3) : 4 * (n % 3) + 4]


def add_kernel(in_ref, out_ref):
    for part in range(3):
        acc = in_ref[part]
        for n in range(part + 3, in_ref.shape[0], 3):
            acc = acc + in_ref[n]
        out_ref[part] = acc


def loss_and_slopes(row):
    sums = [row[:, 96 + k : 97 + k] for k in range(7)]
    precision = (sums[0] + 1.0) / (sums[1] + 1.0)
    sensitivity = (sums[2] + 1.0) / (sums[3] + 1.0)
    both = precision + sensitivity
    loss = 1.0 - 2.0 * precision * sensitivity / both
    by_precision = -2.0 * (sensitivity / both) * (sensitivity / both)
    by_sensitivity = -2.0 * (precision / both) * (precision / both)
    slopes = [
        by_precision / (sums[1] + 1.0),
        -by_precision * precision / (sums[1] + 1.0),
        by_sensitivity / (sums[3] + 1.0),
    ]
    return loss, slopes, sums[4:]


def weight_kernel(
    own_ref, got_ref, feature_ref,
    loss_out_ref, weight_out_ref, bias_out_ref, feature_out_ref,
    loss_ref, weight_ref, bias_ref, sems,
):
    pairs = [
        (feature_ref, feature_out_ref), (loss_ref, loss_out_ref),
        (bias_ref, bias_out_ref), (weight_ref, weight_out_ref),
    ]
    copies = [pltpu.make_async_copy(x, y, sems.at[n]) for n, (x, y) in enumerate(pairs)]
    copies[0].start()
    even = (lax.axis_index("gy") & 1) == 0
    own, got = own_ref[...], got_ref[...]
    first, second = jnp.where(even, own, got), jnp.where(even, got, own)
    acc = jnp.concatenate([x[part] for x in (first, second) for part in range(3)], axis=0)
    loss, slopes, bias_sums = loss_and_slopes(acc[11:12])
    loss_ref[...] = loss
    bias_ref[...] = sum(slopes[f] * bias_sums[f] for f in range(3))
    copies[1].start()
    copies[2].start()
    group = iota((3, 128), 1) >> 5
    last = acc[18:21]
    for b in range(3):
        last = jnp.where(group == b, pltpu.roll(acc[3 * b : 3 * b + 3], (32 * b + 32) % 128, 1), last)
    third = jnp.concatenate([acc[18:24], last], axis=0)
    weight = slopes[0] * acc[0:9] + slopes[1] * acc[9:18] + slopes[2] * third
    for b in range(3):
        part = weight if b == 0 else pltpu.roll(weight, 128 - 32 * b, 1)
        for a in range(3):
            weight_ref[9 * a + 3 * b : 9 * a + 3 * b + 3] = part[3 * a : 3 * a + 3, :32]
    copies[3].start()
    for copy in copies:
        copy.wait()


def feature_kernel(sums_ref, grad_ref, a_ref, out_ref, *, voxels):
    _, slopes, _ = loss_and_slopes(sums_ref[2, 3:4])
    matrix = a_ref[...]
    parts = []
    for z in range(4):
        block = slopes[0] * grad_ref[0, z] + slopes[1] * grad_ref[1, z] + slopes[2] * grad_ref[2, z]
        block = block * voxels
        byd = []
        for d in range(3):
            moved = (shift_cols(block, d - 1) if d != 1 else block)[:, :128]
            upper = moved.astype(BF16)
            byd.append((upper, (moved - upper.astype(F32)).astype(BF16)))
        parts.append(byd)
    none = jnp.zeros((16, 128), BF16)
    for z in range(4):
        acc_z = None
        for level in range(2):
            stack = []
            for a in range(3):
                for d in range(3):
                    at = z - a + 1
                    stack.append(parts[at][d][level] if 0 <= at < 4 else none)
            term = dot(matrix, jnp.concatenate(stack, axis=0), ((0,), (0,)))
            acc_z = term if acc_z is None else acc_z + term
        out_ref[:, z] = acc_z.reshape(32, 8, 128).astype(BF16)


def call(kernel, out_shapes, *args, scratch=(), spaces={}, out_spaces={}):
    in_specs = [pl.BlockSpec(memory_space=spaces.get(n, pltpu.VMEM)) for n in range(len(args))]
    return pl.pallas_call(
        kernel,
        out_shape=[jax.ShapeDtypeStruct(shape, dtype) for shape, dtype in out_shapes],
        in_specs=in_specs,
        out_specs=[
            pl.BlockSpec(memory_space=out_spaces.get(n, pltpu.VMEM)) for n in range(len(out_shapes))
        ],
        scratch_shapes=list(scratch),
        compiler_params=pltpu.CompilerParams(vmem_limit_bytes=VMEM_LIMIT),
    )(*args)


def swapped(x, axis, step, phase):
    count = lax.axis_size(axis)
    pairs = []
    for n in range(count - step):
        if (n // step) % 2 == phase:
            pairs += [(n, n + step), (n + step, n)]
    return lax.ppermute(x, axis, pairs)


def local(features, vessel_label, conv_weight, conv_bias):
    gx, gy = lax.axis_size("gx"), lax.axis_size("gy")
    voxels = float(4 * 8 * gx * 128 * gy)
    matrix, near, far, features = call(
        partial_logits_kernel,
        [((144, 256), BF16), ((80, 128), F32), ((88, 128), F32), (features.shape, BF16)],
        *[pltpu.with_memory_space_constraint(x, pltpu.HBM) for x in (conv_weight, features, vessel_label)],
        scratch=[
            pltpu.VMEM((27, 32), BF16),
            pltpu.VMEM((4, 8, 128), jnp.int32),
            pltpu.SemaphoreType.DMA((3,)),
        ],
        spaces={0: pltpu.HBM, 1: pltpu.HBM, 2: pltpu.HBM},
    )
    two = [swapped(far, "gx", 2, phase) for phase in range(2)]
    one = [swapped(near, "gx", 1, phase) for phase in range(2)]
    main, labels, send_a, send_b = call(
        rows_kernel,
        [((5, 40, 128), F32), ((4, 24, 128), F32), ((40, 128), F32), ((40, 128), F32)],
        near, *two[::-1], *one[::-1],
    )
    got_b = swapped(send_b, "gy", 1, 1)
    got_a = swapped(send_a, "gy", 1, 0)
    field = pltpu.VMEM((ITERS + 1, 4, 24, 256), F32)
    grads, keep, send = call(
        skeleton_kernel,
        [((3, 4, 16, 256), F32), ((12, 128), F32), ((12, 128), F32)],
        conv_bias, features, main, labels, got_b, got_a,
        scratch=[field] * 4, spaces={0: pltpu.SMEM},
    )
    half = call(pair_kernel, [((12, 128), F32)], keep, swapped(send, "gy", 1, 0))[0]
    others = [lax.ppermute(half, "gy", [(n, n ^ mask) for n in range(gy)]) for mask in (2, 4, 6)]
    sums = call(four_kernel, [((3 * gx, 4, 128), F32)], half, *others)[0]
    sums = lax.all_to_all(sums, "gx", 0, 0, tiled=True)
    sums = call(add_kernel, [((3, 4, 128), F32)], sums)[0]
    other = swapped(sums, "gy", 1, 0)

    def feature_part(*refs):
        feature_kernel(*refs, voxels=voxels)

    feature_grad = call(feature_part, [((32, 4, 8, 128), BF16)], sums, grads, matrix)[0]
    loss, weight_grad, bias_grad, feature_grad = call(
        weight_kernel,
        [((1, 1), F32), ((27, 32), F32), ((1, 1), F32), ((32, 4, 8, 128), BF16)],
        sums, other, feature_grad,
        scratch=[
            pltpu.VMEM((1, 1), F32),
            pltpu.VMEM((27, 32), F32),
            pltpu.VMEM((1, 1), F32),
            pltpu.SemaphoreType.DMA((4,)),
        ],
        out_spaces={n: pltpu.HBM for n in range(4)},
    )
    return (loss.reshape(()), weight_grad, bias_grad.reshape((1,)), feature_grad)


def solution(mesh):
    in_specs = (P(None, None, "gx", "gy"), P(None, "gx", "gy"), P(), P())
    out_specs = (P(), P(), P(), P(None, None, "gx", "gy"))
    return jax.shard_map(local, mesh=mesh, in_specs=in_specs, out_specs=out_specs, check_vma=False)
```

```python
import jax
import jax.numpy as jnp
from jax import lax
from jax.experimental import pallas as pl
from jax.experimental.pallas import tpu as pltpu
from jax.sharding import PartitionSpec as P

ITERS = 5
F32 = jnp.float32
BF16 = jnp.bfloat16
SHARP = 10.0
SOFT = 0.05
EDGE = 16
VMEM_LIMIT = 24 * 1024 * 1024


def iota(shape, dim):
    return lax.broadcasted_iota(jnp.int32, shape, dim)


def dot(a, b, dims, precision=None):
    return lax.dot_general(a, b, (dims, ((), ())), precision=precision, preferred_element_type=F32)


def edge_row(q):
    return jnp.where(q < 8, q, jnp.where(q == 8, 8, jnp.where(q == 15, -1, -100)))


def weight_matrix(w):
    spread = jnp.where((iota((32, 256), 1) >> 3) == iota((32, 256), 0), 1.0, 0.0).astype(BF16)
    by_lane = dot(w, spread, ((1,), (0,))).astype(BF16)
    row = iota((144, 27), 0)
    ad = row >> 4
    base = ad + 6 * (jnp.where(ad >= 3, 1, 0) + jnp.where(ad >= 6, 1, 0))
    col = iota((144, 27), 1)
    offset = (iota((144, 256), 1) & 7) - edge_row(iota((144, 256), 0) & 15) + 1
    matrix = jnp.zeros((144, 256), F32)
    for b in range(3):
        pick = jnp.where(col == base + 3 * b, 1.0, 0.0).astype(BF16)
        matrix = matrix + jnp.where(offset == b, dot(pick, by_lane, ((1,), (0,))), 0.0)
    return matrix.astype(BF16)


def turned(x, s):
    return x if s == 0 else pltpu.roll(x, s % x.shape[0], 0)


def at_end(lane):
    return ((lane & 15) == 0) | ((lane & 15) == 15)


def partial_logits_kernel(
    w_hbm, f_hbm, lab_hbm, a_ref, near_ref, far_ref, f_ref, w_ref, lab_ref, sems
):
    pairs = [(w_hbm, w_ref), (f_hbm, f_ref), (lab_hbm, lab_ref)]
    copies = [pltpu.make_async_copy(x, y, sems.at[n]) for n, (x, y) in enumerate(pairs)]
    for copy in copies:
        copy.start()
    copies[0].wait()
    matrix = weight_matrix(w_ref[...])
    a_ref[...] = matrix
    copies[1].wait()
    lane = iota((16, 128), 1)
    sub = iota((8, 128), 0)
    terms = [
        dot(matrix, f_ref[:, z].reshape(256, 128), ((1,), (0,))).reshape(3, 3, 16, 128)
        for z in range(4)
    ]
    corner = jnp.zeros((16, 128), F32)
    edges = jnp.zeros((8, 128), F32)
    for z in range(4):
        byd = []
        for d in range(3):
            byd.append(sum(terms[z + a - 1][a, d] for a in range(3) if 0 <= z + a - 1 < 4))
        main = byd[1]
        main = main + jnp.where(lane >= 1, pltpu.roll(byd[0], 1, 1), 0.0)
        main = main + jnp.where(lane <= 126, pltpu.roll(byd[2], 127, 1), 0.0)
        near_ref[8 * z : 8 * z + 8] = main[:8]
        far_ref[8 * z : 8 * z + 8] = main[:8]
        edges = jnp.where(sub == z, turned(main[8:], z), edges)
        edges = jnp.where(sub == 7 - z, turned(main[8:], -z), edges)
        low, high = 16 * z, 16 * z + 15
        corner = jnp.where(lane == low, pltpu.roll(byd[0], low + 1, 1), corner)
        corner = jnp.where(lane == high, pltpu.roll(byd[2], high, 1), corner)
    corners = jnp.where(at_end(lane[:8]), corner[:8], pltpu.roll(corner[8:], 2, 1))
    near_ref[32:40] = edges
    far_ref[32:40] = edges
    near_ref[40:48] = corners
    far_ref[40:48] = corners
    far_ref[48:88] = jnp.zeros((40, 128), F32)
    copies[2].wait()
    near_ref[48:80] = lab_ref[...].reshape(32, 128).astype(F32)


def rows_kernel(
    own_ref, two_b_ref, two_a_ref, one_b_ref, one_a_ref, main_ref, lab_ref, send_a_ref, send_b_ref
):
    row_block, col_block = lax.axis_index("gx"), lax.axis_index("gy")
    even1 = (row_block & 1) == 0
    even2 = (row_block & 2) == 0
    even_col = (col_block & 1) == 0
    own = own_ref[...]
    one_a, one_b, two_a, two_b = one_a_ref[...], one_b_ref[...], two_a_ref[...], two_b_ref[...]
    before, after = jnp.where(even1, one_b, one_a), jnp.where(even1, one_a, one_b)
    two_a, two_b = two_a[:48], two_b[:48]
    blocks = [jnp.where(even2, two_b, two_a), before, own, after, jnp.where(even2, two_a, two_b)]
    sub = iota((8, 128), 0)
    ends = at_end(iota((8, 128), 1))

    def assemble(tiles, firsts, lasts):
        result = []
        for t in range(5):
            tile = tiles[t]
            if t > 0:
                tile = tile + jnp.where(sub == 0, firsts[t - 1], 0.0)
            if t < 4:
                tile = tile + jnp.where(sub == 7, lasts[t + 1], 0.0)
            result.append(tile)
        return jnp.concatenate(result, axis=0)

    corners = [jnp.where(ends, x[40:48], 0.0) for x in blocks]
    beyond = [jnp.where(ends, pltpu.roll(x[40:48], 126, 1), 0.0) for x in blocks]
    corner = assemble(corners, beyond, beyond)
    main_ref[4] = corner
    lane = iota((40, 128), 1)
    right = jnp.zeros((40, 128), F32)
    left = jnp.zeros((40, 128), F32)
    for z in range(4):
        main = assemble(
            [x[8 * z : 8 * z + 8] for x in blocks],
            [turned(x[32:40], -z) for x in blocks],
            [turned(x[32:40], z) for x in blocks],
        )
        main_ref[z] = main
        lab = jnp.concatenate([x[48 + 8 * z : 56 + 8 * z] for x in (before, own, after)], axis=0)
        lab_ref[z] = lab
        lab = jnp.concatenate([lab, jnp.zeros((16, 128), F32)], axis=0)
        right = jnp.where((lane >> 4) == z, pltpu.roll(main, 16 * z + 16, 1), right)
        right = jnp.where((lane >> 4) == z + 4, pltpu.roll(lab, (16 * z + 80) % 128, 1), right)
        left = jnp.where((lane >> 4) == z, pltpu.roll(main, 16 * z, 1), left)
        left = jnp.where((lane >> 4) == z + 4, pltpu.roll(lab, 16 * z + 64, 1), left)
    right = jnp.where((lane < 64) & ((lane & 15) == 0), corner, right)
    left = jnp.where((lane < 64) & ((lane & 15) == 15), corner, left)
    send_a_ref[...] = jnp.where(even_col, right, left)
    send_b_ref[...] = jnp.where(even_col, left, right)


def shift_rows(x, s):
    return pltpu.roll(x, s % x.shape[0], 0)


def shift_cols(x, s):
    return pltpu.roll(x, s % x.shape[1], 1)


def cross(fields, outside):
    result = []
    for z in range(4):
        x = fields[z]
        around = shift_rows(x, 1) + shift_rows(x, -1) + shift_cols(x, 1) + shift_cols(x, -1)
        before = fields[z - 1] if z > 0 else outside
        after = fields[z + 1] if z < 3 else outside
        result.append((around + (before + after)) * (1.0 / 9.0) + x * (1.0 / 3.0))
    return result


def box(fields, outside, crop):
    result = []
    for z in range(4):
        before = fields[z - 1] if z > 0 else outside
        after = fields[z + 1] if z < 3 else outside
        x = fields[z] + (before + after)
        x = x + shift_rows(x, 1) + shift_rows(x, -1)
        if crop:
            x = x[8:32]
        result.append(x + shift_cols(x, 1) + shift_cols(x, -1))
    return result


def inverse(x):
    return 1.0 / x


def forward_step(i, state, inside, crop, keep):
    def middle(x):
        return x[8:32] if crop else x

    e, q, s = state
    e = [jnp.where(inside, x, 1.0) for x in cross(e, 1.0)]
    q_next = [inverse(x) for x in e]
    mean = box(q_next, 1.0, crop)
    s_next = []
    for z in range(4):
        d_inv = inverse(mean[z] * (1.0 / 27.0))
        qz = middle(q[z])
        ratio = qz * d_inv
        ratio = ratio * ratio
        log_term = jnp.log(1.0 + ratio)
        change = SOFT * log_term
        if i == 0:
            s_next.append(change)
            keep(i, z, qz, d_inv, ratio, None, None, None)
        else:
            rest = 1.0 - s[z]
            power = jnp.exp(log_term * rest)
            s_next.append(s[z] + SOFT * jnp.log(1.0 + power))
            keep(i, z, qz, d_inv, ratio, change, rest, power)
    return e, q_next, s_next


def skeleton_kernel(
    bias_ref, f_ref, main_ref, lab_ref, got_b_ref, got_a_ref,
    grad_ref, keep_ref, send_ref,
    qs_ref, ds_ref, rs_ref, gain_ref,
):
    row_ids = lax.axis_index("gx") * 8 - 16 + iota((40, 256), 0)
    lane = iota((40, 256), 1)
    col = jnp.where(lane < 144, lane, lane - 256)
    col_ids = lax.axis_index("gy") * 128 + col
    inside = (row_ids >= 0) & (row_ids < lax.axis_size("gx") * 8)
    inside = inside & (col_ids >= 0) & (col_ids < lax.axis_size("gy") * 128) & (col >= -16)
    inside_f = jnp.where(inside, 1.0, 0.0)
    inner = inside_f[8:32]
    inner_b = inner > 0.5
    bias = bias_ref[0]

    even_col = (lax.axis_index("gy") & 1) == 0
    from_left = jnp.where(even_col, got_b_ref[...], got_a_ref[...])
    from_right = jnp.where(even_col, got_a_ref[...], got_b_ref[...])
    corner = main_ref[4]
    lane40 = iota((40, 128), 1)
    lane24 = lane40[:24]
    e0, q0, slope, probs, labels = [], [], [], [], []
    for z in range(4):
        to_zero, to_last = (128 - 16 * z) % 128, 112 - 16 * z
        left_zero, left_last = pltpu.roll(from_left, to_zero, 1), pltpu.roll(from_left, to_last, 1)
        right_zero, right_last = pltpu.roll(from_right, to_zero, 1), pltpu.roll(from_right, to_last, 1)
        main = main_ref[z]
        main = main + jnp.where(lane40 == 0, left_zero, jnp.where(lane40 == 127, right_last, 0.0))
        tail = jnp.where(lane40 >= 112, left_last, jnp.where(lane40 < 16, right_zero, 0.0))
        own_zero, own_last = pltpu.roll(corner, to_zero, 1), pltpu.roll(corner, to_last, 1)
        tail = tail + jnp.where(lane40 == 0, own_zero, jnp.where(lane40 == 127, own_last, 0.0))
        lab_left = pltpu.roll(from_left[:24], 48 - 16 * z, 1)
        lab_right = pltpu.roll(from_right[:24], 64 - 16 * z, 1)
        lab_tail = jnp.where(lane24 >= 112, lab_left, jnp.where(lane24 < 16, lab_right, 0.0))
        logits = jnp.concatenate([main, tail], axis=1) + bias
        small = jnp.exp(-jnp.abs(logits))
        scale = inverse(1.0 + small)
        prob = jnp.where(logits >= 0.0, scale, small * scale)
        prob = jnp.where(inside, prob, 0.0)
        e = jnp.exp(-SHARP * prob)
        e0.append(e)
        q0.append(inverse(e))
        weight = (small * scale) * scale
        slope.append(((-SHARP) * e * weight)[8:32] * inner)
        probs.append((prob[8:32], weight[8:32]))
        labels.append(jnp.concatenate([lab_ref[z], lab_tail], axis=1))

    low, high = jnp.exp(-SHARP * jnp.ones((24, 256), F32)), jnp.exp(SHARP * jnp.ones((24, 256), F32))
    true_state = (
        [jnp.where(x > 0.5, low, 1.0) for x in labels],
        [jnp.where(x > 0.5, high, 1.0) for x in labels],
        None,
    )

    def keep(i, z, qz, d_inv, ratio, change, rest, power):
        qs_ref[i, z] = qz
        ds_ref[i, z] = d_inv
        part = (-2.0 * SOFT) * (ratio * inverse(1.0 + ratio))
        if i > 0:
            share = power * inverse(1.0 + power)
            part = part * (share * rest)
            gain_ref[i, z] = 1.0 - share * change
        rs_ref[i, z] = part

    pred_state = (e0, q0, None)
    for i in range(ITERS + 1):
        true_state = forward_step(i, true_state, inner_b, False, lambda *factors: None)
        pred_state = forward_step(i, pred_state, inside, True, keep)
    true_skel = true_state[2]
    q_last, pred_skel = pred_state[1], pred_state[2]

    def own(x):
        return x[8:16, :128]

    def total(values):
        acc = values[0] + values[1] + values[2] + values[3]
        return jnp.sum(jnp.sum(acc, axis=1, keepdims=True), axis=0, keepdims=True)

    t0 = total([own(pred_skel[z] * labels[z]) for z in range(4)])
    t1 = total([own(pred_skel[z]) for z in range(4)])
    t2 = total([own(true_skel[z] * probs[z][0]) for z in range(4)])
    t3 = total([own(true_skel[z]) for z in range(4)])

    weights = [labels, [inner] * 4]
    running = [jnp.ones((24, 256), F32)] * 4
    deep = [None, None]
    for i in range(ITERS, -1, -1):
        coefs = []
        for z in range(4):
            coefs.append(rs_ref[i, z] * running[z])
            if i > 0:
                running[z] = running[z] * gain_ref[i, z]
        for f in range(2):
            scaled = [coefs[z] * weights[f][z] for z in range(4)]
            spread = box([scaled[z] * ds_ref[i, z] for z in range(4)], 0.0, False)
            q_of = [q_last[z][8:32] if i == ITERS else qs_ref[i + 1, z] for z in range(4)]
            incoming = []
            for z in range(4):
                value = spread[z] * (q_of[z] * q_of[z]) * (-1.0 / 27.0)
                if deep[f] is not None:
                    value = value + deep[f][z]
                incoming.append(value * inner)
            moved = cross(incoming, 0.0)
            deep[f] = [moved[z] + scaled[z] * qs_ref[i, z] for z in range(4)]
    fields = [
        [deep[0][z] * slope[z] for z in range(4)],
        [deep[1][z] * slope[z] for z in range(4)],
        [true_skel[z] * probs[z][1] * inner for z in range(4)],
    ]
    bias_sums = [total([own(x) for x in field]) for field in fields]

    sub = iota((8, 256), 0)
    stacks = []
    for z in range(4):
        pieces = []
        for f in range(3):
            x = fields[f][z]
            edge = jnp.where(sub == 0, x[16:24], jnp.where(sub == 7, x[0:8], 0.0))
            block = jnp.concatenate([x[8:16], edge], axis=0)
            grad_ref[f, z] = block
            for d in range(3):
                moved = (shift_cols(block, d - 1) if d != 1 else block)[:, :128]
                upper = moved.astype(BF16)
                lower = (moved - upper.astype(F32)).astype(BF16)
                pieces += [upper, lower]
        stacks.append(jnp.concatenate(pieces, axis=0))
    offset = (iota((16, 256), 1) & 7) - edge_row(iota((16, 256), 0)) + 1
    picked = {}
    for a in range(3):
        moments = jnp.zeros((288, 256), F32)
        for z in range(4):
            if 0 <= z + a - 1 < 4:
                feats = f_ref[:, z + a - 1].reshape(256, 128)
                moments = moments + dot(stacks[z], feats, ((1,), (1,)))
        for f in range(3):
            for d in range(3):
                start = (f * 3 + d) * 32
                pair = moments[start : start + 16] + moments[start + 16 : start + 32]
                for b in range(3):
                    chosen = jnp.where(offset == b, pair, 0.0)
                    picked[b, f, a, d] = jnp.sum(chosen, axis=0, keepdims=True)
    order = [(f, a, d) for f in range(3) for a in range(3) for d in range(3)]
    groups = [[picked[(b,) + at] for at in order[:24]] for b in range(3)]
    rest = [picked[(b,) + at] for b in range(3) for at in order[24:]]
    groups.append(rest + [jnp.zeros((15, 256), F32)])
    stacked = jnp.concatenate([row for rows in groups for row in rows], axis=0)
    high = stacked.astype(BF16)
    left_over = stacked - high.astype(F32)
    middle = left_over.astype(BF16)
    low = (left_over - middle.astype(F32)).astype(BF16)
    collect = jnp.where((iota((256, 128), 0) >> 3) == iota((256, 128), 1), 1.0, 0.0).astype(BF16)
    summed = dot(jnp.concatenate([high, middle, low], axis=0), collect, ((1,), (0,)))
    summed = summed[:96] + summed[96:192] + summed[192:]
    result = summed[:24]
    for b in range(1, 4):
        result = result + pltpu.roll(summed[24 * b : 24 * b + 24], 32 * b, 1)
    row24, lane_of = iota((24, 128), 0), iota((24, 128), 1)
    for k, value in enumerate([t0, t1, t2, t3] + bias_sums):
        result = jnp.where(((row24 == 11) | (row24 == 23)) & (lane_of == 96 + k), value, result)
    keep_ref[...] = jnp.where(even_col, result[:12], result[12:])
    send_ref[...] = jnp.where(even_col, result[12:], result[:12])


def pair_kernel(own_ref, got_ref, out_ref):
    out_ref[...] = own_ref[...] + got_ref[...]


def four_kernel(own_ref, one_ref, two_ref, three_ref, out_ref):
    half = (own_ref[...] + one_ref[...]) + (two_ref[...] + three_ref[...])
    for n in range(out_ref.shape[0]):
        out_ref[n] = half[4 * (n % 3) : 4 * (n % 3) + 4]


def add_kernel(in_ref, out_ref):
    for part in range(3):
        acc = in_ref[part]
        for n in range(part + 3, in_ref.shape[0], 3):
            acc = acc + in_ref[n]
        out_ref[part] = acc


def loss_and_slopes(row):
    sums = [row[:, 96 + k : 97 + k] for k in range(7)]
    precision = (sums[0] + 1.0) / (sums[1] + 1.0)
    sensitivity = (sums[2] + 1.0) / (sums[3] + 1.0)
    both = precision + sensitivity
    loss = 1.0 - 2.0 * precision * sensitivity / both
    by_precision = -2.0 * (sensitivity / both) * (sensitivity / both)
    by_sensitivity = -2.0 * (precision / both) * (precision / both)
    slopes = [
        by_precision / (sums[1] + 1.0),
        -by_precision * precision / (sums[1] + 1.0),
        by_sensitivity / (sums[3] + 1.0),
    ]
    return loss, slopes, sums[4:]


def weight_kernel(
    own_ref, got_ref, feature_ref,
    loss_out_ref, weight_out_ref, bias_out_ref, feature_out_ref,
    loss_ref, weight_ref, bias_ref, sems,
):
    pairs = [
        (feature_ref, feature_out_ref), (loss_ref, loss_out_ref),
        (bias_ref, bias_out_ref), (weight_ref, weight_out_ref),
    ]
    copies = [pltpu.make_async_copy(x, y, sems.at[n]) for n, (x, y) in enumerate(pairs)]
    copies[0].start()
    even = (lax.axis_index("gy") & 1) == 0
    own, got = own_ref[...], got_ref[...]
    first, second = jnp.where(even, own, got), jnp.where(even, got, own)
    acc = jnp.concatenate([x[part] for x in (first, second) for part in range(3)], axis=0)
    loss, slopes, bias_sums = loss_and_slopes(acc[11:12])
    loss_ref[...] = loss
    bias_ref[...] = sum(slopes[f] * bias_sums[f] for f in range(3))
    copies[1].start()
    copies[2].start()
    group = iota((3, 128), 1) >> 5
    last = acc[18:21]
    for b in range(3):
        last = jnp.where(group == b, pltpu.roll(acc[3 * b : 3 * b + 3], (32 * b + 32) % 128, 1), last)
    third = jnp.concatenate([acc[18:24], last], axis=0)
    weight = slopes[0] * acc[0:9] + slopes[1] * acc[9:18] + slopes[2] * third
    for b in range(3):
        part = weight if b == 0 else pltpu.roll(weight, 128 - 32 * b, 1)
        for a in range(3):
            weight_ref[9 * a + 3 * b : 9 * a + 3 * b + 3] = part[3 * a : 3 * a + 3, :32]
    copies[3].start()
    for copy in copies:
        copy.wait()


def feature_kernel(sums_ref, grad_ref, a_ref, out_ref, *, voxels):
    _, slopes, _ = loss_and_slopes(sums_ref[2, 3:4])
    matrix = a_ref[...]
    parts = []
    for z in range(4):
        block = slopes[0] * grad_ref[0, z] + slopes[1] * grad_ref[1, z] + slopes[2] * grad_ref[2, z]
        block = block * voxels
        byd = []
        for d in range(3):
            moved = (shift_cols(block, d - 1) if d != 1 else block)[:, :128]
            upper = moved.astype(BF16)
            byd.append((upper, (moved - upper.astype(F32)).astype(BF16)))
        parts.append(byd)
    none = jnp.zeros((16, 128), BF16)
    for z in range(4):
        acc_z = None
        for level in range(2):
            stack = []
            for a in range(3):
                for d in range(3):
                    at = z - a + 1
                    stack.append(parts[at][d][level] if 0 <= at < 4 else none)
            term = dot(matrix, jnp.concatenate(stack, axis=0), ((0,), (0,)))
            acc_z = term if acc_z is None else acc_z + term
        out_ref[:, z] = acc_z.reshape(32, 8, 128).astype(BF16)


def call(kernel, out_shapes, *args, scratch=(), spaces={}, out_spaces={}):
    in_specs = [pl.BlockSpec(memory_space=spaces.get(n, pltpu.VMEM)) for n in range(len(args))]
    return pl.pallas_call(
        kernel,
        out_shape=[jax.ShapeDtypeStruct(shape, dtype) for shape, dtype in out_shapes],
        in_specs=in_specs,
        out_specs=[
            pl.BlockSpec(memory_space=out_spaces.get(n, pltpu.VMEM)) for n in range(len(out_shapes))
        ],
        scratch_shapes=list(scratch),
        compiler_params=pltpu.CompilerParams(vmem_limit_bytes=VMEM_LIMIT),
    )(*args)


def swapped(x, axis, step, phase):
    count = lax.axis_size(axis)
    pairs = []
    for n in range(count - step):
        if (n // step) % 2 == phase:
            pairs += [(n, n + step), (n + step, n)]
    return lax.ppermute(x, axis, pairs)


def local(features, vessel_label, conv_weight, conv_bias):
    gx, gy = lax.axis_size("gx"), lax.axis_size("gy")
    voxels = float(4 * 8 * gx * 128 * gy)
    matrix, near, far, features = call(
        partial_logits_kernel,
        [((144, 256), BF16), ((80, 128), F32), ((88, 128), F32), (features.shape, BF16)],
        *[pltpu.with_memory_space_constraint(x, pltpu.HBM) for x in (conv_weight, features, vessel_label)],
        scratch=[
            pltpu.VMEM((27, 32), BF16),
            pltpu.VMEM((4, 8, 128), jnp.int32),
            pltpu.SemaphoreType.DMA((3,)),
        ],
        spaces={0: pltpu.HBM, 1: pltpu.HBM, 2: pltpu.HBM},
    )
    two = [swapped(far, "gx", 2, phase) for phase in range(2)]
    one = [swapped(near, "gx", 1, phase) for phase in range(2)]
    main, labels, send_a, send_b = call(
        rows_kernel,
        [((5, 40, 128), F32), ((4, 24, 128), F32), ((40, 128), F32), ((40, 128), F32)],
        near, *two[::-1], *one[::-1],
    )
    got_b = swapped(send_b, "gy", 1, 1)
    got_a = swapped(send_a, "gy", 1, 0)
    field = pltpu.VMEM((ITERS + 1, 4, 24, 256), F32)
    grads, keep, send = call(
        skeleton_kernel,
        [((3, 4, 16, 256), F32), ((12, 128), F32), ((12, 128), F32)],
        conv_bias, features, main, labels, got_b, got_a,
        scratch=[field] * 4, spaces={0: pltpu.SMEM},
    )
    half = call(pair_kernel, [((12, 128), F32)], keep, swapped(send, "gy", 1, 0))[0]
    others = [lax.ppermute(half, "gy", [(n, n ^ mask) for n in range(gy)]) for mask in (2, 4, 6)]
    sums = call(four_kernel, [((3 * gx, 4, 128), F32)], half, *others)[0]
    sums = lax.all_to_all(sums, "gx", 0, 0, tiled=True)
    sums = call(add_kernel, [((3, 4, 128), F32)], sums)[0]
    other = swapped(sums, "gy", 1, 0)

    def feature_part(*refs):
        feature_kernel(*refs, voxels=voxels)

    feature_grad = call(feature_part, [((32, 4, 8, 128), BF16)], sums, grads, matrix)[0]
    loss, weight_grad, bias_grad, feature_grad = call(
        weight_kernel,
        [((1, 1), F32), ((27, 32), F32), ((1, 1), F32), ((32, 4, 8, 128), BF16)],
        sums, other, feature_grad,
        scratch=[
            pltpu.VMEM((1, 1), F32),
            pltpu.VMEM((27, 32), F32),
            pltpu.VMEM((1, 1), F32),
            pltpu.SemaphoreType.DMA((4,)),
        ],
        out_spaces={n: pltpu.HBM for n in range(4)},
    )
    return (loss.reshape(()), weight_grad, bias_grad.reshape((1,)), feature_grad)


def solution(mesh):
    in_specs = (P(None, None, "gx", "gy"), P(None, "gx", "gy"), P(), P())
    out_specs = (P(), P(), P(), P(None, None, "gx", "gy"))
    return jax.shard_map(local, mesh=mesh, in_specs=in_specs, out_specs=out_specs, check_vma=False)
```

```python
import jax
import jax.numpy as jnp
from jax import lax
from jax.experimental import pallas as pl
from jax.experimental.pallas import tpu as pltpu
from jax.sharding import PartitionSpec as P

ITERS = 5
F32 = jnp.float32
BF16 = jnp.bfloat16
SHARP = 10.0
SOFT = 0.05
EDGE = 16
VMEM_LIMIT = 24 * 1024 * 1024


def iota(shape, dim):
    return lax.broadcasted_iota(jnp.int32, shape, dim)


def dot(a, b, dims, precision=None):
    return lax.dot_general(a, b, (dims, ((), ())), precision=precision, preferred_element_type=F32)


def edge_row(q):
    return jnp.where(q < 8, q, jnp.where(q == 8, 8, jnp.where(q == 15, -1, -100)))


def weight_matrix(w):
    spread = jnp.where((iota((32, 256), 1) >> 3) == iota((32, 256), 0), 1.0, 0.0).astype(BF16)
    by_lane = dot(w, spread, ((1,), (0,))).astype(BF16)
    row = iota((144, 27), 0)
    ad = row >> 4
    base = ad + 6 * (jnp.where(ad >= 3, 1, 0) + jnp.where(ad >= 6, 1, 0))
    col = iota((144, 27), 1)
    offset = (iota((144, 256), 1) & 7) - edge_row(iota((144, 256), 0) & 15) + 1
    matrix = jnp.zeros((144, 256), F32)
    for b in range(3):
        pick = jnp.where(col == base + 3 * b, 1.0, 0.0).astype(BF16)
        matrix = matrix + jnp.where(offset == b, dot(pick, by_lane, ((1,), (0,))), 0.0)
    return matrix.astype(BF16)


def turned(x, s):
    return x if s == 0 else pltpu.roll(x, s % x.shape[0], 0)


def at_end(lane):
    return ((lane & 15) == 0) | ((lane & 15) == 15)


def partial_logits_kernel(
    w_hbm, f_hbm, lab_hbm, a_ref, near_ref, far_ref, f_ref, w_ref, lab_ref, sems
):
    pairs = [(w_hbm, w_ref), (f_hbm, f_ref), (lab_hbm, lab_ref)]
    copies = [pltpu.make_async_copy(x, y, sems.at[n]) for n, (x, y) in enumerate(pairs)]
    for copy in copies:
        copy.start()
    copies[0].wait()
    matrix = weight_matrix(w_ref[...])
    a_ref[...] = matrix
    copies[1].wait()
    lane = iota((16, 128), 1)
    sub = iota((8, 128), 0)
    terms = [
        dot(matrix, f_ref[:, z].reshape(256, 128), ((1,), (0,))).reshape(3, 3, 16, 128)
        for z in range(4)
    ]
    corner = jnp.zeros((16, 128), F32)
    edges = jnp.zeros((8, 128), F32)
    for z in range(4):
        byd = []
        for d in range(3):
            byd.append(sum(terms[z + a - 1][a, d] for a in range(3) if 0 <= z + a - 1 < 4))
        main = byd[1]
        main = main + jnp.where(lane >= 1, pltpu.roll(byd[0], 1, 1), 0.0)
        main = main + jnp.where(lane <= 126, pltpu.roll(byd[2], 127, 1), 0.0)
        near_ref[8 * z : 8 * z + 8] = main[:8]
        far_ref[8 * z : 8 * z + 8] = main[:8]
        edges = jnp.where(sub == z, turned(main[8:], z), edges)
        edges = jnp.where(sub == 7 - z, turned(main[8:], -z), edges)
        low, high = 16 * z, 16 * z + 15
        corner = jnp.where(lane == low, pltpu.roll(byd[0], low + 1, 1), corner)
        corner = jnp.where(lane == high, pltpu.roll(byd[2], high, 1), corner)
    corners = jnp.where(at_end(lane[:8]), corner[:8], pltpu.roll(corner[8:], 2, 1))
    near_ref[32:40] = edges
    far_ref[32:40] = edges
    near_ref[40:48] = corners
    far_ref[40:48] = corners
    far_ref[48:88] = jnp.zeros((40, 128), F32)
    copies[2].wait()
    near_ref[48:80] = lab_ref[...].reshape(32, 128).astype(F32)


def rows_kernel(
    own_ref, two_b_ref, two_a_ref, one_b_ref, one_a_ref, main_ref, lab_ref, send_a_ref, send_b_ref
):
    row_block, col_block = lax.axis_index("gx"), lax.axis_index("gy")
    even1 = (row_block & 1) == 0
    even2 = (row_block & 2) == 0
    even_col = (col_block & 1) == 0
    own = own_ref[...]
    one_a, one_b, two_a, two_b = one_a_ref[...], one_b_ref[...], two_a_ref[...], two_b_ref[...]
    before, after = jnp.where(even1, one_b, one_a), jnp.where(even1, one_a, one_b)
    two_a, two_b = two_a[:48], two_b[:48]
    blocks = [jnp.where(even2, two_b, two_a), before, own, after, jnp.where(even2, two_a, two_b)]
    sub = iota((8, 128), 0)
    ends = at_end(iota((8, 128), 1))

    def assemble(tiles, firsts, lasts):
        result = []
        for t in range(5):
            tile = tiles[t]
            if t > 0:
                tile = tile + jnp.where(sub == 0, firsts[t - 1], 0.0)
            if t < 4:
                tile = tile + jnp.where(sub == 7, lasts[t + 1], 0.0)
            result.append(tile)
        return jnp.concatenate(result, axis=0)

    corners = [jnp.where(ends, x[40:48], 0.0) for x in blocks]
    beyond = [jnp.where(ends, pltpu.roll(x[40:48], 126, 1), 0.0) for x in blocks]
    corner = assemble(corners, beyond, beyond)
    main_ref[4] = corner
    lane = iota((40, 128), 1)
    right = jnp.zeros((40, 128), F32)
    left = jnp.zeros((40, 128), F32)
    for z in range(4):
        main = assemble(
            [x[8 * z : 8 * z + 8] for x in blocks],
            [turned(x[32:40], -z) for x in blocks],
            [turned(x[32:40], z) for x in blocks],
        )
        main_ref[z] = main
        lab = jnp.concatenate([x[48 + 8 * z : 56 + 8 * z] for x in (before, own, after)], axis=0)
        lab_ref[z] = lab
        lab = jnp.concatenate([lab, jnp.zeros((16, 128), F32)], axis=0)
        right = jnp.where((lane >> 4) == z, pltpu.roll(main, 16 * z + 16, 1), right)
        right = jnp.where((lane >> 4) == z + 4, pltpu.roll(lab, (16 * z + 80) % 128, 1), right)
        left = jnp.where((lane >> 4) == z, pltpu.roll(main, 16 * z, 1), left)
        left = jnp.where((lane >> 4) == z + 4, pltpu.roll(lab, 16 * z + 64, 1), left)
    right = jnp.where((lane < 64) & ((lane & 15) == 0), corner, right)
    left = jnp.where((lane < 64) & ((lane & 15) == 15), corner, left)
    send_a_ref[...] = jnp.where(even_col, right, left)
    send_b_ref[...] = jnp.where(even_col, left, right)


def shift_rows(x, s):
    return pltpu.roll(x, s % x.shape[0], 0)


def shift_cols(x, s):
    return pltpu.roll(x, s % x.shape[1], 1)


def cross(fields, outside):
    result = []
    for z in range(4):
        x = fields[z]
        around = shift_rows(x, 1) + shift_rows(x, -1) + shift_cols(x, 1) + shift_cols(x, -1)
        before = fields[z - 1] if z > 0 else outside
        after = fields[z + 1] if z < 3 else outside
        result.append((around + (before + after)) * (1.0 / 9.0) + x * (1.0 / 3.0))
    return result


def box(fields, outside, crop):
    result = []
    for z in range(4):
        before = fields[z - 1] if z > 0 else outside
        after = fields[z + 1] if z < 3 else outside
        x = fields[z] + (before + after)
        x = x + shift_rows(x, 1) + shift_rows(x, -1)
        if crop:
            x = x[8:32]
        result.append(x + shift_cols(x, 1) + shift_cols(x, -1))
    return result


def inverse(x):
    return 1.0 / x


def forward_step(i, state, inside, crop, keep):
    def middle(x):
        return x[8:32] if crop else x

    e, q, s = state
    e = [jnp.where(inside, x, 1.0) for x in cross(e, 1.0)]
    q_next = [inverse(x) for x in e]
    mean = box(q_next, 1.0, crop)
    s_next = []
    for z in range(4):
        d_inv = inverse(mean[z])
        qz = middle(q[z])
        ratio = (27.0 * qz) * d_inv
        ratio = ratio * ratio
        log_term = jnp.log(1.0 + ratio)
        change = SOFT * log_term
        if i == 0:
            s_next.append(change)
            keep(i, z, qz, d_inv, ratio, None, None, None)
        else:
            rest = 1.0 - s[z]
            power = jnp.exp(log_term * rest)
            s_next.append(s[z] + SOFT * jnp.log(1.0 + power))
            keep(i, z, qz, d_inv, ratio, change, rest, power)
    return e, q_next, s_next


def skeleton_kernel(
    bias_ref, f_ref, main_ref, lab_ref, got_b_ref, got_a_ref,
    grad_ref, keep_ref, send_ref,
    qs_ref, ds_ref, rs_ref, gain_ref,
):
    row_ids = lax.axis_index("gx") * 8 - 16 + iota((40, 256), 0)
    lane = iota((40, 256), 1)
    col = jnp.where(lane < 144, lane, lane - 256)
    col_ids = lax.axis_index("gy") * 128 + col
    inside = (row_ids >= 0) & (row_ids < lax.axis_size("gx") * 8)
    inside = inside & (col_ids >= 0) & (col_ids < lax.axis_size("gy") * 128) & (col >= -16)
    inside_f = jnp.where(inside, 1.0, 0.0)
    inner = inside_f[8:32]
    inner_b = inner > 0.5
    bias = bias_ref[0]

    even_col = (lax.axis_index("gy") & 1) == 0
    from_left = jnp.where(even_col, got_b_ref[...], got_a_ref[...])
    from_right = jnp.where(even_col, got_a_ref[...], got_b_ref[...])
    corner = main_ref[4]
    lane40 = iota((40, 128), 1)
    lane24 = lane40[:24]
    e0, q0, slope, probs, labels = [], [], [], [], []
    for z in range(4):
        to_zero, to_last = (128 - 16 * z) % 128, 112 - 16 * z
        left_zero, left_last = pltpu.roll(from_left, to_zero, 1), pltpu.roll(from_left, to_last, 1)
        right_zero, right_last = pltpu.roll(from_right, to_zero, 1), pltpu.roll(from_right, to_last, 1)
        main = main_ref[z]
        main = main + jnp.where(lane40 == 0, left_zero, jnp.where(lane40 == 127, right_last, 0.0))
        tail = jnp.where(lane40 >= 112, left_last, jnp.where(lane40 < 16, right_zero, 0.0))
        own_zero, own_last = pltpu.roll(corner, to_zero, 1), pltpu.roll(corner, to_last, 1)
        tail = tail + jnp.where(lane40 == 0, own_zero, jnp.where(lane40 == 127, own_last, 0.0))
        lab_left = pltpu.roll(from_left[:24], 48 - 16 * z, 1)
        lab_right = pltpu.roll(from_right[:24], 64 - 16 * z, 1)
        lab_tail = jnp.where(lane24 >= 112, lab_left, jnp.where(lane24 < 16, lab_right, 0.0))
        logits = jnp.concatenate([main, tail], axis=1) + bias
        small = jnp.exp(-jnp.abs(logits))
        scale = inverse(1.0 + small)
        prob = jnp.where(logits >= 0.0, scale, small * scale)
        prob = jnp.where(inside, prob, 0.0)
        e = jnp.exp(-SHARP * prob)
        e0.append(e)
        q0.append(inverse(e))
        weight = (small * scale) * scale
        slope.append(((-SHARP) * e * weight)[8:32] * inner)
        probs.append((prob[8:32], weight[8:32]))
        labels.append(jnp.concatenate([lab_ref[z], lab_tail], axis=1))

    low, high = jnp.exp(-SHARP * jnp.ones((24, 256), F32)), jnp.exp(SHARP * jnp.ones((24, 256), F32))
    true_state = (
        [jnp.where(x > 0.5, low, 1.0) for x in labels],
        [jnp.where(x > 0.5, high, 1.0) for x in labels],
        None,
    )

    def keep(i, z, qz, d_inv, ratio, change, rest, power):
        qs_ref[i, z] = qz
        ds_ref[i, z] = d_inv
        part = (-2.0 * SOFT) * (ratio * inverse(1.0 + ratio))
        if i > 0:
            share = power * inverse(1.0 + power)
            part = part * (share * rest)
            gain_ref[i, z] = 1.0 - share * change
        rs_ref[i, z] = part

    pred_state = (e0, q0, None)
    for i in range(ITERS + 1):
        true_state = forward_step(i, true_state, inner_b, False, lambda *factors: None)
        pred_state = forward_step(i, pred_state, inside, True, keep)
    true_skel = true_state[2]
    q_last, pred_skel = pred_state[1], pred_state[2]

    def own(x):
        return x[8:16, :128]

    def total(values):
        acc = values[0] + values[1] + values[2] + values[3]
        return jnp.sum(jnp.sum(acc, axis=1, keepdims=True), axis=0, keepdims=True)

    t0 = total([own(pred_skel[z] * labels[z]) for z in range(4)])
    t1 = total([own(pred_skel[z]) for z in range(4)])
    t2 = total([own(true_skel[z] * probs[z][0]) for z in range(4)])
    t3 = total([own(true_skel[z]) for z in range(4)])

    weights = [labels, [inner] * 4]
    running = [jnp.ones((24, 256), F32)] * 4
    deep = [None, None]
    for i in range(ITERS, -1, -1):
        coefs = []
        for z in range(4):
            coefs.append(rs_ref[i, z] * running[z])
            if i > 0:
                running[z] = running[z] * gain_ref[i, z]
        q_of = [q_last[z][8:32] if i == ITERS else qs_ref[i + 1, z] for z in range(4)]
        q_of = [(x * x) * inner for x in q_of]
        for f in range(2):
            scaled = [coefs[z] * weights[f][z] for z in range(4)]
            spread = box([scaled[z] * ds_ref[i, z] for z in range(4)], 0.0, False)
            incoming = []
            for z in range(4):
                if deep[f] is None:
                    incoming.append(-(spread[z] * q_of[z]))
                else:
                    incoming.append(deep[f][z] * inner - spread[z] * q_of[z])
            moved = cross(incoming, 0.0)
            deep[f] = [moved[z] + scaled[z] * qs_ref[i, z] for z in range(4)]
    fields = [
        [deep[0][z] * slope[z] for z in range(4)],
        [deep[1][z] * slope[z] for z in range(4)],
        [true_skel[z] * probs[z][1] * inner for z in range(4)],
    ]
    bias_sums = [total([own(x) for x in field]) for field in fields]

    sub = iota((8, 256), 0)
    stacks = []
    for z in range(4):
        pieces = []
        for f in range(3):
            x = fields[f][z]
            edge = jnp.where(sub == 0, x[16:24], jnp.where(sub == 7, x[0:8], 0.0))
            block = jnp.concatenate([x[8:16], edge], axis=0)
            grad_ref[f, z] = block
            for d in range(3):
                moved = (shift_cols(block, d - 1) if d != 1 else block)[:, :128]
                upper = moved.astype(BF16)
                lower = (moved - upper.astype(F32)).astype(BF16)
                pieces += [upper, lower]
        stacks.append(jnp.concatenate(pieces, axis=0))
    offset = (iota((16, 256), 1) & 7) - edge_row(iota((16, 256), 0)) + 1
    picked = {}
    for a in range(3):
        moments = jnp.zeros((288, 256), F32)
        for z in range(4):
            if 0 <= z + a - 1 < 4:
                feats = f_ref[:, z + a - 1].reshape(256, 128)
                moments = moments + dot(stacks[z], feats, ((1,), (1,)))
        for f in range(3):
            for d in range(3):
                start = (f * 3 + d) * 32
                pair = moments[start : start + 16] + moments[start + 16 : start + 32]
                for b in range(3):
                    chosen = jnp.where(offset == b, pair, 0.0)
                    picked[b, f, a, d] = jnp.sum(chosen, axis=0, keepdims=True)
    order = [(f, a, d) for f in range(3) for a in range(3) for d in range(3)]
    groups = [[picked[(b,) + at] for at in order[:24]] for b in range(3)]
    rest = [picked[(b,) + at] for b in range(3) for at in order[24:]]
    groups.append(rest + [jnp.zeros((15, 256), F32)])
    stacked = jnp.concatenate([row for rows in groups for row in rows], axis=0)
    high = stacked.astype(BF16)
    left_over = stacked - high.astype(F32)
    middle = left_over.astype(BF16)
    low = (left_over - middle.astype(F32)).astype(BF16)
    collect = jnp.where((iota((256, 128), 0) >> 3) == iota((256, 128), 1), 1.0, 0.0).astype(BF16)
    summed = dot(jnp.concatenate([high, middle, low], axis=0), collect, ((1,), (0,)))
    summed = summed[:96] + summed[96:192] + summed[192:]
    result = summed[:24]
    for b in range(1, 4):
        result = result + pltpu.roll(summed[24 * b : 24 * b + 24], 32 * b, 1)
    row24, lane_of = iota((24, 128), 0), iota((24, 128), 1)
    for k, value in enumerate([t0, t1, t2, t3] + bias_sums):
        result = jnp.where(((row24 == 11) | (row24 == 23)) & (lane_of == 96 + k), value, result)
    keep_ref[...] = jnp.where(even_col, result[:12], result[12:])
    send_ref[...] = jnp.where(even_col, result[12:], result[:12])


def pair_kernel(own_ref, got_ref, out_ref):
    out_ref[...] = own_ref[...] + got_ref[...]


def four_kernel(own_ref, one_ref, two_ref, three_ref, out_ref):
    half = (own_ref[...] + one_ref[...]) + (two_ref[...] + three_ref[...])
    for n in range(out_ref.shape[0]):
        out_ref[n] = half[4 * (n % 3) : 4 * (n % 3) + 4]


def add_kernel(in_ref, out_ref):
    for part in range(3):
        acc = in_ref[part]
        for n in range(part + 3, in_ref.shape[0], 3):
            acc = acc + in_ref[n]
        out_ref[part] = acc


def loss_and_slopes(row):
    sums = [row[:, 96 + k : 97 + k] for k in range(7)]
    precision = (sums[0] + 1.0) / (sums[1] + 1.0)
    sensitivity = (sums[2] + 1.0) / (sums[3] + 1.0)
    both = precision + sensitivity
    loss = 1.0 - 2.0 * precision * sensitivity / both
    by_precision = -2.0 * (sensitivity / both) * (sensitivity / both)
    by_sensitivity = -2.0 * (precision / both) * (precision / both)
    slopes = [
        by_precision / (sums[1] + 1.0),
        -by_precision * precision / (sums[1] + 1.0),
        by_sensitivity / (sums[3] + 1.0),
    ]
    return loss, slopes, sums[4:]


def weight_kernel(
    own_ref, got_ref, feature_ref,
    loss_out_ref, weight_out_ref, bias_out_ref, feature_out_ref,
    loss_ref, weight_ref, bias_ref, sems,
):
    pairs = [
        (feature_ref, feature_out_ref), (loss_ref, loss_out_ref),
        (bias_ref, bias_out_ref), (weight_ref, weight_out_ref),
    ]
    copies = [pltpu.make_async_copy(x, y, sems.at[n]) for n, (x, y) in enumerate(pairs)]
    copies[0].start()
    even = (lax.axis_index("gy") & 1) == 0
    own, got = own_ref[...], got_ref[...]
    first, second = jnp.where(even, own, got), jnp.where(even, got, own)
    acc = jnp.concatenate([x[part] for x in (first, second) for part in range(3)], axis=0)
    loss, slopes, bias_sums = loss_and_slopes(acc[11:12])
    loss_ref[...] = loss
    bias_ref[...] = sum(slopes[f] * bias_sums[f] for f in range(3))
    copies[1].start()
    copies[2].start()
    group = iota((3, 128), 1) >> 5
    last = acc[18:21]
    for b in range(3):
        last = jnp.where(group == b, pltpu.roll(acc[3 * b : 3 * b + 3], (32 * b + 32) % 128, 1), last)
    third = jnp.concatenate([acc[18:24], last], axis=0)
    weight = slopes[0] * acc[0:9] + slopes[1] * acc[9:18] + slopes[2] * third
    for b in range(3):
        part = weight if b == 0 else pltpu.roll(weight, 128 - 32 * b, 1)
        for a in range(3):
            weight_ref[9 * a + 3 * b : 9 * a + 3 * b + 3] = part[3 * a : 3 * a + 3, :32]
    copies[3].start()
    for copy in copies:
        copy.wait()


def feature_kernel(sums_ref, grad_ref, a_ref, out_ref, *, voxels):
    _, slopes, _ = loss_and_slopes(sums_ref[2, 3:4])
    matrix = a_ref[...]
    parts = []
    for z in range(4):
        block = slopes[0] * grad_ref[0, z] + slopes[1] * grad_ref[1, z] + slopes[2] * grad_ref[2, z]
        block = block * voxels
        byd = []
        for d in range(3):
            moved = (shift_cols(block, d - 1) if d != 1 else block)[:, :128]
            upper = moved.astype(BF16)
            byd.append((upper, (moved - upper.astype(F32)).astype(BF16)))
        parts.append(byd)
    none = jnp.zeros((16, 128), BF16)
    for z in range(4):
        acc_z = None
        for level in range(2):
            stack = []
            for a in range(3):
                for d in range(3):
                    at = z - a + 1
                    stack.append(parts[at][d][level] if 0 <= at < 4 else none)
            term = dot(matrix, jnp.concatenate(stack, axis=0), ((0,), (0,)))
            acc_z = term if acc_z is None else acc_z + term
        out_ref[:, z] = acc_z.reshape(32, 8, 128).astype(BF16)


def call(kernel, out_shapes, *args, scratch=(), spaces={}, out_spaces={}):
    in_specs = [pl.BlockSpec(memory_space=spaces.get(n, pltpu.VMEM)) for n in range(len(args))]
    return pl.pallas_call(
        kernel,
        out_shape=[jax.ShapeDtypeStruct(shape, dtype) for shape, dtype in out_shapes],
        in_specs=in_specs,
        out_specs=[
            pl.BlockSpec(memory_space=out_spaces.get(n, pltpu.VMEM)) for n in range(len(out_shapes))
        ],
        scratch_shapes=list(scratch),
        compiler_params=pltpu.CompilerParams(vmem_limit_bytes=VMEM_LIMIT),
    )(*args)


def swapped(x, axis, step, phase):
    count = lax.axis_size(axis)
    pairs = []
    for n in range(count - step):
        if (n // step) % 2 == phase:
            pairs += [(n, n + step), (n + step, n)]
    return lax.ppermute(x, axis, pairs)


def local(features, vessel_label, conv_weight, conv_bias):
    gx, gy = lax.axis_size("gx"), lax.axis_size("gy")
    voxels = float(4 * 8 * gx * 128 * gy)
    matrix, near, far, features = call(
        partial_logits_kernel,
        [((144, 256), BF16), ((80, 128), F32), ((88, 128), F32), (features.shape, BF16)],
        *[pltpu.with_memory_space_constraint(x, pltpu.HBM) for x in (conv_weight, features, vessel_label)],
        scratch=[
            pltpu.VMEM((27, 32), BF16),
            pltpu.VMEM((4, 8, 128), jnp.int32),
            pltpu.SemaphoreType.DMA((3,)),
        ],
        spaces={0: pltpu.HBM, 1: pltpu.HBM, 2: pltpu.HBM},
    )
    two = [swapped(far, "gx", 2, phase) for phase in range(2)]
    one = [swapped(near, "gx", 1, phase) for phase in range(2)]
    main, labels, send_a, send_b = call(
        rows_kernel,
        [((5, 40, 128), F32), ((4, 24, 128), F32), ((40, 128), F32), ((40, 128), F32)],
        near, *two[::-1], *one[::-1],
    )
    got_b = swapped(send_b, "gy", 1, 1)
    got_a = swapped(send_a, "gy", 1, 0)
    field = pltpu.VMEM((ITERS + 1, 4, 24, 256), F32)
    grads, keep, send = call(
        skeleton_kernel,
        [((3, 4, 16, 256), F32), ((12, 128), F32), ((12, 128), F32)],
        conv_bias, features, main, labels, got_b, got_a,
        scratch=[field] * 4, spaces={0: pltpu.SMEM},
    )
    half = call(pair_kernel, [((12, 128), F32)], keep, swapped(send, "gy", 1, 0))[0]
    others = [lax.ppermute(half, "gy", [(n, n ^ mask) for n in range(gy)]) for mask in (2, 4, 6)]
    sums = call(four_kernel, [((3 * gx, 4, 128), F32)], half, *others)[0]
    sums = lax.all_to_all(sums, "gx", 0, 0, tiled=True)
    sums = call(add_kernel, [((3, 4, 128), F32)], sums)[0]
    other = swapped(sums, "gy", 1, 0)

    def feature_part(*refs):
        feature_kernel(*refs, voxels=voxels)

    feature_grad = call(feature_part, [((32, 4, 8, 128), BF16)], sums, grads, matrix)[0]
    loss, weight_grad, bias_grad, feature_grad = call(
        weight_kernel,
        [((1, 1), F32), ((27, 32), F32), ((1, 1), F32), ((32, 4, 8, 128), BF16)],
        sums, other, feature_grad,
        scratch=[
            pltpu.VMEM((1, 1), F32),
            pltpu.VMEM((27, 32), F32),
            pltpu.VMEM((1, 1), F32),
            pltpu.SemaphoreType.DMA((4,)),
        ],
        out_spaces={n: pltpu.HBM for n in range(4)},
    )
    return (loss.reshape(()), weight_grad, bias_grad.reshape((1,)), feature_grad)


def solution(mesh):
    in_specs = (P(None, None, "gx", "gy"), P(None, "gx", "gy"), P(), P())
    out_specs = (P(), P(), P(), P(None, None, "gx", "gy"))
    return jax.shard_map(local, mesh=mesh, in_specs=in_specs, out_specs=out_specs, check_vma=False)
```

```python
import jax
import jax.numpy as jnp
from jax import lax
from jax.experimental import pallas as pl
from jax.experimental.pallas import tpu as pltpu
from jax.sharding import PartitionSpec as P

ITERS = 5
F32 = jnp.float32
BF16 = jnp.bfloat16
SHARP = 10.0
SOFT = 0.05
EDGE = 16
VMEM_LIMIT = 24 * 1024 * 1024


def iota(shape, dim):
    return lax.broadcasted_iota(jnp.int32, shape, dim)


def dot(a, b, dims, precision=None):
    return lax.dot_general(a, b, (dims, ((), ())), precision=precision, preferred_element_type=F32)


def edge_row(q):
    return jnp.where(q < 8, q, jnp.where(q == 8, 8, jnp.where(q == 15, -1, -100)))


def weight_matrix(w):
    spread = jnp.where((iota((32, 256), 1) >> 3) == iota((32, 256), 0), 1.0, 0.0).astype(BF16)
    by_lane = dot(w, spread, ((1,), (0,))).astype(BF16)
    row = iota((144, 27), 0)
    ad = row >> 4
    base = ad + 6 * (jnp.where(ad >= 3, 1, 0) + jnp.where(ad >= 6, 1, 0))
    col = iota((144, 27), 1)
    offset = (iota((144, 256), 1) & 7) - edge_row(iota((144, 256), 0) & 15) + 1
    matrix = jnp.zeros((144, 256), F32)
    for b in range(3):
        pick = jnp.where(col == base + 3 * b, 1.0, 0.0).astype(BF16)
        matrix = matrix + jnp.where(offset == b, dot(pick, by_lane, ((1,), (0,))), 0.0)
    return matrix.astype(BF16)


def turned(x, s):
    return x if s == 0 else pltpu.roll(x, s % x.shape[0], 0)


def at_end(lane):
    return ((lane & 15) == 0) | ((lane & 15) == 15)


def partial_logits_kernel(
    w_hbm, f_hbm, lab_hbm, a_ref, near_ref, far_ref, f_ref, w_ref, lab_ref, sems
):
    pairs = [(w_hbm, w_ref), (f_hbm, f_ref), (lab_hbm, lab_ref)]
    copies = [pltpu.make_async_copy(x, y, sems.at[n]) for n, (x, y) in enumerate(pairs)]
    for copy in copies:
        copy.start()
    copies[0].wait()
    matrix = weight_matrix(w_ref[...])
    a_ref[...] = matrix
    copies[1].wait()
    lane = iota((16, 128), 1)
    sub = iota((8, 128), 0)
    terms = [
        dot(matrix, f_ref[:, z].reshape(256, 128), ((1,), (0,))).reshape(3, 3, 16, 128)
        for z in range(4)
    ]
    corner = jnp.zeros((16, 128), F32)
    edges = jnp.zeros((8, 128), F32)
    for z in range(4):
        byd = []
        for d in range(3):
            byd.append(sum(terms[z + a - 1][a, d] for a in range(3) if 0 <= z + a - 1 < 4))
        main = byd[1]
        main = main + jnp.where(lane >= 1, pltpu.roll(byd[0], 1, 1), 0.0)
        main = main + jnp.where(lane <= 126, pltpu.roll(byd[2], 127, 1), 0.0)
        near_ref[8 * z : 8 * z + 8] = main[:8]
        far_ref[8 * z : 8 * z + 8] = main[:8]
        edges = jnp.where(sub == z, turned(main[8:], z), edges)
        edges = jnp.where(sub == 7 - z, turned(main[8:], -z), edges)
        low, high = 16 * z, 16 * z + 15
        corner = jnp.where(lane == low, pltpu.roll(byd[0], low + 1, 1), corner)
        corner = jnp.where(lane == high, pltpu.roll(byd[2], high, 1), corner)
    corners = jnp.where(at_end(lane[:8]), corner[:8], pltpu.roll(corner[8:], 2, 1))
    near_ref[32:40] = edges
    far_ref[32:40] = edges
    near_ref[40:48] = corners
    far_ref[40:48] = corners
    far_ref[48:88] = jnp.zeros((40, 128), F32)
    copies[2].wait()
    near_ref[48:80] = lab_ref[...].reshape(32, 128).astype(F32)


def rows_kernel(
    own_ref, two_b_ref, two_a_ref, one_b_ref, one_a_ref, main_ref, lab_ref, send_a_ref, send_b_ref
):
    row_block, col_block = lax.axis_index("gx"), lax.axis_index("gy")
    even1 = (row_block & 1) == 0
    even2 = (row_block & 2) == 0
    even_col = (col_block & 1) == 0
    own = own_ref[...]
    one_a, one_b, two_a, two_b = one_a_ref[...], one_b_ref[...], two_a_ref[...], two_b_ref[...]
    before, after = jnp.where(even1, one_b, one_a), jnp.where(even1, one_a, one_b)
    two_a, two_b = two_a[:48], two_b[:48]
    blocks = [jnp.where(even2, two_b, two_a), before, own, after, jnp.where(even2, two_a, two_b)]
    sub = iota((8, 128), 0)
    ends = at_end(iota((8, 128), 1))

    def assemble(tiles, firsts, lasts):
        result = []
        for t in range(5):
            tile = tiles[t]
            if t > 0:
                tile = tile + jnp.where(sub == 0, firsts[t - 1], 0.0)
            if t < 4:
                tile = tile + jnp.where(sub == 7, lasts[t + 1], 0.0)
            result.append(tile)
        return jnp.concatenate(result, axis=0)

    corners = [jnp.where(ends, x[40:48], 0.0) for x in blocks]
    beyond = [jnp.where(ends, pltpu.roll(x[40:48], 126, 1), 0.0) for x in blocks]
    corner = assemble(corners, beyond, beyond)
    main_ref[4] = corner
    lane = iota((40, 128), 1)
    right = jnp.zeros((40, 128), F32)
    left = jnp.zeros((40, 128), F32)
    for z in range(4):
        main = assemble(
            [x[8 * z : 8 * z + 8] for x in blocks],
            [turned(x[32:40], -z) for x in blocks],
            [turned(x[32:40], z) for x in blocks],
        )
        main_ref[z] = main
        lab = jnp.concatenate([x[48 + 8 * z : 56 + 8 * z] for x in (before, own, after)], axis=0)
        lab_ref[z] = lab
        lab = jnp.concatenate([lab, jnp.zeros((16, 128), F32)], axis=0)
        right = jnp.where((lane >> 4) == z, pltpu.roll(main, 16 * z + 16, 1), right)
        right = jnp.where((lane >> 4) == z + 4, pltpu.roll(lab, (16 * z + 80) % 128, 1), right)
        left = jnp.where((lane >> 4) == z, pltpu.roll(main, 16 * z, 1), left)
        left = jnp.where((lane >> 4) == z + 4, pltpu.roll(lab, 16 * z + 64, 1), left)
    right = jnp.where((lane < 64) & ((lane & 15) == 0), corner, right)
    left = jnp.where((lane < 64) & ((lane & 15) == 15), corner, left)
    send_a_ref[...] = jnp.where(even_col, right, left)
    send_b_ref[...] = jnp.where(even_col, left, right)


def shift_rows(x, s):
    return pltpu.roll(x, s % x.shape[0], 0)


def shift_cols(x, s):
    return pltpu.roll(x, s % x.shape[1], 1)


def cross(fields, outside):
    result = []
    for z in range(4):
        x = fields[z]
        around = shift_rows(x, 1) + shift_rows(x, -1) + shift_cols(x, 1) + shift_cols(x, -1)
        before = fields[z - 1] if z > 0 else outside
        after = fields[z + 1] if z < 3 else outside
        result.append((around + (before + after)) * (1.0 / 9.0) + x * (1.0 / 3.0))
    return result


def box(fields, outside, crop):
    result = []
    for z in range(4):
        before = fields[z - 1] if z > 0 else outside
        after = fields[z + 1] if z < 3 else outside
        x = fields[z] + (before + after)
        x = x + shift_rows(x, 1) + shift_rows(x, -1)
        if crop:
            x = x[8:32]
        result.append(x + shift_cols(x, 1) + shift_cols(x, -1))
    return result


def inverse(x):
    return 1.0 / x


def forward_step(i, state, inside, crop, keep):
    def middle(x):
        return x[8:32] if crop else x

    e, q, s = state
    e = [jnp.where(inside, x, 1.0) for x in cross(e, 1.0)]
    q_next = [inverse(x) for x in e]
    mean = box(q_next, 1.0, crop)
    s_next = []
    for z in range(4):
        d_inv = inverse(mean[z])
        qz = middle(q[z])
        ratio = (27.0 * qz) * d_inv
        ratio = ratio * ratio
        log_term = jnp.log(1.0 + ratio)
        change = SOFT * log_term
        if i == 0:
            s_next.append(change)
            keep(i, z, qz, d_inv, ratio, None, None, None)
        else:
            rest = 1.0 - s[z]
            power = jnp.exp(log_term * rest)
            s_next.append(s[z] + SOFT * jnp.log(1.0 + power))
            keep(i, z, qz, d_inv, ratio, change, rest, power)
    return e, q_next, s_next


def skeleton_kernel(
    bias_ref, f_ref, main_ref, lab_ref, got_b_ref, got_a_ref,
    grad_ref, keep_ref, send_ref,
    qs_ref, ds_ref, rs_ref, gain_ref,
):
    row_ids = lax.axis_index("gx") * 8 - 16 + iota((40, 256), 0)
    lane = iota((40, 256), 1)
    col = jnp.where(lane < 144, lane, lane - 256)
    col_ids = lax.axis_index("gy") * 128 + col
    inside = (row_ids >= 0) & (row_ids < lax.axis_size("gx") * 8)
    inside = inside & (col_ids >= 0) & (col_ids < lax.axis_size("gy") * 128) & (col >= -16)
    inside_f = jnp.where(inside, 1.0, 0.0)
    inner = inside_f[8:32]
    inner_b = inner > 0.5
    bias = bias_ref[0]

    even_col = (lax.axis_index("gy") & 1) == 0
    from_left = jnp.where(even_col, got_b_ref[...], got_a_ref[...])
    from_right = jnp.where(even_col, got_a_ref[...], got_b_ref[...])
    corner = main_ref[4]
    lane40 = iota((40, 128), 1)
    lane24 = lane40[:24]
    e0, q0, slope, probs, labels = [], [], [], [], []
    for z in range(4):
        to_zero, to_last = (128 - 16 * z) % 128, 112 - 16 * z
        left_zero, left_last = pltpu.roll(from_left, to_zero, 1), pltpu.roll(from_left, to_last, 1)
        right_zero, right_last = pltpu.roll(from_right, to_zero, 1), pltpu.roll(from_right, to_last, 1)
        main = main_ref[z]
        main = main + jnp.where(lane40 == 0, left_zero, jnp.where(lane40 == 127, right_last, 0.0))
        tail = jnp.where(lane40 >= 112, left_last, jnp.where(lane40 < 16, right_zero, 0.0))
        own_zero, own_last = pltpu.roll(corner, to_zero, 1), pltpu.roll(corner, to_last, 1)
        tail = tail + jnp.where(lane40 == 0, own_zero, jnp.where(lane40 == 127, own_last, 0.0))
        lab_left = pltpu.roll(from_left[:24], 48 - 16 * z, 1)
        lab_right = pltpu.roll(from_right[:24], 64 - 16 * z, 1)
        lab_tail = jnp.where(lane24 >= 112, lab_left, jnp.where(lane24 < 16, lab_right, 0.0))
        logits = jnp.concatenate([main, tail], axis=1) + bias
        small = jnp.exp(-jnp.abs(logits))
        scale = inverse(1.0 + small)
        prob = jnp.where(logits >= 0.0, scale, small * scale)
        prob = jnp.where(inside, prob, 0.0)
        e = jnp.exp(-SHARP * prob)
        e0.append(e)
        q0.append(inverse(e))
        weight = (small * scale) * scale
        slope.append(((-SHARP) * e * weight)[8:32] * inner)
        probs.append((prob[8:32], weight[8:32]))
        labels.append(jnp.concatenate([lab_ref[z], lab_tail], axis=1))

    low, high = jnp.exp(-SHARP * jnp.ones((24, 256), F32)), jnp.exp(SHARP * jnp.ones((24, 256), F32))
    true_state = (
        [jnp.where(x > 0.5, low, 1.0) for x in labels],
        [jnp.where(x > 0.5, high, 1.0) for x in labels],
        None,
    )

    def keep(i, z, qz, d_inv, ratio, change, rest, power):
        qs_ref[i, z] = qz
        ds_ref[i, z] = d_inv
        part = (-2.0 * SOFT) * (ratio * inverse(1.0 + ratio))
        if i > 0:
            share = power * inverse(1.0 + power)
            part = part * (share * rest)
            gain_ref[i, z] = 1.0 - share * change
        rs_ref[i, z] = part

    pred_state = (e0, q0, None)
    for i in range(ITERS + 1):
        true_state = forward_step(i, true_state, inner_b, False, lambda *factors: None)
        pred_state = forward_step(i, pred_state, inside, True, keep)
    true_skel = true_state[2]
    q_last, pred_skel = pred_state[1], pred_state[2]

    def own(x):
        return x[8:16, :128]

    def total(values):
        acc = values[0] + values[1] + values[2] + values[3]
        return jnp.sum(jnp.sum(acc, axis=1, keepdims=True), axis=0, keepdims=True)

    t0 = total([own(pred_skel[z] * labels[z]) for z in range(4)])
    t1 = total([own(pred_skel[z]) for z in range(4)])
    t2 = total([own(true_skel[z] * probs[z][0]) for z in range(4)])
    t3 = total([own(true_skel[z]) for z in range(4)])

    running = [inner] * 4
    deep = [None, None]
    for i in range(ITERS, -1, -1):
        coefs = []
        for z in range(4):
            coefs.append(rs_ref[i, z] * running[z])
            if i > 0:
                running[z] = running[z] * gain_ref[i, z]
        q_of = [q_last[z][8:32] if i == ITERS else qs_ref[i + 1, z] for z in range(4)]
        q_of = [(x * x) * inner for x in q_of]
        for f in range(2):
            scaled = [coefs[z] * labels[z] for z in range(4)] if f == 0 else coefs
            spread = box([scaled[z] * ds_ref[i, z] for z in range(4)], 0.0, False)
            incoming = []
            for z in range(4):
                if deep[f] is None:
                    incoming.append(-(spread[z] * q_of[z]))
                else:
                    incoming.append(deep[f][z] * inner - spread[z] * q_of[z])
            moved = cross(incoming, 0.0)
            deep[f] = [moved[z] + scaled[z] * qs_ref[i, z] for z in range(4)]
    fields = [
        [deep[0][z] * slope[z] for z in range(4)],
        [deep[1][z] * slope[z] for z in range(4)],
        [true_skel[z] * probs[z][1] * inner for z in range(4)],
    ]
    bias_sums = [total([own(x) for x in field]) for field in fields]

    sub = iota((8, 256), 0)
    stacks = []
    for z in range(4):
        pieces = []
        for f in range(3):
            x = fields[f][z]
            edge = jnp.where(sub == 0, x[16:24], jnp.where(sub == 7, x[0:8], 0.0))
            block = jnp.concatenate([x[8:16], edge], axis=0)
            grad_ref[f, z] = block
            for d in range(3):
                moved = (shift_cols(block, d - 1) if d != 1 else block)[:, :128]
                upper = moved.astype(BF16)
                lower = (moved - upper.astype(F32)).astype(BF16)
                pieces += [upper, lower]
        stacks.append(jnp.concatenate(pieces, axis=0))
    offset = (iota((16, 256), 1) & 7) - edge_row(iota((16, 256), 0)) + 1
    picked = {}
    for a in range(3):
        moments = jnp.zeros((288, 256), F32)
        for z in range(4):
            if 0 <= z + a - 1 < 4:
                feats = f_ref[:, z + a - 1].reshape(256, 128)
                moments = moments + dot(stacks[z], feats, ((1,), (1,)))
        for f in range(3):
            for d in range(3):
                start = (f * 3 + d) * 32
                pair = moments[start : start + 16] + moments[start + 16 : start + 32]
                for b in range(3):
                    chosen = jnp.where(offset == b, pair, 0.0)
                    picked[b, f, a, d] = jnp.sum(chosen, axis=0, keepdims=True)
    order = [(f, a, d) for f in range(3) for a in range(3) for d in range(3)]
    groups = [[picked[(b,) + at] for at in order[:24]] for b in range(3)]
    rest = [picked[(b,) + at] for b in range(3) for at in order[24:]]
    groups.append(rest + [jnp.zeros((15, 256), F32)])
    stacked = jnp.concatenate([row for rows in groups for row in rows], axis=0)
    high = stacked.astype(BF16)
    left_over = stacked - high.astype(F32)
    middle = left_over.astype(BF16)
    low = (left_over - middle.astype(F32)).astype(BF16)
    collect = jnp.where((iota((256, 128), 0) >> 3) == iota((256, 128), 1), 1.0, 0.0).astype(BF16)
    summed = dot(jnp.concatenate([high, middle, low], axis=0), collect, ((1,), (0,)))
    summed = summed[:96] + summed[96:192] + summed[192:]
    result = summed[:24]
    for b in range(1, 4):
        result = result + pltpu.roll(summed[24 * b : 24 * b + 24], 32 * b, 1)
    row24, lane_of = iota((24, 128), 0), iota((24, 128), 1)
    for k, value in enumerate([t0, t1, t2, t3] + bias_sums):
        result = jnp.where(((row24 == 11) | (row24 == 23)) & (lane_of == 96 + k), value, result)
    keep_ref[...] = jnp.where(even_col, result[:12], result[12:])
    send_ref[...] = jnp.where(even_col, result[12:], result[:12])


def pair_kernel(own_ref, got_ref, out_ref):
    out_ref[...] = own_ref[...] + got_ref[...]


def four_kernel(own_ref, one_ref, two_ref, three_ref, out_ref):
    half = (own_ref[...] + one_ref[...]) + (two_ref[...] + three_ref[...])
    for n in range(out_ref.shape[0]):
        out_ref[n] = half[4 * (n % 3) : 4 * (n % 3) + 4]


def add_kernel(in_ref, out_ref):
    for part in range(3):
        acc = in_ref[part]
        for n in range(part + 3, in_ref.shape[0], 3):
            acc = acc + in_ref[n]
        out_ref[part] = acc


def loss_and_slopes(row):
    sums = [row[:, 96 + k : 97 + k] for k in range(7)]
    precision = (sums[0] + 1.0) / (sums[1] + 1.0)
    sensitivity = (sums[2] + 1.0) / (sums[3] + 1.0)
    both = precision + sensitivity
    loss = 1.0 - 2.0 * precision * sensitivity / both
    by_precision = -2.0 * (sensitivity / both) * (sensitivity / both)
    by_sensitivity = -2.0 * (precision / both) * (precision / both)
    slopes = [
        by_precision / (sums[1] + 1.0),
        -by_precision * precision / (sums[1] + 1.0),
        by_sensitivity / (sums[3] + 1.0),
    ]
    return loss, slopes, sums[4:]


def weight_kernel(
    own_ref, got_ref, feature_ref,
    loss_out_ref, weight_out_ref, bias_out_ref, feature_out_ref,
    loss_ref, weight_ref, bias_ref, sems,
):
    pairs = [
        (feature_ref, feature_out_ref), (loss_ref, loss_out_ref),
        (bias_ref, bias_out_ref), (weight_ref, weight_out_ref),
    ]
    copies = [pltpu.make_async_copy(x, y, sems.at[n]) for n, (x, y) in enumerate(pairs)]
    copies[0].start()
    even = (lax.axis_index("gy") & 1) == 0
    own, got = own_ref[...], got_ref[...]
    first, second = jnp.where(even, own, got), jnp.where(even, got, own)
    acc = jnp.concatenate([x[part] for x in (first, second) for part in range(3)], axis=0)
    loss, slopes, bias_sums = loss_and_slopes(acc[11:12])
    loss_ref[...] = loss
    bias_ref[...] = sum(slopes[f] * bias_sums[f] for f in range(3))
    copies[1].start()
    copies[2].start()
    group = iota((3, 128), 1) >> 5
    last = acc[18:21]
    for b in range(3):
        last = jnp.where(group == b, pltpu.roll(acc[3 * b : 3 * b + 3], (32 * b + 32) % 128, 1), last)
    third = jnp.concatenate([acc[18:24], last], axis=0)
    weight = slopes[0] * acc[0:9] + slopes[1] * acc[9:18] + slopes[2] * third
    for b in range(3):
        part = weight if b == 0 else pltpu.roll(weight, 128 - 32 * b, 1)
        for a in range(3):
            weight_ref[9 * a + 3 * b : 9 * a + 3 * b + 3] = part[3 * a : 3 * a + 3, :32]
    copies[3].start()
    for copy in copies:
        copy.wait()


def feature_kernel(sums_ref, grad_ref, a_ref, out_ref, *, voxels):
    _, slopes, _ = loss_and_slopes(sums_ref[2, 3:4])
    matrix = a_ref[...]
    parts = []
    for z in range(4):
        block = slopes[0] * grad_ref[0, z] + slopes[1] * grad_ref[1, z] + slopes[2] * grad_ref[2, z]
        block = block * voxels
        byd = []
        for d in range(3):
            moved = (shift_cols(block, d - 1) if d != 1 else block)[:, :128]
            upper = moved.astype(BF16)
            byd.append((upper, (moved - upper.astype(F32)).astype(BF16)))
        parts.append(byd)
    none = jnp.zeros((16, 128), BF16)
    for z in range(4):
        acc_z = None
        for level in range(2):
            stack = []
            for a in range(3):
                for d in range(3):
                    at = z - a + 1
                    stack.append(parts[at][d][level] if 0 <= at < 4 else none)
            term = dot(matrix, jnp.concatenate(stack, axis=0), ((0,), (0,)))
            acc_z = term if acc_z is None else acc_z + term
        out_ref[:, z] = acc_z.reshape(32, 8, 128).astype(BF16)


def call(kernel, out_shapes, *args, scratch=(), spaces={}, out_spaces={}):
    in_specs = [pl.BlockSpec(memory_space=spaces.get(n, pltpu.VMEM)) for n in range(len(args))]
    return pl.pallas_call(
        kernel,
        out_shape=[jax.ShapeDtypeStruct(shape, dtype) for shape, dtype in out_shapes],
        in_specs=in_specs,
        out_specs=[
            pl.BlockSpec(memory_space=out_spaces.get(n, pltpu.VMEM)) for n in range(len(out_shapes))
        ],
        scratch_shapes=list(scratch),
        compiler_params=pltpu.CompilerParams(vmem_limit_bytes=VMEM_LIMIT),
    )(*args)


def swapped(x, axis, step, phase):
    count = lax.axis_size(axis)
    pairs = []
    for n in range(count - step):
        if (n // step) % 2 == phase:
            pairs += [(n, n + step), (n + step, n)]
    return lax.ppermute(x, axis, pairs)


def local(features, vessel_label, conv_weight, conv_bias):
    gx, gy = lax.axis_size("gx"), lax.axis_size("gy")
    voxels = float(4 * 8 * gx * 128 * gy)
    matrix, near, far, features = call(
        partial_logits_kernel,
        [((144, 256), BF16), ((80, 128), F32), ((88, 128), F32), (features.shape, BF16)],
        *[pltpu.with_memory_space_constraint(x, pltpu.HBM) for x in (conv_weight, features, vessel_label)],
        scratch=[
            pltpu.VMEM((27, 32), BF16),
            pltpu.VMEM((4, 8, 128), jnp.int32),
            pltpu.SemaphoreType.DMA((3,)),
        ],
        spaces={0: pltpu.HBM, 1: pltpu.HBM, 2: pltpu.HBM},
    )
    two = [swapped(far, "gx", 2, phase) for phase in range(2)]
    one = [swapped(near, "gx", 1, phase) for phase in range(2)]
    main, labels, send_a, send_b = call(
        rows_kernel,
        [((5, 40, 128), F32), ((4, 24, 128), F32), ((40, 128), F32), ((40, 128), F32)],
        near, *two[::-1], *one[::-1],
    )
    got_b = swapped(send_b, "gy", 1, 1)
    got_a = swapped(send_a, "gy", 1, 0)
    field = pltpu.VMEM((ITERS + 1, 4, 24, 256), F32)
    grads, keep, send = call(
        skeleton_kernel,
        [((3, 4, 16, 256), F32), ((12, 128), F32), ((12, 128), F32)],
        conv_bias, features, main, labels, got_b, got_a,
        scratch=[field] * 4, spaces={0: pltpu.SMEM},
    )
    half = call(pair_kernel, [((12, 128), F32)], keep, swapped(send, "gy", 1, 0))[0]
    others = [lax.ppermute(half, "gy", [(n, n ^ mask) for n in range(gy)]) for mask in (2, 4, 6)]
    sums = call(four_kernel, [((3 * gx, 4, 128), F32)], half, *others)[0]
    sums = lax.all_to_all(sums, "gx", 0, 0, tiled=True)
    sums = call(add_kernel, [((3, 4, 128), F32)], sums)[0]
    other = swapped(sums, "gy", 1, 0)

    def feature_part(*refs):
        feature_kernel(*refs, voxels=voxels)

    feature_grad = call(feature_part, [((32, 4, 8, 128), BF16)], sums, grads, matrix)[0]
    loss, weight_grad, bias_grad, feature_grad = call(
        weight_kernel,
        [((1, 1), F32), ((27, 32), F32), ((1, 1), F32), ((32, 4, 8, 128), BF16)],
        sums, other, feature_grad,
        scratch=[
            pltpu.VMEM((1, 1), F32),
            pltpu.VMEM((27, 32), F32),
            pltpu.VMEM((1, 1), F32),
            pltpu.SemaphoreType.DMA((4,)),
        ],
        out_spaces={n: pltpu.HBM for n in range(4)},
    )
    return (loss.reshape(()), weight_grad, bias_grad.reshape((1,)), feature_grad)


def solution(mesh):
    in_specs = (P(None, None, "gx", "gy"), P(None, "gx", "gy"), P(), P())
    out_specs = (P(), P(), P(), P(None, None, "gx", "gy"))
    return jax.shard_map(local, mesh=mesh, in_specs=in_specs, out_specs=out_specs, check_vma=False)
```
